32 devices in a mesh: dp: 4 (over z), ctx: 8 (over y, x, core).
Axes of the slice: x: 2, y: 2, z: 4, core: 2. Of those that a mesh axis runs over, the one named last changes fastest.
Arguments:
- query_in: bfloat16 [4, 1024, 4096], P('dp', 'ctx'), may hold values from -6 to 6
- key_in: bfloat16 [4, 1024, 4096], P('dp', 'ctx'), may hold values from -6 to 6
- value_in: bfloat16 [4, 1024, 4096], P('dp', 'ctx'), may hold values from -6 to 6
- grad_out: bfloat16 [4, 1024, 4096], P('dp', 'ctx'), may hold values from -6 to 6
- filters: float32 [4096, 1024], P('ctx'), may hold values from -0.1875 to 0.1875
- skip_gain: float32 [4096], replicated, may hold values from 0.1 to 1.9
Outputs:
- mixed_out: bfloat16 [4, 1024, 4096], P('dp', 'ctx')
- grad_query: bfloat16 [4, 1024, 4096], P('dp', 'ctx')
- grad_key: bfloat16 [4, 1024, 4096], P('dp', 'ctx')
- grad_value: bfloat16 [4, 1024, 4096], P('dp', 'ctx')
- grad_filter: float32 [4096, 1024], P('ctx', 'dp')
The draws below stay inside these ranges and needn't reach their ends.
All inputs are finite; a program needn't handle non-finite values.
Results may differ from the reference program's by a relative error of at most 0.0085.
Values may be sent and summed in bfloat16 or wider, within the bound.
No kernel may reach another device: no remote copies, remote signals or barrier semaphores. Data moves between devices by JAX's collectives and lax.ppermute only.
A program may use at most 192 MiB of HBM per device.

```python
import jax
import jax.numpy as jnp
from jax import lax

CH = 4096
LEN = 1024
SEQS = 4


def block_scale(stream_key, shape, cuts, smallest, largest):
    loudness = 1.0
    for dim, blocks in cuts:
        heights = jax.random.uniform(jax.random.fold_in(jax.random.fold_in(stream_key, 6), dim), (blocks,), jnp.float32, smallest / len(cuts), largest / len(cuts))
        loudness = loudness * jnp.repeat(jnp.exp(heights), shape[dim] // blocks).reshape((-1,) + (1,) * (len(shape) - 1 - dim))
    return loudness


def normal_values(stream_key, extent, spread, reach, pieces=(), held_as=jnp.bfloat16):
    values = spread * jax.random.normal(stream_key, extent, jnp.float32)
    if pieces:
        values = values * block_scale(stream_key, extent, pieces, -0.22, 0.18)
    return jnp.clip(values, -reach, reach).astype(held_as)


def setup_inputs(seed: int = 0) -> dict:
    key_of = jax.random.split(jax.random.key(seed), 7)
    query_in = normal_values(key_of[0], (SEQS, LEN, CH), 1.0, 6.0, ((0, 4), (1, 8)))
    key_in = normal_values(key_of[1], (SEQS, LEN, CH), 1.0, 6.0, ((0, 4), (1, 8)))
    value_in = normal_values(key_of[2], (SEQS, LEN, CH), 1.0, 6.0, ((0, 4), (1, 8)))
    grad_out = normal_values(key_of[3], (SEQS, LEN, CH), 1.0, 6.0, ((0, 4), (1, 8)))
    filters = normal_values(key_of[4], (CH, LEN), LEN ** -0.5, 0.1875, ((0, 8),), jnp.float32)
    skip_gain = jnp.clip(1.0 + 0.18 * jax.random.normal(key_of[5], (CH,), jnp.float32), 0.1, 1.9)
    return dict(query_in=query_in, key_in=key_in, value_in=value_in, grad_out=grad_out, filters=filters, skip_gain=skip_gain)


def reference(query_in, key_in, value_in, grad_out, filters, skip_gain):
    full_length = 2 * LEN
    spectrum = jnp.fft.rfft(filters, n=full_length, axis=1).T

    def one_sequence(running, sequence_items):
        query_rows, key_rows, value_rows, grad_rows = sequence_items
        key_value = (key_rows.astype(jnp.float32) * value_rows.astype(jnp.float32)).astype(jnp.bfloat16)
        weighted = (grad_rows.astype(jnp.float32) * query_rows.astype(jnp.float32)).astype(jnp.bfloat16)
        kv_spec = jnp.fft.rfft(key_value.astype(jnp.float32), n=full_length, axis=0)
        wt_spec = jnp.fft.rfft(weighted.astype(jnp.float32), n=full_length, axis=0)
        conv_out = jnp.fft.irfft(kv_spec * spectrum, n=full_length, axis=0)[:LEN].astype(jnp.bfloat16)
        corr_back = jnp.fft.irfft(wt_spec * jnp.conj(spectrum), n=full_length, axis=0)[:LEN].astype(jnp.bfloat16)
        filter_term = jnp.fft.irfft(wt_spec * jnp.conj(kv_spec), n=full_length, axis=0)[:LEN].T
        mixing = conv_out.astype(jnp.float32) + skip_gain * key_value.astype(jnp.float32)
        mixed_out = (query_rows.astype(jnp.float32) * mixing).astype(jnp.bfloat16)
        grad_query = (grad_rows.astype(jnp.float32) * mixing).astype(jnp.bfloat16)
        back_sum = corr_back.astype(jnp.float32) + skip_gain * weighted.astype(jnp.float32)
        grad_key = (back_sum * value_rows.astype(jnp.float32)).astype(jnp.bfloat16)
        grad_value = (back_sum * key_rows.astype(jnp.float32)).astype(jnp.bfloat16)
        return running + filter_term.astype(running.dtype), (mixed_out, grad_query, grad_key, grad_value)

    initial = jnp.zeros((CH, LEN), jnp.float32)
    grad_filter, results = lax.scan(one_sequence, initial, (query_in, key_in, value_in, grad_out))
    return results[0], results[1], results[2], results[3], grad_filter
```

```python
import functools
import math

import jax
import jax.numpy as jnp
import ml_dtypes
import numpy as np
from jax import lax
from jax.experimental import pallas as pl
from jax.experimental.pallas import tpu as pltpu
from jax.sharding import PartitionSpec as P

F32 = jnp.float32
BF16 = jnp.bfloat16
VMEM_LIMIT = 56 * 1024 * 1024
ROWS = 16


def odd_forward(xs):
    n = len(xs)
    if n == 1:
        return [(xs[0], None)]
    even, odd = odd_forward(xs[0::2]), odd_forward(xs[1::2])
    out = [None] * n
    for k in range(n // 2):
        angle = 2 * math.pi * (2 * k + 1) / (4 * n)
        c, s = math.cos(angle), math.sin(angle)
        (er, ei), (zr, zi) = even[k], odd[k]
        if zi is None:
            tr, ti = c * zr, -s * zr
            out[k], out[n - 1 - k] = (er + tr, ti), (er - tr, ti)
        else:
            tr, ti = c * zr + s * zi, c * zi - s * zr
            out[k], out[n - 1 - k] = (er + tr, ei + ti), (er - tr, ti - ei)
    return out


def odd_back(ys):
    n = len(ys)
    if n == 1:
        return [ys[0][0]]
    even, odd = [], []
    for k in range(n // 2):
        angle = 2 * math.pi * (2 * k + 1) / (4 * n)
        c, s = math.cos(angle), math.sin(angle)
        (ar, ai), (br, bi) = ys[k], ys[n - 1 - k]
        dr, di = ar - br, ai + bi
        if n == 2:
            even.append((ar + br, None))
            odd.append((c * dr - s * di, None))
        else:
            even.append((ar + br, ai - bi))
            odd.append((c * dr - s * di, c * di + s * dr))
    even, odd = odd_back(even), odd_back(odd)
    return [x for pair in zip(even, odd) for x in pair]


def tables(n, b):
    k1 = np.arange(n)[:, None, None]
    k2 = np.arange(b)[None, :, None]
    n2 = np.arange(b)[None, None, :]
    turn = (n2 * (2 * k1 + 1 + 4 * n * k2)) % (4 * n * b)
    angle = 2 * np.pi * turn / (4 * n * b)
    c, s = np.cos(angle), np.sin(angle)
    forward = np.concatenate([np.concatenate([c, s], 2), np.concatenate([-s, c], 2)], 1)
    back = np.swapaxes(forward, 1, 2) / (n * b)

    def halves(x):
        hi = x.astype(ml_dtypes.bfloat16)
        lo = (x - hi.astype(np.float64)).astype(ml_dtypes.bfloat16)
        return hi, lo

    return halves(forward) + halves(back)


def halves(x):
    hi = x.astype(BF16)
    return hi, (x - hi.astype(F32)).astype(BF16)


def dot3(a_hi, a_lo, b_hi, b_lo, dims=((1,), (0,))):
    def one(a, b):
        return lax.dot_general(a, b, (dims, ((), ())), preferred_element_type=F32)

    return one(a_hi, b_hi) + one(a_lo, b_hi) + one(a_hi, b_lo)


def first_stage(x, hi, lo):
    n, b, width = x.shape

    def step(i, carry):
        r = pl.multiple_of(i * ROWS, ROWS)
        for c in range(0, width, 128):
            xs = [x[p, pl.ds(r, ROWS), c : c + 128].astype(F32) for p in range(n)]
            for k, parts in enumerate(odd_forward(xs)):
                for q, part in enumerate(parts):
                    h, l = halves(part)
                    hi[k, pl.ds(q * b + r, ROWS), c : c + 128] = h
                    lo[k, pl.ds(q * b + r, ROWS), c : c + 128] = l
        return carry

    lax.fori_loop(0, b // ROWS, step, 0)


def last_stage(z, store):
    n, b2, width = z.shape
    b = b2 // 2

    def step(i, carry):
        r = pl.multiple_of(i * ROWS, ROWS)
        for c in range(0, width, 128):
            ys = [
                (z[k, pl.ds(r, ROWS), c : c + 128], z[k, pl.ds(b + r, ROWS), c : c + 128])
                for k in range(n)
            ]
            for p, y in enumerate(odd_back(ys)):
                store(p, r, c, y)
        return carry

    lax.fori_loop(0, b // ROWS, step, 0)


def times(x, f, conj):
    b = x.shape[0] // 2
    xr, xi, fr, fi = x[:b], x[b:], f[:b], f[b:]
    if conj:
        return xr * fr + xi * fi, xi * fr - xr * fi
    return xr * fr - xi * fi, xr * fi + xi * fr


def back_product(y, back_hi, back_lo):
    (rh, rl), (ih, il) = halves(y[0]), halves(y[1])
    return dot3(back_hi, back_lo, jnp.concatenate([rh, ih], 0), jnp.concatenate([rl, il], 0))


def product_kernel(n, me, a, b, *outs):
    j = pl.program_id(0)
    value = (a[...].astype(F32) * b[...].astype(F32)).astype(BF16)
    for i in range(n):

        @pl.when(j == i)
        def _():
            outs[i][...] = value


def product_blocks(me, a, b, n):
    rows, total = a.shape
    width = total // n
    block = pl.BlockSpec((rows, width), lambda j, me: (0, me[0] ^ j))
    return pl.pallas_call(
        functools.partial(product_kernel, n),
        grid_spec=pltpu.PrefetchScalarGridSpec(
            num_scalar_prefetch=1,
            grid=(n,),
            in_specs=[block, block],
            out_specs=[pl.BlockSpec((rows, width), lambda j, me: (0, 0))] * n,
        ),
        out_shape=[jax.ShapeDtypeStruct((rows, width), BF16)] * n,
        compiler_params=pltpu.CompilerParams(vmem_limit_bytes=VMEM_LIMIT),
        name="products",
    )(me, a, b)


def filter_kernel(filt, fwd_hi, fwd_lo, spec, hi, lo):
    n, chans, b2 = hi.shape
    b = b2 // 2

    def step(i, carry):
        r = pl.multiple_of(i * ROWS, ROWS)
        xs = [filt[pl.ds(r, ROWS), p * b : (p + 1) * b] for p in range(n)]
        for k, parts in enumerate(odd_forward(xs)):
            for q, part in enumerate(parts):
                h, l = halves(part)
                hi[k, pl.ds(r, ROWS), q * b : (q + 1) * b] = h
                lo[k, pl.ds(r, ROWS), q * b : (q + 1) * b] = l
        return carry

    lax.fori_loop(0, chans // ROWS, step, 0)
    for k in range(n):
        spec[k] = dot3(fwd_hi[k], fwd_lo[k], hi[k], lo[k], ((1,), (1,)))


def filter_spectrum(filters, fwd_hi, fwd_lo, chunk):
    chans, length = filters.shape
    n, b2, _ = fwd_hi.shape
    table = pl.BlockSpec((n, b2, b2), lambda c: (0, 0, 0))
    return pl.pallas_call(
        filter_kernel,
        grid=(chans // chunk,),
        in_specs=[pl.BlockSpec((chunk, length), lambda c: (c, 0)), table, table],
        out_specs=pl.BlockSpec((n, b2, chunk), lambda c: (0, 0, c)),
        out_shape=jax.ShapeDtypeStruct((n, b2, chans), F32),
        scratch_shapes=[pltpu.VMEM((n, chunk, b2), BF16)] * 2,
        compiler_params=pltpu.CompilerParams(vmem_limit_bytes=VMEM_LIMIT),
        name="filter_spectrum",
    )(filters, fwd_hi, fwd_lo)


def conv_kernel(n, me, *refs):
    blocks, (filt, fwd_hi, fwd_lo, back_hi, back_lo, spec), refs = refs[:n], refs[n : n + 6], refs[n + 6 :]
    outs, (x, hi, lo, z, y) = refs[:n], refs[n:]
    for j in range(n):
        x[me[0] ^ j] = blocks[j][...]
    first_stage(x, hi, lo)
    for k in range(n):
        s = dot3(fwd_hi[k], fwd_lo[k], hi[k], lo[k])
        spec[k] = s
        z[k] = back_product(times(s, filt[k], False), back_hi[k], back_lo[k])

    def store(p, r, c, value):
        y[p, pl.ds(r, ROWS), c : c + 128] = value.astype(BF16)

    last_stage(z, store)
    for j in range(n):
        outs[j][...] = y[me[0] ^ j]


def back_kernel(n, d, me, *refs):
    blocks, refs = refs[:n], refs[n:]
    (filt, spec, fwd_hi, fwd_lo, back_hi, back_lo), refs = refs[:6], refs[6:]
    outs, grads, (x, hi, lo, z, zg, y, g) = refs[:n], refs[n : n + d], refs[n + d :]
    b = x.shape[1]
    for j in range(n):
        x[me[0] ^ j] = blocks[j][...]
    first_stage(x, hi, lo)
    for k in range(n):
        s = dot3(fwd_hi[k], fwd_lo[k], hi[k], lo[k])
        z[k] = back_product(times(s, filt[k], True), back_hi[k], back_lo[k])
        zg[k] = back_product(times(s, spec[k], True), back_hi[k], back_lo[k])

    def store(p, r, c, value):
        y[p, pl.ds(r, ROWS), c : c + 128] = value.astype(BF16)

    last_stage(z, store)
    for j in range(n):
        outs[j][...] = y[me[0] ^ j]

    def store_grad(p, r, c, value):
        g[p, pl.ds(r, ROWS), c : c + 128] = value

    last_stage(zg, store_grad)
    per = n // d
    for j in range(d):
        for i in range(per):
            part = g[(me[1] ^ j) * per + i]
            grads[j][i * b : (i + 1) * b] = part.astype(grads[j].dtype)


def conv(me, blocks, filt, fwd, back, chunk):
    n = len(blocks)
    b, chans = blocks[0].shape
    table = pl.BlockSpec((n, 2 * b, 2 * b), lambda c, me: (0, 0, 0))
    block = pl.BlockSpec((b, chunk), lambda c, me: (0, c))
    wide = pl.BlockSpec((n, 2 * b, chunk), lambda c, me: (0, 0, c))
    out = pl.pallas_call(
        functools.partial(conv_kernel, n),
        grid_spec=pltpu.PrefetchScalarGridSpec(
            num_scalar_prefetch=1,
            grid=(chans // chunk,),
            in_specs=[block] * n + [wide] + [table] * 4,
            out_specs=[wide] + [block] * n,
            scratch_shapes=[
                pltpu.VMEM((n, b, chunk), BF16),
                pltpu.VMEM((n, 2 * b, chunk), BF16),
                pltpu.VMEM((n, 2 * b, chunk), BF16),
                pltpu.VMEM((n, 2 * b, chunk), F32),
                pltpu.VMEM((n, b, chunk), BF16),
            ],
        ),
        out_shape=[jax.ShapeDtypeStruct((n, 2 * b, chans), F32)]
        + [jax.ShapeDtypeStruct((b, chans), BF16)] * n,
        compiler_params=pltpu.CompilerParams(vmem_limit_bytes=VMEM_LIMIT),
        name="conv",
    )(me, *blocks, filt, *fwd, *back)
    return out[0], out[1:]


def backward(me, blocks, filt, spec, fwd, back, chunk, d):
    n = len(blocks)
    b, chans = blocks[0].shape
    table = pl.BlockSpec((n, 2 * b, 2 * b), lambda c, me: (0, 0, 0))
    block = pl.BlockSpec((b, chunk), lambda c, me: (0, c))
    wide = pl.BlockSpec((n, 2 * b, chunk), lambda c, me: (0, 0, c))
    grad_rows = n * b // d
    grad = pl.BlockSpec((grad_rows, chunk), lambda c, me: (0, c))
    out = pl.pallas_call(
        functools.partial(back_kernel, n, d),
        grid_spec=pltpu.PrefetchScalarGridSpec(
            num_scalar_prefetch=1,
            grid=(chans // chunk,),
            in_specs=[block] * n + [wide, wide] + [table] * 4,
            out_specs=[block] * n + [grad] * d,
            scratch_shapes=[
                pltpu.VMEM((n, b, chunk), BF16),
                pltpu.VMEM((n, 2 * b, chunk), BF16),
                pltpu.VMEM((n, 2 * b, chunk), BF16),
                pltpu.VMEM((n, 2 * b, chunk), F32),
                pltpu.VMEM((n, 2 * b, chunk), F32),
                pltpu.VMEM((n, b, chunk), BF16),
                pltpu.VMEM((n, b, chunk), F32),
            ],
        ),
        out_shape=[jax.ShapeDtypeStruct((b, chans), BF16)] * n
        + [jax.ShapeDtypeStruct((grad_rows, chans), F32 if j == 0 else BF16) for j in range(d)],
        compiler_params=pltpu.CompilerParams(vmem_limit_bytes=VMEM_LIMIT),
        name="backward",
    )(me, *blocks, filt, spec, *fwd, *back)
    return out[:n], out[n:]


def gate_kernel(n, me, gain, left, right, out_left, out_right, *refs):
    blocks, (first, second) = refs[:n], refs[n:]
    j = pl.program_id(0)
    a, b = left[...].astype(F32), right[...].astype(F32)
    direct = (out_left[...].astype(F32) * out_right[...].astype(F32)).astype(BF16).astype(F32)
    for i in range(n):

        @pl.when(j == i)
        def _():
            total = blocks[i][...].astype(F32) + gain[...] * direct
            first[...] = (a * total).astype(BF16)
            second[...] = (b * total).astype(BF16)


def gate(me, gain, left, right, pair, blocks):
    n = len(blocks)
    rows, total = left.shape
    width = total // n
    block = pl.BlockSpec((rows, width), lambda j, me: (0, me[0] ^ j))
    whole = pl.BlockSpec((rows, width), lambda j, me: (0, 0))
    return pl.pallas_call(
        functools.partial(gate_kernel, n),
        grid_spec=pltpu.PrefetchScalarGridSpec(
            num_scalar_prefetch=1,
            grid=(n,),
            in_specs=[pl.BlockSpec((1, width), lambda j, me: (0, me[0] ^ j))]
            + [block] * 4
            + [whole] * n,
            out_specs=[block, block],
        ),
        out_shape=[jax.ShapeDtypeStruct((rows, total), BF16)] * 2,
        compiler_params=pltpu.CompilerParams(vmem_limit_bytes=VMEM_LIMIT),
        name="gate",
    )(me, gain, left, right, *pair, *blocks)


def sum_kernel(d, *refs):
    parts, out = refs[:d], refs[d]
    total = parts[0][...].astype(F32)
    for part in parts[1:]:
        total = total + part[...].astype(F32)
    out[...] = total.T


def sum_grads(parts):
    rows, chans = parts[0].shape
    return pl.pallas_call(
        functools.partial(sum_kernel, len(parts)),
        out_shape=jax.ShapeDtypeStruct((chans, rows), F32),
        compiler_params=pltpu.CompilerParams(vmem_limit_bytes=VMEM_LIMIT),
        name="sum_grads",
    )(*parts)


def exchange(blocks, axis):
    n = len(blocks)
    got = [blocks[0]] + [None] * (n - 1)
    for j in range(n - 1, 0, -1):
        got[j] = lax.ppermute(blocks[j], axis, [(i, i ^ j) for i in range(n)])
    return got


def local(n, d, query_in, key_in, value_in, grad_out, filters, skip_gain):
    query, key, value, grad = query_in[0], key_in[0], value_in[0], grad_out[0]
    b = query.shape[0]
    chunk = min(256, filters.shape[0])
    me = jnp.stack([lax.axis_index("ctx"), lax.axis_index("dp")]).astype(jnp.int32)
    tabs = [jnp.asarray(t) for t in tables(n, b)]
    fwd, back = tabs[:2], tabs[2:]
    gain = skip_gain[None, :]

    kv = exchange(product_blocks(me, key, value, n), "ctx")
    wt = exchange(product_blocks(me, query, grad, n), "ctx")
    filt = filter_spectrum(filters, *fwd, chunk)
    spec, conv_blocks = conv(me, kv, filt, fwd, back, chunk)
    conv_back = exchange(conv_blocks, "ctx")
    corr_blocks, grads = backward(me, wt, filt, spec, fwd, back, chunk, d)
    corr_back = exchange(corr_blocks, "ctx")
    grads = exchange(grads, "dp")
    mixed_out, grad_query = gate(me, gain, query, grad, (key, value), conv_back)
    grad_filter = sum_grads(grads)
    grad_key, grad_value = gate(me, gain, value, key, (query, grad), corr_back)
    return mixed_out[None], grad_query[None], grad_key[None], grad_value[None], grad_filter


def solution(mesh):
    rows = P("dp", "ctx", None)
    return jax.shard_map(
        functools.partial(local, mesh.shape["ctx"], mesh.shape["dp"]),
        mesh=mesh,
        in_specs=(rows, rows, rows, rows, P("ctx", None), P()),
        out_specs=(rows, rows, rows, rows, P("ctx", "dp")),
        check_vma=False,
    )
```

```python
import functools
import math

import jax
import jax.numpy as jnp
import ml_dtypes
import numpy as np
from jax import lax
from jax.experimental import pallas as pl
from jax.experimental.pallas import tpu as pltpu
from jax.sharding import PartitionSpec as P

F32 = jnp.float32
BF16 = jnp.bfloat16
VMEM_LIMIT = 56 * 1024 * 1024
CLASSES = 8
ROWS = 16
HALVES = 2
PARAMS = pltpu.CompilerParams(vmem_limit_bytes=VMEM_LIMIT)
VMEM = pl.BlockSpec(memory_space=pltpu.VMEM)
ANY = pl.BlockSpec(memory_space=pl.ANY)


def tables(length):
    m2 = length // CLASSES
    c = np.arange(CLASSES)[:, None, None]
    j = np.arange(m2)[None, :, None]
    m = np.arange(m2)[None, None, :]
    turn = ((CLASSES * m + c) * (2 * j + 1)) % (4 * length)
    angle = 2 * np.pi * turn / (4 * length)
    forward = np.concatenate([np.cos(angle), -np.sin(angle)], 1)
    back = np.swapaxes(forward, 1, 2) / length

    def parts(x):
        hi = x.astype(ml_dtypes.bfloat16)
        return hi, (x - hi.astype(np.float64)).astype(ml_dtypes.bfloat16)

    return np.concatenate(parts(forward), 2), np.concatenate(parts(back), 1)


def parts(x):
    hi = x.astype(BF16)
    return hi, (x - hi.astype(F32)).astype(BF16)


def dot(a, b):
    return jnp.dot(a, b, preferred_element_type=F32)


def dft(z, sign):
    n = len(z)
    if n == 1:
        return z
    even, odd = dft(z[0::2], sign), dft(z[1::2], sign)
    low, high = [], []
    for k in range(n // 2):
        (er, ei), (zr, zi) = even[k], odd[k]
        if k == 0:
            tr, ti = zr, zi
        elif 4 * k == n:
            tr, ti = (-zi, zr) if sign > 0 else (zi, -zr)
        else:
            c, s = math.cos(2 * math.pi * k / n), sign * math.sin(2 * math.pi * k / n)
            if 8 * k == n:
                tr, ti = (c * (zr - zi), c * (zi + zr)) if sign > 0 else (c * (zr + zi), c * (zi - zr))
            elif 8 * k == 3 * n:
                tr, ti = (c * (zr + zi), c * (zi - zr)) if sign > 0 else (c * (zr - zi), c * (zi + zr))
            else:
                tr, ti = c * zr - s * zi, c * zi + s * zr
        low.append((er + tr, ei + ti))
        high.append((er - tr, ei - ti))
    return low + high


def times(x, f, conj):
    (xr, xi), (fr, fi) = x, f
    if conj:
        return xr * fr + xi * fi, xi * fr - xr * fi
    return xr * fr - xi * fi, xr * fi + xi * fr


def column_copies(arrays, bufs, sems, half, width, into):
    blocks = arrays[0].shape[1] // (HALVES * width)
    copies = []
    for p in range(blocks):
        row = []
        for a, array in enumerate(arrays):
            cols = array.at[:, pl.ds((HALVES * p + half) * width, width)]
            ends = (cols, bufs.at[a, p]) if into else (bufs.at[a, p], cols)
            row.append(pltpu.make_async_copy(*ends, sems.at[a, p]))
        copies.append(row)
    return copies


def product_kernel(half, key, value, query, grad, out, bufs, sems):
    width = out.shape[-1]
    copies = column_copies((key, value, query, grad), bufs, sems, half, width, True)
    for row in copies:
        for copy in row:
            copy.start()
    for p, row in enumerate(copies):
        for copy in row:
            copy.wait()
        out[p, 0] = (bufs[0, p].astype(F32) * bufs[1, p].astype(F32)).astype(BF16)
        out[p, 1] = (bufs[3, p].astype(F32) * bufs[2, p].astype(F32)).astype(BF16)


def products(half, n, key, value, query, grad):
    rows, total = key.shape
    width = total // n // HALVES
    return pl.pallas_call(
        functools.partial(product_kernel, half),
        in_specs=[ANY] * 4,
        out_specs=VMEM,
        out_shape=jax.ShapeDtypeStruct((n, 2, rows, width), BF16),
        scratch_shapes=[
            pltpu.VMEM((4, n, rows, width), BF16),
            pltpu.SemaphoreType.DMA((4, n)),
        ],
        compiler_params=PARAMS,
        name="products",
    )(key, value, query, grad)


def split_rows(x, c, lanes):
    return x[pl.ds(c, x.shape[0] // CLASSES, stride=CLASSES), lanes]


def lane_groups(width):
    return [slice(i, i + 128) for i in range(0, width, 128)]


def filter_kernel(filt, fwd, spec, x, u):
    m2 = x.shape[1] // CLASSES
    width = filt.shape[0]
    for g in range(width // 128):
        x[g] = filt[g * 128 : (g + 1) * 128, :].T
    for c in range(CLASSES):
        for g in range(width // 128):
            hi, lo = parts(x[g, pl.ds(c, m2, stride=CLASSES), :])
            u[c, :, g * 128 : (g + 1) * 128] = dot(fwd[c], jnp.concatenate([hi, hi], 0)) + dot(
                fwd[c, :, :m2], lo
            )

    def step(i, carry):
        r = pl.multiple_of(i * ROWS, ROWS)
        for lanes in lane_groups(width):
            z = [(u[c, pl.ds(r, ROWS), lanes], u[c, pl.ds(m2 + r, ROWS), lanes]) for c in range(CLASSES)]
            for k, (re, im) in enumerate(dft(z, -1)):
                spec[k, pl.ds(r, ROWS), lanes] = re
                spec[k, pl.ds(m2 + r, ROWS), lanes] = im
        return carry

    lax.fori_loop(0, m2 // ROWS, step, 0)


def filter_spectrum(half, filters, fwd):
    chans, length = filters.shape
    width = chans // HALVES
    m2 = length // CLASSES
    return pl.pallas_call(
        filter_kernel,
        grid=(1,),
        in_specs=[
            pl.BlockSpec((width, length), lambda i: (half, 0)),
            pl.BlockSpec(fwd.shape, lambda i: (0, 0, 0)),
        ],
        out_specs=pl.BlockSpec((CLASSES, 2 * m2, width), lambda i: (0, 0, 0)),
        out_shape=jax.ShapeDtypeStruct((CLASSES, 2 * m2, width), F32),
        scratch_shapes=[
            pltpu.VMEM((width // 128, length, 128), F32),
            pltpu.VMEM((CLASSES, 2 * m2, width), F32),
        ],
        compiler_params=PARAMS,
        name="filter_spectrum",
    )(filters, fwd)


def conv_kernel(got, filt, fwd, back, out, grads, nat, x, u, hi, lo):
    n, _, rows, width = got.shape
    groups = width // 128
    length = n * rows
    m2 = length // CLASSES
    d, per, _ = grads.shape

    for a in range(2):
        for g in range(groups):
            lanes = slice(g * 128, (g + 1) * 128)
            for p in range(n):
                nat[g, p * rows : (p + 1) * rows] = got[p, a, :, lanes].astype(F32)
            for c in range(CLASSES):
                x[c, :, lanes] = nat[g, pl.ds(c, m2, stride=CLASSES), :].astype(BF16)
        for c in range(CLASSES):
            data = x[c]
            u[a, c] = dot(fwd[c], jnp.concatenate([data, data], 0))

    def step(i, carry):
        r = pl.multiple_of(i * ROWS, ROWS)
        re, im = pl.ds(r, ROWS), pl.ds(m2 + r, ROWS)
        for lanes in lane_groups(width):
            kv = dft([(u[0, c, re, lanes], u[0, c, im, lanes]) for c in range(CLASSES)], -1)
            wt = dft([(u[1, c, re, lanes], u[1, c, im, lanes]) for c in range(CLASSES)], -1)
            fs = [(filt[k, re, lanes], filt[k, im, lanes]) for k in range(CLASSES)]
            for o, (left, right, conj) in enumerate([(kv, fs, False), (wt, fs, True), (wt, kv, True)]):
                y = dft([times(s, t, conj) for s, t in zip(left, right)], 1)
                for c in range(CLASSES):
                    for q, rows_at in enumerate((re, im)):
                        h, l = parts(y[c][q])
                        hi[o, c, rows_at, lanes] = h
                        lo[o, c, rows_at, lanes] = l
        return carry

    lax.fori_loop(0, m2 // ROWS, step, 0)

    for o in range(3):
        for c in range(CLASSES):
            both = dot(back[c], hi[o, c])
            y = both[:m2] + both[m2:] + dot(back[c, :m2], lo[o, c])
            for g in range(groups):
                nat[g, pl.ds(c, m2, stride=CLASSES), :] = y[:, g * 128 : (g + 1) * 128]
        for g in range(groups):
            lanes = slice(g * 128, (g + 1) * 128)
            if o < 2:
                for p in range(n):
                    out[p, o, :, lanes] = nat[g, p * rows : (p + 1) * rows].astype(BF16)
            else:
                for s in range(d):
                    grads[s, :, lanes] = nat[g, s * per : (s + 1) * per].astype(BF16)


def conv(d, got, filt, fwd, back):
    n, _, rows, width = got.shape
    length = n * rows
    m2 = length // CLASSES
    return pl.pallas_call(
        conv_kernel,
        in_specs=[VMEM] * 4,
        out_specs=[VMEM] * 2,
        out_shape=[
            jax.ShapeDtypeStruct((n, 2, rows, width), BF16),
            jax.ShapeDtypeStruct((d, length // d, width), BF16),
        ],
        scratch_shapes=[
            pltpu.VMEM((width // 128, length, 128), F32),
            pltpu.VMEM((CLASSES, m2, width), BF16),
            pltpu.VMEM((2, CLASSES, 2 * m2, width), F32),
            pltpu.VMEM((3, CLASSES, 2 * m2, width), BF16),
            pltpu.VMEM((3, CLASSES, 2 * m2, width), BF16),
        ],
        compiler_params=PARAMS,
        name="conv",
    )(got, filt, fwd, back)


def gate_kernel(half, query, grad, value, key, gain, got, *refs):
    outs, (bufs, sent, sems, out_sems) = refs[-8:-4], refs[-4:]
    n, _, _, width = got.shape
    copies = column_copies((query, grad, value, key), bufs, sems, half, width, True)
    stores = column_copies(outs, sent, out_sems, half, width, False)
    for row in copies:
        for copy in row:
            copy.start()
    for p, row in enumerate(copies):
        for copy in row:
            copy.wait()
        at = (HALVES * p + half) * width
        scale = gain[:, at : at + width]
        q, g, v, k = (bufs[a, p].astype(F32) for a in range(4))
        mixing = got[p, 0].astype(F32) + scale * (k * v).astype(BF16).astype(F32)
        sent[0, p] = (q * mixing).astype(BF16)
        sent[1, p] = (g * mixing).astype(BF16)
        total = got[p, 1].astype(F32) + scale * (g * q).astype(BF16).astype(F32)
        sent[2, p] = (total * v).astype(BF16)
        sent[3, p] = (total * k).astype(BF16)
        for copy in stores[p]:
            copy.start()
    for row in stores:
        for copy in row:
            copy.wait()


def gate(half, query, grad, value, key, gain, got, outs):
    n, _, rows, width = got.shape
    shape = (4, n, rows, width)
    return pl.pallas_call(
        functools.partial(gate_kernel, half),
        in_specs=[ANY] * 4 + [VMEM, VMEM] + [ANY] * len(outs),
        out_specs=[ANY] * 4,
        out_shape=[jax.ShapeDtypeStruct(query.shape, BF16)] * 4,
        scratch_shapes=[
            pltpu.VMEM(shape, BF16),
            pltpu.VMEM(shape, BF16),
            pltpu.SemaphoreType.DMA(shape[:2]),
            pltpu.SemaphoreType.DMA(shape[:2]),
        ],
        input_output_aliases={6 + i: i for i in range(len(outs))},
        compiler_params=PARAMS,
        name="gate",
    )(query, grad, value, key, gain, got, *outs)


def turn_kernel(*refs):
    out = refs[-1]
    for half, part in enumerate(refs[:-1]):
        width = part.shape[1]
        out[half * width : (half + 1) * width] = part[...].astype(F32).T


def turn_grads(parts_):
    rows, width = parts_[0].shape
    return pl.pallas_call(
        turn_kernel,
        in_specs=[VMEM] * len(parts_),
        out_specs=VMEM,
        out_shape=jax.ShapeDtypeStruct((len(parts_) * width, rows), F32),
        compiler_params=PARAMS,
        name="turn_grads",
    )(*parts_)


def local(n, d, query_in, key_in, value_in, grad_out, filters, skip_gain):
    query, key, value, grad = query_in[0], key_in[0], value_in[0], grad_out[0]
    fwd, back = (jnp.asarray(t) for t in tables(filters.shape[1]))
    gain = skip_gain[None, :]

    def swap(x):
        return lax.all_to_all(x, "ctx", split_axis=0, concat_axis=0, tiled=True)

    got = [swap(products(h, n, key, value, query, grad)) for h in range(HALVES)]
    specs = [filter_spectrum(h, filters, fwd) for h in range(HALVES)]
    outs, grads = [], []
    for h in range(HALVES):
        mixed, part = conv(d, got[h], specs[h], fwd, back)
        back_rows = swap(mixed)
        part = lax.psum_scatter(part, "dp", scatter_dimension=0, tiled=False)
        outs = gate(h, query, grad, value, key, gain, back_rows, outs)
        grads.append(part)
    mixed_out, grad_query, grad_key, grad_value = outs
    return mixed_out[None], grad_query[None], grad_key[None], grad_value[None], turn_grads(grads)


def solution(mesh):
    rows = P("dp", "ctx", None)
    return jax.shard_map(
        functools.partial(local, mesh.shape["ctx"], mesh.shape["dp"]),
        mesh=mesh,
        in_specs=(rows, rows, rows, rows, P("ctx", None), P()),
        out_specs=(rows, rows, rows, rows, P("ctx", "dp")),
        check_vma=False,
    )
```

```python
import functools
import math

import jax
import jax.numpy as jnp
import ml_dtypes
import numpy as np
from jax import lax
from jax.experimental import pallas as pl
from jax.experimental.pallas import tpu as pltpu
from jax.sharding import PartitionSpec as P

F32 = jnp.float32
BF16 = jnp.bfloat16
VMEM_LIMIT = 20 * 1024 * 1024
CLASSES = 8
ROWS = 16
HALVES = 2
PAIRED = (False, True)
PARAMS = pltpu.CompilerParams(vmem_limit_bytes=VMEM_LIMIT)
SMEM = pl.BlockSpec(memory_space=pltpu.SMEM)
VMEM = pl.BlockSpec(memory_space=pltpu.VMEM)
ANY = pl.BlockSpec(memory_space=pl.ANY)


def tables(length):
    m2 = length // CLASSES
    c = np.arange(CLASSES)[:, None, None]
    j = np.arange(m2)[None, :, None]
    m = np.arange(m2)[None, None, :]
    turn = ((CLASSES * m + c) * (2 * j + 1)) % (4 * length)
    angle = 2 * np.pi * turn / (4 * length)
    forward = np.concatenate([np.cos(angle), -np.sin(angle)], 1)
    back = np.swapaxes(forward, 1, 2) / length

    def parts(x):
        hi = x.astype(ml_dtypes.bfloat16)
        return hi, (x - hi.astype(np.float64)).astype(ml_dtypes.bfloat16)

    return np.concatenate(parts(forward), 2), np.concatenate(parts(back), 1)


def parts(x):
    hi = x.astype(BF16)
    return hi, (x - hi.astype(F32)).astype(BF16)


def dot(a, b):
    return jnp.dot(a, b, preferred_element_type=F32)


def dft(z, sign):
    n = len(z)
    if n == 1:
        return z
    even, odd = dft(z[0::2], sign), dft(z[1::2], sign)
    low, high = [], []
    for k in range(n // 2):
        (er, ei), (zr, zi) = even[k], odd[k]
        if k == 0:
            tr, ti = zr, zi
        elif 4 * k == n:
            tr, ti = (-zi, zr) if sign > 0 else (zi, -zr)
        else:
            c, s = math.cos(2 * math.pi * k / n), sign * math.sin(2 * math.pi * k / n)
            if 8 * k == n:
                tr, ti = (c * (zr - zi), c * (zi + zr)) if sign > 0 else (c * (zr + zi), c * (zi - zr))
            elif 8 * k == 3 * n:
                tr, ti = (c * (zr + zi), c * (zi - zr)) if sign > 0 else (c * (zr - zi), c * (zi + zr))
            else:
                tr, ti = c * zr - s * zi, c * zi + s * zr
        low.append((er + tr, ei + ti))
        high.append((er - tr, ei - ti))
    return low + high


def times(x, f, conj):
    (xr, xi), (fr, fi) = x, f
    if conj:
        return xr * fr + xi * fi, xi * fr - xr * fi
    return xr * fr - xi * fi, xr * fi + xi * fr


def resident(x):
    return pltpu.with_memory_space_constraint(x, pltpu.VMEM)


def device(me, j):
    return j if me is None else me[0] ^ j


def columns(me, half, j, width):
    return pl.ds(pl.multiple_of((HALVES * device(me, j) + half) * width, 128), width)


def product_kernel(half, n, me, key, value, query, grad, *outs):
    if len(outs) == 1:
        me, outs = None, [outs[0].at[p] for p in range(n)]
    width = outs[0].shape[-1]
    for j, out in enumerate(outs):
        cols = columns(me, half, j, width)
        out[0] = (key[:, cols].astype(F32) * value[:, cols].astype(F32)).astype(BF16)
        out[1] = (grad[:, cols].astype(F32) * query[:, cols].astype(F32)).astype(BF16)


def products(half, n, paired, me, key, value, query, grad):
    rows, total = key.shape
    width = total // n // HALVES
    if paired:
        shapes = [pltpu.VMEM((2, rows, width), BF16)] * n
    else:
        shapes = [pltpu.VMEM((n, 2, rows, width), BF16)]
    out = pl.pallas_call(
        functools.partial(product_kernel, half, n),
        in_specs=[SMEM] + [VMEM] * 4,
        out_specs=[VMEM] * len(shapes),
        out_shape=shapes,
        compiler_params=PARAMS,
        name="products",
    )(me, key, value, query, grad)
    return out


def lane_groups(width):
    return [slice(i, i + 128) for i in range(0, width, 128)]


def filter_kernel(half, filt, fwd, spec, x, u):
    m2 = x.shape[1] // CLASSES
    width = spec.shape[-1]
    for g in range(width // 128):
        x[g] = filt[half * width + g * 128 : half * width + (g + 1) * 128, :].T
    for c in range(CLASSES):
        for g in range(width // 128):
            hi, lo = parts(x[g, pl.ds(c, m2, stride=CLASSES), :])
            u[c, :, g * 128 : (g + 1) * 128] = dot(fwd[c], jnp.concatenate([hi, hi], 0)) + dot(
                fwd[c, :, :m2], lo
            )

    def step(i, carry):
        r = pl.multiple_of(i * ROWS, ROWS)
        for lanes in lane_groups(width):
            z = [(u[c, pl.ds(r, ROWS), lanes], u[c, pl.ds(m2 + r, ROWS), lanes]) for c in range(CLASSES)]
            for k, (re, im) in enumerate(dft(z, -1)):
                spec[k, pl.ds(r, ROWS), lanes] = re
                spec[k, pl.ds(m2 + r, ROWS), lanes] = im
        return carry

    lax.fori_loop(0, m2 // ROWS, step, 0)


def filter_spectrum(half, filters, fwd):
    chans, length = filters.shape
    width = chans // HALVES
    m2 = length // CLASSES
    return pl.pallas_call(
        functools.partial(filter_kernel, half),
        in_specs=[VMEM, VMEM],
        out_specs=VMEM,
        out_shape=pltpu.VMEM((CLASSES, 2 * m2, width), F32),
        scratch_shapes=[
            pltpu.VMEM((width // 128, length, 128), F32),
            pltpu.VMEM((CLASSES, 2 * m2, width), F32),
        ],
        compiler_params=PARAMS,
        name="filter_spectrum",
    )(filters, fwd)


def conv_kernel(n, d, paired, me, *refs):
    count = n if paired else 1
    got, (filt, fwd, back), refs = refs[:count], refs[count : count + 3], refs[count + 3 :]
    out, grads, (nat, x, u, hi, lo) = refs[:count], refs[count : count + d], refs[count + d :]
    mine = me if paired else None
    if not paired:
        got, out = ([r[0].at[p] for p in range(n)] for r in (got, out))
    _, rows, width = got[0].shape
    groups = width // 128
    m2 = n * rows // CLASSES
    per = grads[0].shape[0]

    for a in range(2):
        for g in range(groups):
            lanes = slice(g * 128, (g + 1) * 128)
            for j in range(n):
                at = pl.multiple_of(device(mine, j) * rows, rows)
                nat[g, pl.ds(at, rows)] = got[j][a, :, lanes].astype(F32)
            for c in range(CLASSES):
                x[c, :, lanes] = nat[g, pl.ds(c, m2, stride=CLASSES), :].astype(BF16)
        for c in range(CLASSES):
            data = x[c]
            u[a, c] = dot(fwd[c], jnp.concatenate([data, data], 0))

    def step(i, carry):
        r = pl.multiple_of(i * ROWS, ROWS)
        re, im = pl.ds(r, ROWS), pl.ds(m2 + r, ROWS)
        for lanes in lane_groups(width):
            kv = dft([(u[0, c, re, lanes], u[0, c, im, lanes]) for c in range(CLASSES)], -1)
            wt = dft([(u[1, c, re, lanes], u[1, c, im, lanes]) for c in range(CLASSES)], -1)
            fs = [(filt[k, re, lanes], filt[k, im, lanes]) for k in range(CLASSES)]
            for o, (left, right, conj) in enumerate([(kv, fs, False), (wt, fs, True), (wt, kv, True)]):
                y = dft([times(s, t, conj) for s, t in zip(left, right)], 1)
                for c in range(CLASSES):
                    for q, rows_at in enumerate((re, im)):
                        h, l = parts(y[c][q])
                        hi[o, c, rows_at, lanes] = h
                        lo[o, c, rows_at, lanes] = l
        return carry

    lax.fori_loop(0, m2 // ROWS, step, 0)

    for o in range(3):
        for c in range(CLASSES):
            both = dot(back[c], hi[o, c])
            y = both[:m2] + both[m2:] + dot(back[c, :m2], lo[o, c])
            for g in range(groups):
                nat[g, pl.ds(c, m2, stride=CLASSES), :] = y[:, g * 128 : (g + 1) * 128]
        for g in range(groups):
            lanes = slice(g * 128, (g + 1) * 128)
            if o < 2:
                for j in range(n):
                    at = pl.multiple_of(device(mine, j) * rows, rows)
                    out[j][o, :, lanes] = nat[g, pl.ds(at, rows)].astype(BF16)
            else:
                for j in range(d):
                    at = pl.multiple_of((me[1] ^ j) * per, per)
                    grads[j][:, lanes] = nat[g, pl.ds(at, per)].astype(grads[j].dtype)


def conv(n, d, paired, me, got, filt, fwd, back):
    rows, width = got[0].shape[-2:]
    length = n * rows
    m2 = length // CLASSES
    shapes = [pltpu.VMEM(got[0].shape, BF16)] * len(got)
    shapes += [pltpu.VMEM((length // d, width), F32 if j == 0 else BF16) for j in range(d)]
    out = pl.pallas_call(
        functools.partial(conv_kernel, n, d, paired),
        in_specs=[SMEM] + [VMEM] * (len(got) + 3),
        out_specs=[VMEM] * len(shapes),
        out_shape=shapes,
        scratch_shapes=[
            pltpu.VMEM((width // 128, length, 128), F32),
            pltpu.VMEM((CLASSES, m2, width), BF16),
            pltpu.VMEM((2, CLASSES, 2 * m2, width), F32),
            pltpu.VMEM((3, CLASSES, 2 * m2, width), BF16),
            pltpu.VMEM((3, CLASSES, 2 * m2, width), BF16),
        ],
        compiler_params=PARAMS,
        name="conv",
    )(me, *got, filt, fwd, back)
    return out[: len(got)], out[len(got) :]


def gate_kernel(half, n, paired, me, query, grad, value, key, gain, *refs):
    count = n if paired else 1
    got, (outs, sent, sems) = refs[:count], (refs[-6:-2], *refs[-2:])
    mine = me if paired else None
    if not paired:
        got = [got[0].at[p] for p in range(n)]
    width = got[0].shape[-1]
    copies = []
    for j in range(n):
        cols = columns(mine, half, j, width)
        scale = gain[:, cols]
        q, g, v, k = (x[:, cols].astype(F32) for x in (query, grad, value, key))
        mixing = got[j][0].astype(F32) + scale * (k * v).astype(BF16).astype(F32)
        sent[0, j] = (q * mixing).astype(BF16)
        sent[1, j] = (g * mixing).astype(BF16)
        total = got[j][1].astype(F32) + scale * (g * q).astype(BF16).astype(F32)
        sent[2, j] = (total * v).astype(BF16)
        sent[3, j] = (total * k).astype(BF16)
        for a in range(4):
            copy = pltpu.make_async_copy(sent.at[a, j], outs[a].at[:, cols], sems.at[a, j])
            copy.start()
            copies.append(copy)
    for copy in copies:
        copy.wait()


def gate(half, n, paired, me, query, grad, value, key, gain, got, outs):
    rows, width = got[0].shape[-2:]
    first = 6 + len(got)
    return pl.pallas_call(
        functools.partial(gate_kernel, half, n, paired),
        in_specs=[SMEM] + [VMEM] * (5 + len(got)) + [ANY] * len(outs),
        out_specs=[ANY] * 4,
        out_shape=[jax.ShapeDtypeStruct(query.shape, BF16)] * 4,
        scratch_shapes=[
            pltpu.VMEM((4, n, rows, width), BF16),
            pltpu.SemaphoreType.DMA((4, n)),
        ],
        input_output_aliases={first + i: i for i in range(len(outs))},
        compiler_params=PARAMS,
        name="gate",
    )(me, query, grad, value, key, gain, *got, *outs)


def turn_kernel(halves, out):
    for half, refs in enumerate(halves):
        total = refs[0][...]
        for ref in refs[1:]:
            total = total + ref[...].astype(F32)
        width = total.shape[1]
        out[half * width : (half + 1) * width] = total.T


def turn_grads(halves):
    rows, width = halves[0][0].shape
    return pl.pallas_call(
        turn_kernel,
        in_specs=[[[VMEM] * len(h) for h in halves]],
        out_specs=VMEM,
        out_shape=jax.ShapeDtypeStruct((len(halves) * width, rows), F32),
        compiler_params=PARAMS,
        name="turn_grads",
    )(halves)


def exchange(blocks, axis):
    n = len(blocks)
    return [blocks[0]] + [
        resident(lax.ppermute(blocks[j], axis, [(i, i ^ j) for i in range(n)])) for j in range(1, n)
    ]


def swap(blocks, paired):
    if paired:
        return exchange(blocks, "ctx")
    (block,) = blocks
    return [resident(lax.all_to_all(block, "ctx", split_axis=0, concat_axis=0, tiled=True))]


def local(n, d, query_in, key_in, value_in, grad_out, filters, skip_gain):
    query, key, value, grad = (resident(x[0]) for x in (query_in, key_in, value_in, grad_out))
    fwd, back = (resident(jnp.asarray(t)) for t in tables(filters.shape[1]))
    filters = resident(filters)
    gain = skip_gain[None, :]
    me = jnp.stack([lax.axis_index("ctx"), lax.axis_index("dp")]).astype(jnp.int32)

    got = [swap(products(h, n, PAIRED[h], me, key, value, query, grad), PAIRED[h]) for h in range(HALVES)]
    specs = [filter_spectrum(h, filters, fwd) for h in range(HALVES)]
    outs, grads = [], []
    for h in range(HALVES):
        mixed, part = conv(n, d, PAIRED[h], me, got[h], specs[h], fwd, back)
        got[h] = swap(mixed, PAIRED[h])
        grads.append(exchange(part, "dp"))
    for h in range(HALVES):
        outs = gate(h, n, PAIRED[h], me, query, grad, value, key, gain, got[h], outs)
    mixed_out, grad_query, grad_key, grad_value = outs
    return mixed_out[None], grad_query[None], grad_key[None], grad_value[None], turn_grads(grads)


def solution(mesh):
    rows = P("dp", "ctx", None)
    return jax.shard_map(
        functools.partial(local, mesh.shape["ctx"], mesh.shape["dp"]),
        mesh=mesh,
        in_specs=(rows, rows, rows, rows, P("ctx", None), P()),
        out_specs=(rows, rows, rows, rows, P("ctx", "dp")),
        check_vma=False,
    )
```

```python
import functools
import math

import jax
import jax.numpy as jnp
import ml_dtypes
import numpy as np
from jax import lax
from jax.experimental import pallas as pl
from jax.experimental.pallas import tpu as pltpu
from jax.sharding import PartitionSpec as P

F32 = jnp.float32
BF16 = jnp.bfloat16
VMEM_LIMIT = 20 * 1024 * 1024
CLASSES = 8
ROWS = 16
HALVES = 2
PARAMS = pltpu.CompilerParams(vmem_limit_bytes=VMEM_LIMIT)
SMEM = pl.BlockSpec(memory_space=pltpu.SMEM)
VMEM = pl.BlockSpec(memory_space=pltpu.VMEM)
HBM = pl.BlockSpec(memory_space=pltpu.HBM)


def tables(length):
    m2 = length // CLASSES
    c = np.arange(CLASSES)[:, None, None]
    j = np.arange(m2)[None, :, None]
    m = np.arange(m2)[None, None, :]
    turn = ((CLASSES * m + c) * (2 * j + 1)) % (4 * length)
    angle = 2 * np.pi * turn / (4 * length)
    forward = np.concatenate([np.cos(angle), -np.sin(angle)], 1)
    back = np.swapaxes(forward, 1, 2) / length

    def parts(x):
        hi = x.astype(ml_dtypes.bfloat16)
        return hi, (x - hi.astype(np.float64)).astype(ml_dtypes.bfloat16)

    return np.concatenate(parts(forward), 2), np.concatenate(parts(back), 1)


def parts(x):
    hi = x.astype(BF16)
    return hi, (x - hi.astype(F32)).astype(BF16)


def dot(a, b):
    return jnp.dot(a, b, preferred_element_type=F32)


def dft(z, sign):
    n = len(z)
    if n == 1:
        return z
    even, odd = dft(z[0::2], sign), dft(z[1::2], sign)
    low, high = [], []
    for k in range(n // 2):
        (er, ei), (zr, zi) = even[k], odd[k]
        if k == 0:
            tr, ti = zr, zi
        elif 4 * k == n:
            tr, ti = (-zi, zr) if sign > 0 else (zi, -zr)
        else:
            c, s = math.cos(2 * math.pi * k / n), sign * math.sin(2 * math.pi * k / n)
            if 8 * k == n:
                tr, ti = (c * (zr - zi), c * (zi + zr)) if sign > 0 else (c * (zr + zi), c * (zi - zr))
            elif 8 * k == 3 * n:
                tr, ti = (c * (zr + zi), c * (zi - zr)) if sign > 0 else (c * (zr - zi), c * (zi + zr))
            else:
                tr, ti = c * zr - s * zi, c * zi + s * zr
        low.append((er + tr, ei + ti))
        high.append((er - tr, ei - ti))
    return low + high


def times(x, f, conj):
    (xr, xi), (fr, fi) = x, f
    if conj:
        return xr * fr + xi * fi, xi * fr - xr * fi
    return xr * fr - xi * fi, xr * fi + xi * fr


def resident(x):
    return pltpu.with_memory_space_constraint(x, pltpu.VMEM)


def in_hbm(x):
    return pltpu.with_memory_space_constraint(x, pltpu.HBM)


def peer_columns(me, half, j, width):
    return pl.ds(pl.multiple_of((HALVES * (me[0] ^ j) + half) * width, 128), width)


def product_kernel(n, me, key, value, query, grad, *refs):
    bufs, outs, sems = refs[:4], refs[4:-1], refs[-1]
    width = outs[0].shape[-1]
    copies = {}
    for half in range(HALVES):
        for j in range(n):
            cols = peer_columns(me, half, j, width)
            copies[half, j] = [
                pltpu.make_async_copy(src.at[:, cols], dst.at[:, cols], sems.at[a, half, j])
                for a, (src, dst) in enumerate(zip((key, value, query, grad), bufs))
            ]
            for copy in copies[half, j]:
                copy.start()
    for (half, j), row in copies.items():
        for copy in row:
            copy.wait()
        k, v, q, g = (buf[:, peer_columns(me, half, j, width)].astype(F32) for buf in bufs)
        outs[half * n + j][0] = (k * v).astype(BF16)
        outs[half * n + j][1] = (g * q).astype(BF16)


def products(n, me, key, value, query, grad):
    rows, total = key.shape
    width = total // n // HALVES
    out = pl.pallas_call(
        functools.partial(product_kernel, n),
        in_specs=[SMEM] + [HBM] * 4,
        out_specs=[VMEM] * (4 + HALVES * n),
        out_shape=[pltpu.VMEM(key.shape, BF16)] * 4
        + [pltpu.VMEM((2, rows, width), BF16)] * (HALVES * n),
        scratch_shapes=[pltpu.SemaphoreType.DMA((4, HALVES, n))],
        compiler_params=PARAMS,
        name="products",
    )(me, key, value, query, grad)
    return out[:4], [out[4 + h * n : 4 + (h + 1) * n] for h in range(HALVES)]


def lane_groups(width):
    return [slice(i, i + 128) for i in range(0, width, 128)]


def filter_kernel(half, filt, fwd, spec, x, u):
    m2 = x.shape[1] // CLASSES
    width = spec.shape[-1]
    for g in range(width // 128):
        x[g] = filt[half * width + g * 128 : half * width + (g + 1) * 128, :].T
    for c in range(CLASSES):
        for g in range(width // 128):
            hi, lo = parts(x[g, pl.ds(c, m2, stride=CLASSES), :])
            u[c, :, g * 128 : (g + 1) * 128] = dot(fwd[c], jnp.concatenate([hi, hi], 0)) + dot(
                fwd[c, :, :m2], lo
            )

    def step(i, carry):
        r = pl.multiple_of(i * ROWS, ROWS)
        for lanes in lane_groups(width):
            z = [(u[c, pl.ds(r, ROWS), lanes], u[c, pl.ds(m2 + r, ROWS), lanes]) for c in range(CLASSES)]
            for k, (re, im) in enumerate(dft(z, -1)):
                spec[k, pl.ds(r, ROWS), lanes] = re
                spec[k, pl.ds(m2 + r, ROWS), lanes] = im
        return carry

    lax.fori_loop(0, m2 // ROWS, step, 0)


def filter_spectrum(half, filters, fwd):
    chans, length = filters.shape
    width = chans // HALVES
    m2 = length // CLASSES
    return pl.pallas_call(
        functools.partial(filter_kernel, half),
        in_specs=[VMEM, VMEM],
        out_specs=VMEM,
        out_shape=pltpu.VMEM((CLASSES, 2 * m2, width), F32),
        scratch_shapes=[
            pltpu.VMEM((width // 128, length, 128), F32),
            pltpu.VMEM((CLASSES, 2 * m2, width), F32),
        ],
        compiler_params=PARAMS,
        name="filter_spectrum",
    )(filters, fwd)


def conv_kernel(n, d, half, me, *refs):
    got, (filt, fwd, back), refs = refs[:n], refs[n : n + 3], refs[n + 3 :]
    refs = refs[d * (half > 0) :]
    out, grads, (nat, x, u, y) = refs[:n], refs[n : n + d], refs[n + d :]
    _, rows, width = got[0].shape
    m2 = n * rows // CLASSES
    per = grads[0].shape[1]
    groups = lane_groups(width)

    for a in range(2):
        for g, lanes in enumerate(groups):
            for j in range(n):
                at = pl.multiple_of((me[0] ^ j) * rows, rows)
                nat[a, g, pl.ds(at, rows)] = got[j][a, :, lanes].astype(F32)
            for c in range(CLASSES):
                x[a, c, :, lanes] = nat[a, g, pl.ds(c, m2, stride=CLASSES), :].astype(BF16)
        for c in range(CLASSES):
            data = x[a, c]
            u[a, c] = dot(fwd[c], jnp.concatenate([data, data], 0))

    def step(i, carry):
        r = pl.multiple_of(i * ROWS, ROWS)
        re, im = pl.ds(r, ROWS), pl.ds(m2 + r, ROWS)
        for lanes in groups:
            kv = dft([(u[0, c, re, lanes], u[0, c, im, lanes]) for c in range(CLASSES)], -1)
            wt = dft([(u[1, c, re, lanes], u[1, c, im, lanes]) for c in range(CLASSES)], -1)
            fs = [(filt[k, re, lanes], filt[k, im, lanes]) for k in range(CLASSES)]
            for o, (left, right, conj) in enumerate([(kv, fs, False), (wt, fs, True), (wt, kv, True)]):
                z = dft([times(s, t, conj) for s, t in zip(left, right)], 1)
                for c in range(CLASSES):
                    y[o, c, re, lanes] = z[c][0].astype(BF16)
                    y[o, c, im, lanes] = z[c][1].astype(BF16)
        return carry

    lax.fori_loop(0, m2 // ROWS, step, 0)

    for o in range(3):
        for c in range(CLASSES):
            both = dot(back[c], y[o, c])
            both = both[:m2] + both[m2:]
            for g, lanes in enumerate(groups):
                nat[o, g, pl.ds(c, m2, stride=CLASSES), :] = both[:, lanes]
        for g, lanes in enumerate(groups):
            if o < 2:
                for j in range(n):
                    at = pl.multiple_of((me[0] ^ j) * rows, rows)
                    out[j][o, :, lanes] = nat[o, g, pl.ds(at, rows)].astype(BF16)
            else:
                for j in range(d):
                    at = pl.multiple_of((me[1] ^ j) * per, per)
                    grads[j][half, :, lanes] = nat[o, g, pl.ds(at, per)].astype(grads[j].dtype)


def conv(n, d, half, me, got, filt, fwd, back, grads):
    _, rows, width = got[0].shape
    length = n * rows
    m2 = length // CLASSES
    out = pl.pallas_call(
        functools.partial(conv_kernel, n, d, half),
        in_specs=[SMEM] + [VMEM] * (n + 3 + len(grads)),
        out_specs=[VMEM] * (n + d),
        out_shape=[pltpu.VMEM(got[0].shape, BF16)] * n
        + [pltpu.VMEM((HALVES, length // d, width), F32 if j == 0 else BF16) for j in range(d)],
        scratch_shapes=[
            pltpu.VMEM((3, width // 128, length, 128), F32),
            pltpu.VMEM((2, CLASSES, m2, width), BF16),
            pltpu.VMEM((2, CLASSES, 2 * m2, width), F32),
            pltpu.VMEM((3, CLASSES, 2 * m2, width), BF16),
        ],
        input_output_aliases={n + 4 + j: n + j for j in range(len(grads))},
        compiler_params=PARAMS,
        name="conv",
    )(me, *got, filt, fwd, back, *grads)
    return out[:n], out[n:]


def gate_kernel(half, n, me, query, grad, value, key, gain, *refs):
    got, outs, (sent, sems) = refs[:n], refs[-6:-2], refs[-2:]
    width = got[0].shape[-1]
    copies = []
    for j in range(n):
        cols = peer_columns(me, half, j, width)
        scale = gain[:, cols]
        q, g, v, k = (x[:, cols].astype(F32) for x in (query, grad, value, key))
        mixing = got[j][0].astype(F32) + scale * (k * v).astype(BF16).astype(F32)
        sent[0, j] = (q * mixing).astype(BF16)
        sent[1, j] = (g * mixing).astype(BF16)
        total = got[j][1].astype(F32) + scale * (g * q).astype(BF16).astype(F32)
        sent[2, j] = (total * v).astype(BF16)
        sent[3, j] = (total * k).astype(BF16)
        for a in range(4):
            copy = pltpu.make_async_copy(sent.at[a, j], outs[a].at[:, cols], sems.at[a, j])
            copy.start()
            copies.append(copy)
    for copy in copies:
        copy.wait()


def gate(half, me, query, grad, value, key, gain, got, outs):
    n = len(got)
    _, rows, width = got[0].shape
    return pl.pallas_call(
        functools.partial(gate_kernel, half, n),
        in_specs=[SMEM] + [VMEM] * (5 + n) + [HBM] * len(outs),
        out_specs=[HBM] * 4,
        out_shape=[jax.ShapeDtypeStruct(query.shape, BF16)] * 4,
        scratch_shapes=[
            pltpu.VMEM((4, n, rows, width), BF16),
            pltpu.SemaphoreType.DMA((4, n)),
        ],
        input_output_aliases={6 + n + i: i for i in range(len(outs))},
        compiler_params=PARAMS,
        name="gate",
    )(me, query, grad, value, key, gain, *got, *outs)


def turn_kernel(*refs):
    parts, out = refs[:-1], refs[-1]
    for half in range(HALVES):
        total = parts[0][half]
        for part in parts[1:]:
            total = total + part[half].astype(F32)
        width = total.shape[1]
        out[half * width : (half + 1) * width] = total.T


def turn_grads(parts):
    _, rows, width = parts[0].shape
    return pl.pallas_call(
        turn_kernel,
        in_specs=[VMEM] * len(parts),
        out_specs=VMEM,
        out_shape=jax.ShapeDtypeStruct((HALVES * width, rows), F32),
        compiler_params=PARAMS,
        name="turn_grads",
    )(*parts)


def exchange(blocks, axis):
    n = len(blocks)
    return [blocks[0]] + [
        resident(lax.ppermute(blocks[j], axis, [(i, i ^ j) for i in range(n)])) for j in range(1, n)
    ]


def local(n, d, query_in, key_in, value_in, grad_out, filters, skip_gain):
    fwd, back = (resident(jnp.asarray(t)) for t in tables(filters.shape[1]))
    filters = resident(filters)
    gain = skip_gain[None, :]
    me = jnp.stack([lax.axis_index("ctx"), lax.axis_index("dp")]).astype(jnp.int32)

    arrays = [in_hbm(x[0]) for x in (key_in, value_in, query_in, grad_out)]
    (key, value, query, grad), got = products(n, me, *arrays)
    got = [exchange(blocks, "ctx") for blocks in got]
    specs = [filter_spectrum(h, filters, fwd) for h in range(HALVES)]
    outs, grads = [], []
    for h in range(HALVES):
        mixed, grads = conv(n, d, h, me, got[h], specs[h], fwd, back, grads)
        got[h] = exchange(mixed, "ctx")
    grads = exchange(grads, "dp")
    for h in range(HALVES):
        outs = gate(h, me, query, grad, value, key, gain, got[h], outs)
    mixed_out, grad_query, grad_key, grad_value = outs
    return mixed_out[None], grad_query[None], grad_key[None], grad_value[None], turn_grads(grads)


def solution(mesh):
    rows = P("dp", "ctx", None)
    return jax.shard_map(
        functools.partial(local, mesh.shape["ctx"], mesh.shape["dp"]),
        mesh=mesh,
        in_specs=(rows, rows, rows, rows, P("ctx", None), P()),
        out_specs=(rows, rows, rows, rows, P("ctx", "dp")),
        check_vma=False,
    )
```

```python
import functools
import math

import jax
import jax.numpy as jnp
import ml_dtypes
import numpy as np
from jax import lax
from jax.experimental import pallas as pl
from jax.experimental.pallas import tpu as pltpu
from jax.sharding import PartitionSpec as P

F32 = jnp.float32
BF16 = jnp.bfloat16
VMEM_LIMIT = 20 * 1024 * 1024
CLASSES = 8
ROWS = 16
HALVES = 2
PARAMS = pltpu.CompilerParams(vmem_limit_bytes=VMEM_LIMIT)
SMEM = pl.BlockSpec(memory_space=pltpu.SMEM)
VMEM = pl.BlockSpec(memory_space=pltpu.VMEM)
HBM = pl.BlockSpec(memory_space=pltpu.HBM)


def tables(length):
    m2 = length // CLASSES
    c = np.arange(CLASSES)[:, None, None]
    j = np.arange(m2)[None, :, None]
    m = np.arange(m2)[None, None, :]
    turn = ((CLASSES * m + c) * (2 * j + 1)) % (4 * length)
    angle = 2 * np.pi * turn / (4 * length)
    forward = np.concatenate([np.cos(angle), -np.sin(angle)], 1)
    back = np.swapaxes(forward, 1, 2) / length

    def parts(x):
        hi = x.astype(ml_dtypes.bfloat16)
        return hi, (x - hi.astype(np.float64)).astype(ml_dtypes.bfloat16)

    return np.concatenate(parts(forward), 2), np.concatenate(parts(back), 1)


def parts(x):
    hi = x.astype(BF16)
    return hi, (x - hi.astype(F32)).astype(BF16)


def dot(a, b):
    return jnp.dot(a, b, preferred_element_type=F32)


def dft(z, sign):
    n = len(z)
    if n == 1:
        return z
    even, odd = dft(z[0::2], sign), dft(z[1::2], sign)
    low, high = [], []
    for k in range(n // 2):
        (er, ei), (zr, zi) = even[k], odd[k]
        if k == 0:
            tr, ti = zr, zi
        elif 4 * k == n:
            tr, ti = (-zi, zr) if sign > 0 else (zi, -zr)
        else:
            c, s = math.cos(2 * math.pi * k / n), sign * math.sin(2 * math.pi * k / n)
            if 8 * k == n:
                tr, ti = (c * (zr - zi), c * (zi + zr)) if sign > 0 else (c * (zr + zi), c * (zi - zr))
            elif 8 * k == 3 * n:
                tr, ti = (c * (zr + zi), c * (zi - zr)) if sign > 0 else (c * (zr - zi), c * (zi + zr))
            else:
                tr, ti = c * zr - s * zi, c * zi + s * zr
        low.append((er + tr, ei + ti))
        high.append((er - tr, ei - ti))
    return low + high


def times(x, f, conj):
    (xr, xi), (fr, fi) = x, f
    if conj:
        return xr * fr + xi * fi, xi * fr - xr * fi
    return xr * fr - xi * fi, xr * fi + xi * fr


def resident(x):
    return pltpu.with_memory_space_constraint(x, pltpu.VMEM)


def in_hbm(x):
    return pltpu.with_memory_space_constraint(x, pltpu.HBM)


def peer_columns(me, half, j, width):
    return pl.ds(pl.multiple_of((HALVES * (me[0] ^ j) + half) * width, 128), width)


def product_kernel(n, me, key, value, query, grad, *refs):
    bufs, outs, sems = refs[:4], refs[4:-1], refs[-1]
    width = outs[0].shape[-1]
    copies = {}
    for half in range(HALVES):
        for j in range(n):
            cols = peer_columns(me, half, j, width)
            copies[half, j] = [
                pltpu.make_async_copy(src.at[:, cols], dst.at[:, cols], sems.at[a, half, j])
                for a, (src, dst) in enumerate(zip((key, value, query, grad), bufs))
            ]
            for copy in copies[half, j]:
                copy.start()
    for (half, j), row in copies.items():
        for copy in row:
            copy.wait()
        k, v, q, g = (buf[:, peer_columns(me, half, j, width)].astype(F32) for buf in bufs)
        outs[half * n + j][0] = (k * v).astype(BF16)
        outs[half * n + j][1] = (g * q).astype(BF16)


def products(n, me, key, value, query, grad):
    rows, total = key.shape
    width = total // n // HALVES
    out = pl.pallas_call(
        functools.partial(product_kernel, n),
        in_specs=[SMEM] + [HBM] * 4,
        out_specs=[VMEM] * (4 + HALVES * n),
        out_shape=[pltpu.VMEM(key.shape, BF16)] * 4
        + [pltpu.VMEM((2, rows, width), BF16)] * (HALVES * n),
        scratch_shapes=[pltpu.SemaphoreType.DMA((4, HALVES, n))],
        compiler_params=PARAMS,
        name="products",
    )(me, key, value, query, grad)
    return out[:4], [out[4 + h * n : 4 + (h + 1) * n] for h in range(HALVES)]


def lane_groups(width):
    return [slice(i, i + 128) for i in range(0, width, 128)]


def filter_kernel(filt, fwd, *refs):
    specs, (x, u) = refs[-2 - HALVES : -2], refs[-2:]
    m2 = x.shape[1] // CLASSES
    width = specs[0].shape[-1]
    groups = lane_groups(width)
    for half, spec in enumerate(specs):
        for g, lanes in enumerate(groups):
            x[g] = filt[half * width + lanes.start : half * width + lanes.stop, :].T
        for c in range(CLASSES):
            for g, lanes in enumerate(groups):
                hi, lo = parts(x[g, pl.ds(c, m2, stride=CLASSES), :])
                u[c, :, lanes] = dot(fwd[c], jnp.concatenate([hi, hi], 0)) + dot(fwd[c, :, :m2], lo)

        def step(i, carry):
            r = pl.multiple_of(i * ROWS, ROWS)
            re, im = pl.ds(r, ROWS), pl.ds(m2 + r, ROWS)
            for lanes in groups:
                z = dft([(u[c, re, lanes], u[c, im, lanes]) for c in range(CLASSES)], -1)
                for k in range(CLASSES):
                    spec[k, re, lanes], spec[k, im, lanes] = z[k]
            return carry

        lax.fori_loop(0, m2 // ROWS, step, 0)


def filter_spectra(filters, fwd, after, then):
    chans, length = filters.shape
    width = chans // HALVES
    m2 = length // CLASSES
    out = pl.pallas_call(
        filter_kernel,
        in_specs=[VMEM] * (2 + len(after) + len(then)),
        out_specs=[VMEM] * (len(then) + HALVES),
        out_shape=[pltpu.VMEM(t.shape, t.dtype) for t in then]
        + [pltpu.VMEM((CLASSES, 2 * m2, width), F32)] * HALVES,
        scratch_shapes=[
            pltpu.VMEM((width // 128, length, 128), F32),
            pltpu.VMEM((CLASSES, 2 * m2, width), F32),
        ],
        input_output_aliases={2 + len(after) + i: i for i in range(len(then))},
        compiler_params=PARAMS,
        name="filter_spectra",
    )(filters, fwd, *after, *then)
    return out[len(then) :], out[: len(then)]


def conv_kernel(n, d, me, *refs):
    got, (filt, fwd, back) = refs[:n], refs[n : n + 3]
    refs = refs[-(n + d + 4) :]
    out, grads, (nat, x, u, y) = refs[:n], refs[n : n + d], refs[n + d :]
    _, rows, width = got[0].shape
    m2 = n * rows // CLASSES
    per = grads[0].shape[0]
    groups = lane_groups(width)

    for a in range(2):
        for g, lanes in enumerate(groups):
            for j in range(n):
                at = pl.multiple_of((me[0] ^ j) * rows, rows)
                nat[a, g, pl.ds(at, rows)] = got[j][a, :, lanes].astype(F32)
            for c in range(CLASSES):
                x[a, c, :, lanes] = nat[a, g, pl.ds(c, m2, stride=CLASSES), :].astype(BF16)
        for c in range(CLASSES):
            data = x[a, c]
            u[a, c] = dot(fwd[c], jnp.concatenate([data, data], 0))

    def step(i, carry):
        r = pl.multiple_of(i * ROWS, ROWS)
        re, im = pl.ds(r, ROWS), pl.ds(m2 + r, ROWS)
        for lanes in groups:
            kv = dft([(u[0, c, re, lanes], u[0, c, im, lanes]) for c in range(CLASSES)], -1)
            wt = dft([(u[1, c, re, lanes], u[1, c, im, lanes]) for c in range(CLASSES)], -1)
            fs = [(filt[k, re, lanes], filt[k, im, lanes]) for k in range(CLASSES)]
            for o, (left, right, conj) in enumerate([(kv, fs, False), (wt, fs, True), (wt, kv, True)]):
                z = dft([times(s, t, conj) for s, t in zip(left, right)], 1)
                for c in range(CLASSES):
                    y[o, c, re, lanes] = z[c][0].astype(BF16)
                    y[o, c, im, lanes] = z[c][1].astype(BF16)
        return carry

    lax.fori_loop(0, m2 // ROWS, step, 0)

    for o in range(3):
        for c in range(CLASSES):
            both = dot(back[c], y[o, c])
            both = both[:m2] + both[m2:]
            for g, lanes in enumerate(groups):
                nat[o, g, pl.ds(c, m2, stride=CLASSES), :] = both[:, lanes]
        for g, lanes in enumerate(groups):
            if o < 2:
                for j in range(n):
                    at = pl.multiple_of((me[0] ^ j) * rows, rows)
                    out[j][o, :, lanes] = nat[o, g, pl.ds(at, rows)].astype(BF16)
            else:
                for j in range(d):
                    at = pl.multiple_of((me[1] ^ j) * per, per)
                    grads[j][:, lanes] = nat[o, g, pl.ds(at, per)].astype(grads[j].dtype)


def conv(n, d, me, got, filt, fwd, back, after):
    _, rows, width = got[0].shape
    length = n * rows
    m2 = length // CLASSES
    out = pl.pallas_call(
        functools.partial(conv_kernel, n, d),
        in_specs=[SMEM] + [VMEM] * (n + 3 + len(after)),
        out_specs=[VMEM] * (n + d),
        out_shape=[pltpu.VMEM(got[0].shape, BF16)] * n
        + [pltpu.VMEM((length // d, width), F32 if j == 0 else BF16) for j in range(d)],
        scratch_shapes=[
            pltpu.VMEM((3, width // 128, length, 128), F32),
            pltpu.VMEM((2, CLASSES, m2, width), BF16),
            pltpu.VMEM((2, CLASSES, 2 * m2, width), F32),
            pltpu.VMEM((3, CLASSES, 2 * m2, width), BF16),
        ],
        compiler_params=PARAMS,
        name="conv",
    )(me, *got, filt, fwd, back, *after)
    return out[:n], out[n:]


def gate_kernel(half, n, me, query, grad, value, key, gain, *refs):
    got, outs, (sent, sems) = refs[:n], refs[-6:-2], refs[-2:]
    width = got[0].shape[-1]
    copies = []
    for j in range(n):
        cols = peer_columns(me, half, j, width)
        scale = gain[:, cols]
        q, g, v, k = (x[:, cols].astype(F32) for x in (query, grad, value, key))
        mixing = got[j][0].astype(F32) + scale * (k * v).astype(BF16).astype(F32)
        sent[0, j] = (q * mixing).astype(BF16)
        sent[1, j] = (g * mixing).astype(BF16)
        total = got[j][1].astype(F32) + scale * (g * q).astype(BF16).astype(F32)
        sent[2, j] = (total * v).astype(BF16)
        sent[3, j] = (total * k).astype(BF16)
        for a in range(4):
            copy = pltpu.make_async_copy(sent.at[a, j], outs[a].at[:, cols], sems.at[a, j])
            copy.start()
            copies.append(copy)
    for copy in copies:
        copy.wait()


def gate(half, me, query, grad, value, key, gain, got, outs):
    n = len(got)
    _, rows, width = got[0].shape
    return pl.pallas_call(
        functools.partial(gate_kernel, half, n),
        in_specs=[SMEM] + [VMEM] * (5 + n) + [HBM] * len(outs),
        out_specs=[HBM] * 4,
        out_shape=[jax.ShapeDtypeStruct(query.shape, BF16)] * 4,
        scratch_shapes=[
            pltpu.VMEM((4, n, rows, width), BF16),
            pltpu.SemaphoreType.DMA((4, n)),
        ],
        input_output_aliases={6 + n + i: i for i in range(len(outs))},
        compiler_params=PARAMS,
        name="gate",
    )(me, query, grad, value, key, gain, *got, *outs)


def turn_kernel(d, *refs):
    out = refs[-1]
    for half in range(HALVES):
        first, *rest = refs[half * d : (half + 1) * d]
        total = first[...]
        for part in rest:
            total = total + part[...].astype(F32)
        width = total.shape[1]
        out[half * width : (half + 1) * width] = total.T


def turn_grads(halves):
    d = len(halves[0])
    rows, width = halves[0][0].shape
    return pl.pallas_call(
        functools.partial(turn_kernel, d),
        in_specs=[VMEM] * (HALVES * d),
        out_specs=VMEM,
        out_shape=jax.ShapeDtypeStruct((HALVES * width, rows), F32),
        compiler_params=PARAMS,
        name="turn_grads",
    )(*halves[0], *halves[1])


def exchange(blocks, axis):
    n = len(blocks)
    return [blocks[0]] + [
        resident(lax.ppermute(blocks[j], axis, [(i, i ^ j) for i in range(n)])) for j in range(1, n)
    ]


def local(n, d, query_in, key_in, value_in, grad_out, filters, skip_gain):
    fwd, back = (resident(jnp.asarray(t)) for t in tables(filters.shape[1]))
    filters = resident(filters)
    gain = skip_gain[None, :]
    me = jnp.stack([lax.axis_index("ctx"), lax.axis_index("dp")]).astype(jnp.int32)

    arrays = [in_hbm(x[0]) for x in (key_in, value_in, query_in, grad_out)]
    (key, value, query, grad), got = products(n, me, *arrays)
    first = exchange(got[0], "ctx")
    specs, sent = filter_spectra(filters, fwd, first[1:5], got[1])
    second = exchange(sent, "ctx")
    mixed, part = conv(n, d, me, first, specs[0], fwd, back, [])
    first = exchange(mixed, "ctx")
    grads = [exchange(part, "dp")]
    mixed, part = conv(n, d, me, second, specs[1], fwd, back, first[1:3])
    grads.append(exchange(part, "dp"))
    second = exchange(mixed, "ctx")
    outs = gate(0, me, query, grad, value, key, gain, first, [])
    outs = gate(1, me, query, grad, value, key, gain, second, outs)
    mixed_out, grad_query, grad_key, grad_value = outs
    return mixed_out[None], grad_query[None], grad_key[None], grad_value[None], turn_grads(grads)


def solution(mesh):
    rows = P("dp", "ctx", None)
    return jax.shard_map(
        functools.partial(local, mesh.shape["ctx"], mesh.shape["dp"]),
        mesh=mesh,
        in_specs=(rows, rows, rows, rows, P("ctx", None), P()),
        out_specs=(rows, rows, rows, rows, P("ctx", "dp")),
        check_vma=False,
    )
```

```python
import functools
import math

import jax
import jax.numpy as jnp
import ml_dtypes
import numpy as np
from jax import lax
from jax.experimental import pallas as pl
from jax.experimental.pallas import tpu as pltpu
from jax.sharding import PartitionSpec as P

F32 = jnp.float32
BF16 = jnp.bfloat16
CLASSES = 8
HALVES = 2
STEPS = 4
PARAMS = pltpu.CompilerParams(vmem_limit_bytes=16 * 1024 * 1024)
CONV_PARAMS = pltpu.CompilerParams(vmem_limit_bytes=34 * 1024 * 1024)
SMEM = pl.BlockSpec(memory_space=pltpu.SMEM)
VMEM = pl.BlockSpec(memory_space=pltpu.VMEM)
HBM = pl.BlockSpec(memory_space=pltpu.HBM)


def tables(length):
    m2 = length // CLASSES
    c = np.arange(CLASSES)[:, None, None]
    j = np.arange(m2)[None, :, None]
    m = np.arange(m2)[None, None, :]
    turn = ((CLASSES * m + c) * (2 * j + 1)) % (4 * length)
    angle = 2 * np.pi * turn / (4 * length)
    forward = np.concatenate([np.cos(angle), -np.sin(angle)], 1)
    back = np.swapaxes(forward, 1, 2) / length

    def parts(x):
        hi = x.astype(ml_dtypes.bfloat16)
        return hi, (x - hi.astype(np.float64)).astype(ml_dtypes.bfloat16)

    return np.concatenate(parts(forward), 2), np.concatenate(parts(back), 1)


def parts(x):
    hi = x.astype(BF16)
    return hi, (x - hi.astype(F32)).astype(BF16)


def dot(a, b):
    return jnp.dot(a, b, preferred_element_type=F32)


def dft(z, sign):
    n = len(z)
    if n == 1:
        return z
    even, odd = dft(z[0::2], sign), dft(z[1::2], sign)
    low, high = [], []
    for k in range(n // 2):
        (er, ei), (zr, zi) = even[k], odd[k]
        if k == 0:
            tr, ti = zr, zi
        elif 4 * k == n:
            tr, ti = (-zi, zr) if sign > 0 else (zi, -zr)
        else:
            c, s = math.cos(2 * math.pi * k / n), sign * math.sin(2 * math.pi * k / n)
            if 8 * k == n:
                tr, ti = (c * (zr - zi), c * (zi + zr)) if sign > 0 else (c * (zr + zi), c * (zi - zr))
            elif 8 * k == 3 * n:
                tr, ti = (c * (zr + zi), c * (zi - zr)) if sign > 0 else (c * (zr - zi), c * (zi + zr))
            else:
                tr, ti = c * zr - s * zi, c * zi + s * zr
        low.append((er + tr, ei + ti))
        high.append((er - tr, ei - ti))
    return low + high


def times(x, f, conj):
    (xr, xi), (fr, fi) = x, f
    if conj:
        return xr * fr + xi * fi, xi * fr - xr * fi
    return xr * fr - xi * fi, xr * fi + xi * fr


def resident(x):
    return pltpu.with_memory_space_constraint(x, pltpu.VMEM)


def in_hbm(x):
    return pltpu.with_memory_space_constraint(x, pltpu.HBM)


def peer_columns(me, j, width):
    return pl.ds(pl.multiple_of((me[0] ^ j) * width, 128), width)


def product_kernel(n, me, key, value, query, grad, *refs):
    bufs, outs, sems = refs[:4], refs[4:-1], refs[-1]
    _, rows, width = outs[0].shape
    step = rows // STEPS
    copies = []
    for i in range(STEPS):
        at = pl.ds(i * step, step)
        copies.append(
            [
                pltpu.make_async_copy(src.at[at], dst.at[at], sems.at[a, i])
                for a, (src, dst) in enumerate(zip((key, value, query, grad), bufs))
            ]
        )
        for copy in copies[i]:
            copy.start()
    for i in range(STEPS):
        at = pl.ds(i * step, step)
        for a, (left, right) in enumerate((bufs[:2], bufs[2:])):
            copies[i][2 * a].wait()
            copies[i][2 * a + 1].wait()
            for j, out in enumerate(outs):
                cols = peer_columns(me, j, width)
                out[a, at] = (left[at, cols].astype(F32) * right[at, cols].astype(F32)).astype(BF16)


def products(n, me, key, value, query, grad):
    rows, total = key.shape
    out = pl.pallas_call(
        functools.partial(product_kernel, n),
        in_specs=[SMEM] + [HBM] * 4,
        out_specs=[VMEM] * (4 + n),
        out_shape=[pltpu.VMEM(key.shape, BF16)] * 4
        + [pltpu.VMEM((2, rows, total // n), BF16)] * n,
        scratch_shapes=[pltpu.SemaphoreType.DMA((4, STEPS))],
        compiler_params=PARAMS,
        name="products",
    )(me, key, value, query, grad)
    return out[:4], out[4:]


def lane_groups(width):
    return [slice(i, i + 128) for i in range(0, width, 128)]


def filter_kernel(filt, fwd, spec, x, u):
    m2, width = x.shape[1] // CLASSES, u.shape[-1]
    groups = lane_groups(width)
    rows = m2 // CLASSES
    for half in range(HALVES):
        for g, lanes in enumerate(groups):
            x[g] = filt[half * width + lanes.start : half * width + lanes.stop, :].T
        for c in range(CLASSES):
            for g, lanes in enumerate(groups):
                hi, lo = parts(x[g, pl.ds(c, m2, stride=CLASSES), :])
                u[c, :, lanes] = dot(fwd[c], jnp.concatenate([hi, hi], 0)) + dot(fwd[c, :, :m2], lo)

        def step(i, carry):
            r = pl.multiple_of(i * rows, rows)
            re, im = pl.ds(r, rows), pl.ds(m2 + r, rows)
            for lanes in groups:
                z = dft([(u[c, re, lanes], u[c, im, lanes]) for c in range(CLASSES)], -1)
                for k in range(CLASSES):
                    spec[half, k, re, lanes], spec[half, k, im, lanes] = z[k]
            return carry

        lax.fori_loop(0, CLASSES, step, 0)


def filter_spectra(filters, fwd):
    chans, length = filters.shape
    width = chans // HALVES
    m2 = length // CLASSES
    return pl.pallas_call(
        filter_kernel,
        in_specs=[VMEM, VMEM],
        out_specs=VMEM,
        out_shape=pltpu.VMEM((HALVES, CLASSES, 2 * m2, width), F32),
        scratch_shapes=[
            pltpu.VMEM((width // 128, length, 128), F32),
            pltpu.VMEM((CLASSES, 2 * m2, width), F32),
        ],
        compiler_params=PARAMS,
        name="filter_spectra",
    )(filters, fwd)


def conv_kernel(n, d, me, *refs):
    got, (filt, fwd, back), refs = refs[:n], refs[n : n + 3], refs[n + 3 :]
    out, (keep, send, nat), refs = refs[:n], refs[n : n + 3], refs[n + 3 :]
    xs, us, ys, turned = (refs[i : i + HALVES] for i in range(0, 4 * HALVES, HALVES))
    rows = got[0].shape[1]
    m2, width = xs[0].shape[2:]
    per = keep.shape[1]
    groups = lane_groups(width)
    step_rows = m2 // CLASSES

    def load(half):
        for a in range(2):
            for g, lanes in enumerate(groups):
                chans = slice(half * width + lanes.start, half * width + lanes.stop)
                for j in range(n):
                    at = pl.multiple_of((me[0] ^ j) * rows, rows)
                    nat[a, g, pl.ds(at, rows)] = got[j][a, :, chans].astype(F32)
                for c in range(CLASSES):
                    piece = nat[a, g, pl.ds(c, m2, stride=CLASSES), :]
                    xs[half][a, c, :, lanes] = piece.astype(BF16)

    def forward(half, c):
        for a in range(2):
            data = xs[half][a, c]
            us[half][a, c] = dot(fwd[c], jnp.concatenate([data, data], 0))

    def middle(half, i):
        u, y = us[half], ys[half]
        r = pl.multiple_of(i * step_rows, step_rows)
        re, im = pl.ds(r, step_rows), pl.ds(m2 + r, step_rows)
        for lanes in groups:
            kv = dft([(u[0, c, re, lanes], u[0, c, im, lanes]) for c in range(CLASSES)], -1)
            wt = dft([(u[1, c, re, lanes], u[1, c, im, lanes]) for c in range(CLASSES)], -1)
            fs = [(filt[half, k, re, lanes], filt[half, k, im, lanes]) for k in range(CLASSES)]
            for o, (left, right, conj) in enumerate([(kv, fs, False), (wt, fs, True), (wt, kv, True)]):
                z = dft([times(s, t, conj) for s, t in zip(left, right)], 1)
                for c in range(CLASSES):
                    y[o, c, re, lanes] = z[c][0].astype(BF16)
                    y[o, c, im, lanes] = z[c][1].astype(BF16)

    def inverse(half, c):
        for o in range(3):
            both = dot(back[c], ys[half][o, c])
            both = both[:m2] + both[m2:]
            for g, lanes in enumerate(groups):
                turned[half][o, g, pl.ds(c, m2, stride=CLASSES), :] = both[:, lanes]

    def store(half):
        for g, lanes in enumerate(groups):
            chans = slice(half * width + lanes.start, half * width + lanes.stop)
            for o in range(2):
                for j in range(n):
                    at = pl.multiple_of((me[0] ^ j) * rows, rows)
                    out[j][o, :, chans] = turned[half][o, g, pl.ds(at, rows)].astype(BF16)
            for j in range(d):
                at = pl.multiple_of((me[1] ^ j) * per, per)
                part = turned[half][2, g, pl.ds(at, per)]
                if j % 2:
                    send[j // 2, :, chans] = part.astype(BF16)
                else:
                    keep[j // 2, :, chans] = part

    def first(i, carry):
        middle(0, i)
        forward(1, i)
        return carry

    def second(i, carry):
        middle(1, i)
        inverse(0, i)
        return carry

    load(0)
    for c in range(CLASSES):
        forward(0, c)
    load(1)
    lax.fori_loop(0, CLASSES, first, 0)
    lax.fori_loop(0, CLASSES, second, 0)
    store(0)
    for c in range(CLASSES):
        inverse(1, c)
    store(1)


def conv(n, d, me, got, filt, fwd, back):
    _, rows, chans = got[0].shape
    width = chans // HALVES
    length = n * rows
    m2 = length // CLASSES
    natural = (width // 128, length, 128)
    out = pl.pallas_call(
        functools.partial(conv_kernel, n, d),
        in_specs=[SMEM] + [VMEM] * (n + 3),
        out_specs=[VMEM] * (n + 2),
        out_shape=[pltpu.VMEM(got[0].shape, BF16)] * n
        + [pltpu.VMEM((d // 2, length // d, chans), dtype) for dtype in (F32, BF16)],
        scratch_shapes=[pltpu.VMEM((2, *natural), F32)]
        + [pltpu.VMEM((2, CLASSES, m2, width), BF16)] * HALVES
        + [pltpu.VMEM((2, CLASSES, 2 * m2, width), F32)] * HALVES
        + [pltpu.VMEM((3, CLASSES, 2 * m2, width), BF16)] * HALVES
        + [pltpu.VMEM((3, *natural), F32)] * HALVES,
        compiler_params=CONV_PARAMS,
        name="conv",
    )(me, *got, filt, fwd, back)
    return out[:n], out[n], out[n + 1]


def gate_kernel(js, me, query, grad, value, key, gain, *refs):
    got, outs, (sent, sems) = refs[: len(js)], refs[-6:-2], refs[-2:]
    width = got[0].shape[-1]
    copies = []
    for i, j in enumerate(js):
        cols = peer_columns(me, j, width)
        scale = gain[:, cols]
        q, g, v, k = (x[:, cols].astype(F32) for x in (query, grad, value, key))
        mixing = got[i][0].astype(F32) + scale * (k * v).astype(BF16).astype(F32)
        sent[0, i] = (q * mixing).astype(BF16)
        sent[1, i] = (g * mixing).astype(BF16)
        total = got[i][1].astype(F32) + scale * (g * q).astype(BF16).astype(F32)
        sent[2, i] = (total * v).astype(BF16)
        sent[3, i] = (total * k).astype(BF16)
        for a in range(4):
            copy = pltpu.make_async_copy(sent.at[a, i], outs[a].at[:, cols], sems.at[a, i])
            copy.start()
            copies.append(copy)
    for copy in copies:
        copy.wait()


def gate(js, me, query, grad, value, key, gain, got, outs):
    _, rows, width = got[0].shape
    return pl.pallas_call(
        functools.partial(gate_kernel, js),
        in_specs=[SMEM] + [VMEM] * (5 + len(js)) + [HBM] * len(outs),
        out_specs=[HBM] * 4,
        out_shape=[jax.ShapeDtypeStruct(query.shape, BF16)] * 4,
        scratch_shapes=[
            pltpu.VMEM((4, len(js), rows, width), BF16),
            pltpu.SemaphoreType.DMA((4, len(js))),
        ],
        input_output_aliases={6 + len(js) + i: i for i in range(len(outs))},
        compiler_params=PARAMS,
        name="gate",
    )(me, query, grad, value, key, gain, *(got[j] for j in js), *outs)


def add_kernel(keep, got, new_keep, new_send):
    for i in range(new_keep.shape[0]):
        new_keep[i] = keep[2 * i] + got[2 * i].astype(F32)
        new_send[i] = (keep[2 * i + 1] + got[2 * i + 1].astype(F32)).astype(BF16)


def turn_kernel(keep, got, out):
    out[...] = (keep[0] + got[0].astype(F32)).T


def sum_grads(d, keep, send):
    _, per, chans = keep.shape
    bit = 1
    while True:
        got = resident(lax.ppermute(send, "dp", [(i, i ^ bit) for i in range(d)]))
        if keep.shape[0] == 1:
            break
        shape = (keep.shape[0] // 2, per, chans)
        keep, send = pl.pallas_call(
            add_kernel,
            in_specs=[VMEM] * 2,
            out_specs=[VMEM] * 2,
            out_shape=[pltpu.VMEM(shape, F32), pltpu.VMEM(shape, BF16)],
            compiler_params=PARAMS,
            name="add_grads",
        )(keep, got)
        bit *= 2
    return pl.pallas_call(
        turn_kernel,
        in_specs=[VMEM] * 2,
        out_specs=VMEM,
        out_shape=jax.ShapeDtypeStruct((chans, per), F32),
        compiler_params=PARAMS,
        name="turn_grads",
    )(keep, got)


def exchange(blocks, axis):
    n = len(blocks)
    return [blocks[0]] + [
        resident(lax.ppermute(blocks[j], axis, [(i, i ^ j) for i in range(n)])) for j in range(1, n)
    ]


def local(n, d, query_in, key_in, value_in, grad_out, filters, skip_gain):
    fwd, back = (resident(jnp.asarray(t)) for t in tables(filters.shape[1]))
    filters = resident(filters)
    gain = skip_gain[None, :]
    me = jnp.stack([lax.axis_index("ctx"), lax.axis_index("dp")]).astype(jnp.int32)

    arrays = [in_hbm(x[0]) for x in (key_in, value_in, query_in, grad_out)]
    (key, value, query, grad), got = products(n, me, *arrays)
    got = exchange(got, "ctx")
    spec = filter_spectra(filters, fwd)
    mixed, keep, send = conv(n, d, me, got, spec, fwd, back)
    grad_filter = sum_grads(d, keep, send)
    mixed = exchange(mixed, "ctx")
    early = 3 * n // 4
    outs = gate(range(early), me, query, grad, value, key, gain, mixed, [])
    outs = gate(range(early, n), me, query, grad, value, key, gain, mixed, outs)
    return *(x[None] for x in outs), grad_filter


def solution(mesh):
    rows = P("dp", "ctx", None)
    return jax.shard_map(
        functools.partial(local, mesh.shape["ctx"], mesh.shape["dp"]),
        mesh=mesh,
        in_specs=(rows, rows, rows, rows, P("ctx", None), P()),
        out_specs=(rows, rows, rows, rows, P("ctx", "dp")),
        check_vma=False,
    )
```

```python
import functools
import math

import jax
import jax.numpy as jnp
import ml_dtypes
import numpy as np
from jax import lax
from jax.experimental import pallas as pl
from jax.experimental.pallas import tpu as pltpu
from jax.sharding import PartitionSpec as P

F32 = jnp.float32
BF16 = jnp.bfloat16
CLASSES = 8
HALVES = 2
STEPS = 4
PARAMS = pltpu.CompilerParams(vmem_limit_bytes=16 * 1024 * 1024)
CONV_PARAMS = pltpu.CompilerParams(vmem_limit_bytes=34 * 1024 * 1024)
SMEM = pl.BlockSpec(memory_space=pltpu.SMEM)
VMEM = pl.BlockSpec(memory_space=pltpu.VMEM)
HBM = pl.BlockSpec(memory_space=pltpu.HBM)


def tables(length):
    m2 = length // CLASSES
    c = np.arange(CLASSES)[:, None, None]
    j = np.arange(m2)[None, :, None]
    m = np.arange(m2)[None, None, :]
    turn = ((CLASSES * m + c) * (2 * j + 1)) % (4 * length)
    angle = 2 * np.pi * turn / (4 * length)
    forward = np.concatenate([np.cos(angle), -np.sin(angle)], 1)
    back = np.swapaxes(forward, 1, 2) / length

    def parts(x):
        hi = x.astype(ml_dtypes.bfloat16)
        return hi, (x - hi.astype(np.float64)).astype(ml_dtypes.bfloat16)

    return np.concatenate(parts(forward), 2), back.astype(ml_dtypes.bfloat16)


def parts(x):
    hi = x.astype(BF16)
    return hi, (x - hi.astype(F32)).astype(BF16)


def dot(a, b):
    return jnp.dot(a, b, preferred_element_type=F32)


def dft(z, sign):
    n = len(z)
    if n == 1:
        return z
    even, odd = dft(z[0::2], sign), dft(z[1::2], sign)
    low, high = [], []
    for k in range(n // 2):
        (er, ei), (zr, zi) = even[k], odd[k]
        if k == 0:
            tr, ti = zr, zi
        elif 4 * k == n:
            tr, ti = (-zi, zr) if sign > 0 else (zi, -zr)
        else:
            c, s = math.cos(2 * math.pi * k / n), sign * math.sin(2 * math.pi * k / n)
            if 8 * k == n:
                tr, ti = (c * (zr - zi), c * (zi + zr)) if sign > 0 else (c * (zr + zi), c * (zi - zr))
            elif 8 * k == 3 * n:
                tr, ti = (c * (zr + zi), c * (zi - zr)) if sign > 0 else (c * (zr - zi), c * (zi + zr))
            else:
                tr, ti = c * zr - s * zi, c * zi + s * zr
        low.append((er + tr, ei + ti))
        high.append((er - tr, ei - ti))
    return low + high


def times(x, f, conj):
    (xr, xi), (fr, fi) = x, f
    if conj:
        return xr * fr + xi * fi, xi * fr - xr * fi
    return xr * fr - xi * fi, xr * fi + xi * fr


def resident(x):
    return pltpu.with_memory_space_constraint(x, pltpu.VMEM)


def in_hbm(x):
    return pltpu.with_memory_space_constraint(x, pltpu.HBM)


def peer_columns(me, j, width):
    return pl.ds(pl.multiple_of((me[0] ^ j) * width, 128), width)


def product_kernel(n, me, key, value, query, grad, *refs):
    bufs, outs, sems = refs[:4], refs[4:-1], refs[-1]
    _, rows, width = outs[0].shape
    width *= HALVES
    step = rows // STEPS
    copies = []
    for i in range(STEPS):
        at = pl.ds(i * step, step)
        copies.append(
            [
                pltpu.make_async_copy(src.at[at], dst.at[at], sems.at[a, i])
                for a, (src, dst) in enumerate(zip((key, value, query, grad), bufs))
            ]
        )
        for copy in copies[i]:
            copy.start()
    for s in range(STEPS):
        at = pl.ds(s * step, step)
        for a, (left, right) in enumerate((bufs[:2], bufs[2:])):
            copies[s][2 * a].wait()
            copies[s][2 * a + 1].wait()
            for i, j in enumerate(peers(n)):
                cols = peer_columns(me, j, width)
                value = (left[at, cols].astype(F32) * right[at, cols].astype(F32)).astype(BF16)
                for half in range(HALVES):
                    outs[half * n + i][a, at] = value[:, half * width // HALVES :][:, : width // HALVES]


def products(n, me, key, value, query, grad):
    rows, total = key.shape
    width = total // n // HALVES
    out = pl.pallas_call(
        functools.partial(product_kernel, n),
        in_specs=[SMEM] + [HBM] * 4,
        out_specs=[VMEM] * (4 + HALVES * n),
        out_shape=[pltpu.VMEM(key.shape, BF16)] * 4
        + [pltpu.VMEM((2, rows, width), BF16)] * (HALVES * n),
        scratch_shapes=[pltpu.SemaphoreType.DMA((4, STEPS))],
        compiler_params=PARAMS,
        name="products",
    )(me, key, value, query, grad)
    return out[:4], [out[4 + h * n : 4 + (h + 1) * n] for h in range(HALVES)]


def lane_groups(width):
    return [slice(i, i + 128) for i in range(0, width, 128)]


def filter_kernel(filt, fwd, *refs):
    spec, x, u = refs[-3:]
    m2, width = x.shape[1] // CLASSES, u.shape[-1]
    groups = lane_groups(width)
    rows = m2 // CLASSES
    for half in range(HALVES):
        for g, lanes in enumerate(groups):
            x[g] = filt[half * width + lanes.start : half * width + lanes.stop, :].T
        for c in range(CLASSES):
            for g, lanes in enumerate(groups):
                hi, lo = parts(x[g, pl.ds(c, m2, stride=CLASSES), :])
                u[c, :, lanes] = dot(fwd[c], jnp.concatenate([hi, hi], 0)) + dot(fwd[c, :, :m2], lo)

        def step(i, carry):
            r = pl.multiple_of(i * rows, rows)
            re, im = pl.ds(r, rows), pl.ds(m2 + r, rows)
            for lanes in groups:
                z = dft([(u[c, re, lanes], u[c, im, lanes]) for c in range(CLASSES)], -1)
                for k in range(CLASSES):
                    spec[half, k, re, lanes], spec[half, k, im, lanes] = z[k]
            return carry

        lax.fori_loop(0, CLASSES, step, 0)


def filter_spectra(filters, fwd, after, then):
    chans, length = filters.shape
    width = chans // HALVES
    m2 = length // CLASSES
    out = pl.pallas_call(
        filter_kernel,
        in_specs=[VMEM] * (2 + len(after) + len(then)),
        out_specs=[VMEM] * (len(then) + 1),
        out_shape=[pltpu.VMEM(t.shape, t.dtype) for t in then]
        + [pltpu.VMEM((HALVES, CLASSES, 2 * m2, width), F32)],
        scratch_shapes=[
            pltpu.VMEM((width // 128, length, 128), F32),
            pltpu.VMEM((CLASSES, 2 * m2, width), F32),
        ],
        input_output_aliases={2 + len(after) + i: i for i in range(len(then))},
        compiler_params=PARAMS,
        name="filter_spectra",
    )(filters, fwd, *after, *then)
    return out[-1], out[:-1]


def conv_kernel(n, d, half, me, *refs):
    got, (filt, fwd, back) = refs[:n], refs[n : n + 3]
    refs = refs[-(n + 2 + 6) :]
    out, (keep, send), (nat, x, u, y, turned, grad) = refs[:n], refs[n : n + 2], refs[n + 2 :]
    _, rows, width = got[0].shape
    m2 = x.shape[2]
    per = keep.shape[1] // CLASSES
    groups = lane_groups(width)
    step_rows = m2 // CLASSES
    part_rows = rows // CLASSES
    chans = slice(half * width, (half + 1) * width)

    for a in range(2):
        for g, lanes in enumerate(groups):
            for i, j in enumerate(peers(n)):
                at = pl.multiple_of((me[0] ^ j) * rows, rows)
                nat[a, g, pl.ds(at, rows)] = got[i][a, :, lanes].astype(F32)
            for c in range(CLASSES):
                x[a, c, :, lanes] = nat[a, g, pl.ds(c, m2, stride=CLASSES), :].astype(BF16)
        for c in range(CLASSES):
            data = x[a, c]
            u[a, c] = dot(fwd[c], jnp.concatenate([data, data], 0))

    def middle(i, carry):
        r = pl.multiple_of(i * step_rows, step_rows)
        re, im = pl.ds(r, step_rows), pl.ds(m2 + r, step_rows)
        for lanes in groups:
            kv = dft([(u[0, c, re, lanes], u[0, c, im, lanes]) for c in range(CLASSES)], -1)
            wt = dft([(u[1, c, re, lanes], u[1, c, im, lanes]) for c in range(CLASSES)], -1)
            fs = [(filt[half, k, re, lanes], filt[half, k, im, lanes]) for k in range(CLASSES)]
            for o, (left, right, conj) in enumerate([(kv, fs, False), (wt, fs, True), (wt, kv, True)]):
                z = dft([times(s, t, conj) for s, t in zip(left, right)], 1)
                for c in range(CLASSES):
                    y[o, c, re, lanes] = z[c][0].astype(BF16)
                    y[o, c, im, lanes] = z[c][1].astype(BF16)
        return carry

    lax.fori_loop(0, CLASSES, middle, 0)

    for c in range(CLASSES):
        grad[c] = dot(back[c], y[2, c])
        for o in range(2):
            turned[o, c] = dot(back[c], y[o, c]).astype(BF16)
    for i, j in enumerate(peers(n)):
        at = pl.multiple_of((me[0] ^ j) * part_rows, part_rows)
        for o in range(2):
            for c in range(CLASSES):
                out[i][half, o, c * part_rows : (c + 1) * part_rows] = turned[o, c, pl.ds(at, part_rows)]
    for j in range(d):
        at = pl.multiple_of((me[1] ^ j) * per, per)
        for c in range(CLASSES):
            part = grad[c, pl.ds(at, per)]
            if j % 2:
                send[j // 2, c * per : (c + 1) * per, chans] = part.astype(BF16)
            else:
                keep[j // 2, c * per : (c + 1) * per, chans] = part


def conv(n, d, half, me, got, filt, fwd, back, before):
    _, rows, width = got[0].shape
    length = n * rows
    m2 = length // CLASSES
    out = pl.pallas_call(
        functools.partial(conv_kernel, n, d, half),
        in_specs=[SMEM] + [VMEM] * (n + 3 + len(before)),
        out_specs=[VMEM] * (n + 2),
        out_shape=[pltpu.VMEM((HALVES, 2, rows, width), BF16)] * n
        + [pltpu.VMEM((d // 2, length // d, HALVES * width), dtype) for dtype in (F32, BF16)],
        scratch_shapes=[
            pltpu.VMEM((2, width // 128, length, 128), F32),
            pltpu.VMEM((2, CLASSES, m2, width), BF16),
            pltpu.VMEM((2, CLASSES, 2 * m2, width), F32),
            pltpu.VMEM((3, CLASSES, 2 * m2, width), BF16),
            pltpu.VMEM((2, CLASSES, m2, width), BF16),
            pltpu.VMEM((CLASSES, m2, width), F32),
        ],
        input_output_aliases={n + 4 + i: i for i in range(len(before))},
        compiler_params=CONV_PARAMS,
        name="conv",
    )(me, *got, filt, fwd, back, *before)
    return out


def natural(scratch, piece):
    rows = piece.shape[0] // CLASSES
    for c in range(CLASSES):
        scratch[pl.ds(c, rows, stride=CLASSES), :] = piece[c * rows : (c + 1) * rows]
    return scratch[...]


def gate_kernel(js, me, query, grad, value, key, gain, *refs):
    got, outs, (sent, sems, nat) = refs[: len(js)], refs[-7:-3], refs[-3:]
    _, _, rows, width = got[0].shape
    copies = []
    for i, j in enumerate(js):
        block = peer_columns(me, j, HALVES * width)
        for half in range(HALVES):
            for g, lanes in enumerate(lane_groups(width)):
                at = half * width + lanes.start
                start = pl.multiple_of((me[0] ^ j) * HALVES * width + at, 128)
                cols = pl.ds(start, 128)
                to = slice(at, at + 128)
                scale = gain[:, cols]
                q, g_, v, k = (x[:, cols].astype(F32) for x in (query, grad, value, key))
                conv_out, corr_back = (
                    natural(nat.at[i, o, half, g], got[i][half, o, :, lanes].astype(F32)) for o in range(2)
                )
                mixing = conv_out + scale * (k * v).astype(BF16).astype(F32)
                sent[0, i, :, to] = (q * mixing).astype(BF16)
                sent[1, i, :, to] = (g_ * mixing).astype(BF16)
                total = corr_back + scale * (g_ * q).astype(BF16).astype(F32)
                sent[2, i, :, to] = (total * v).astype(BF16)
                sent[3, i, :, to] = (total * k).astype(BF16)
        for a in range(4):
            copy = pltpu.make_async_copy(sent.at[a, i], outs[a].at[:, block], sems.at[a, i])
            copy.start()
            copies.append(copy)
    for copy in copies:
        copy.wait()


def gate(js, me, query, grad, value, key, gain, got, outs):
    _, _, rows, width = got[0].shape
    return pl.pallas_call(
        functools.partial(gate_kernel, js),
        in_specs=[SMEM] + [VMEM] * (5 + len(js)) + [HBM] * len(outs),
        out_specs=[HBM] * 4,
        out_shape=[jax.ShapeDtypeStruct(query.shape, BF16)] * 4,
        scratch_shapes=[
            pltpu.VMEM((4, len(js), rows, HALVES * width), BF16),
            pltpu.SemaphoreType.DMA((4, len(js))),
            pltpu.VMEM((len(js), 2, HALVES, width // 128, rows, 128), F32),
        ],
        input_output_aliases={6 + len(js) + i: i for i in range(len(outs))},
        compiler_params=PARAMS,
        name="gate",
    )(me, query, grad, value, key, gain, *got, *outs)


def add_kernel(keep, got, new_keep, new_send):
    for i in range(new_keep.shape[0]):
        new_keep[i] = keep[2 * i] + got[2 * i].astype(F32)
        new_send[i] = (keep[2 * i + 1] + got[2 * i + 1].astype(F32)).astype(BF16)


def turn_kernel(keep, got, out, nat):
    for g, lanes in enumerate(lane_groups(keep.shape[2])):
        total = keep[0, :, lanes] + got[0, :, lanes].astype(F32)
        out[lanes, :] = natural(nat.at[g], total).T


def sum_grads(d, keep, send):
    _, per, chans = keep.shape
    bit = 1
    while True:
        got = resident(lax.ppermute(send, "dp", [(i, i ^ bit) for i in range(d)]))
        if keep.shape[0] == 1:
            break
        shape = (keep.shape[0] // 2, per, chans)
        keep, send = pl.pallas_call(
            add_kernel,
            in_specs=[VMEM] * 2,
            out_specs=[VMEM] * 2,
            out_shape=[pltpu.VMEM(shape, F32), pltpu.VMEM(shape, BF16)],
            compiler_params=PARAMS,
            name="add_grads",
        )(keep, got)
        bit *= 2
    return pl.pallas_call(
        turn_kernel,
        in_specs=[VMEM] * 2,
        out_specs=VMEM,
        out_shape=jax.ShapeDtypeStruct((chans, per), F32),
        scratch_shapes=[pltpu.VMEM((chans // 128, per, 128), F32)],
        compiler_params=PARAMS,
        name="turn_grads",
    )(keep, got)


def peers(n):
    return [0, *range(2, n, 2), *range(1, n, 2)]


def exchange(blocks, axis):
    n = len(blocks)
    got = [blocks[0]]
    for j, block in zip(peers(n)[1:], blocks[1:]):
        got.append(resident(lax.ppermute(block, axis, [(i, i ^ j) for i in range(n)])))
    return got


def local(n, d, query_in, key_in, value_in, grad_out, filters, skip_gain):
    fwd, back = (resident(jnp.asarray(t)) for t in tables(filters.shape[1]))
    filters = resident(filters)
    gain = skip_gain[None, :]
    me = jnp.stack([lax.axis_index("ctx"), lax.axis_index("dp")]).astype(jnp.int32)

    arrays = [in_hbm(x[0]) for x in (key_in, value_in, query_in, grad_out)]
    (key, value, query, grad), got = products(n, me, *arrays)
    first = exchange(got[0], "ctx")
    spec, second = filter_spectra(filters, fwd, [first[1]], got[1])
    second = exchange(second, "ctx")
    results = conv(n, d, 0, me, first, spec, fwd, back, [])
    *mixed, keep, send = conv(n, d, 1, me, second, spec, fwd, back, results)
    mixed = exchange(mixed, "ctx")
    grad_filter = sum_grads(d, keep, send)
    outs = []
    early = 3 * n // 4
    for at in (slice(early), slice(early, n)):
        outs = gate(peers(n)[at], me, query, grad, value, key, gain, mixed[at], outs)
    return *(x[None] for x in outs), grad_filter


def solution(mesh):
    rows = P("dp", "ctx", None)
    return jax.shard_map(
        functools.partial(local, mesh.shape["ctx"], mesh.shape["dp"]),
        mesh=mesh,
        in_specs=(rows, rows, rows, rows, P("ctx", None), P()),
        out_specs=(rows, rows, rows, rows, P("ctx", "dp")),
        check_vma=False,
    )
```

```python
import functools
import math

import jax
import jax.numpy as jnp
import ml_dtypes
import numpy as np
from jax import lax
from jax.experimental import pallas as pl
from jax.experimental.pallas import tpu as pltpu
from jax.sharding import PartitionSpec as P

F32 = jnp.float32
BF16 = jnp.bfloat16
CLASSES = 8
HALVES = 2
STEPS = 4
PARAMS = pltpu.CompilerParams(vmem_limit_bytes=16 * 1024 * 1024)
CONV_PARAMS = pltpu.CompilerParams(vmem_limit_bytes=34 * 1024 * 1024)
SMEM = pl.BlockSpec(memory_space=pltpu.SMEM)
VMEM = pl.BlockSpec(memory_space=pltpu.VMEM)
HBM = pl.BlockSpec(memory_space=pltpu.HBM)


def tables(length):
    m2 = length // CLASSES
    c = np.arange(CLASSES)[:, None, None]
    j = np.arange(m2)[None, :, None]
    m = np.arange(m2)[None, None, :]
    turn = ((CLASSES * m + c) * (2 * j + 1)) % (4 * length)
    angle = 2 * np.pi * turn / (4 * length)
    forward = np.concatenate([np.cos(angle), -np.sin(angle)], 1)
    back = np.swapaxes(forward, 1, 2) / length

    def parts(x):
        hi = x.astype(ml_dtypes.bfloat16)
        return hi, (x - hi.astype(np.float64)).astype(ml_dtypes.bfloat16)

    return np.concatenate(parts(forward), 2), back.astype(ml_dtypes.bfloat16)


def parts(x):
    hi = x.astype(BF16)
    return hi, (x - hi.astype(F32)).astype(BF16)


def dot(a, b):
    return jnp.dot(a, b, preferred_element_type=F32)


def dft(z, sign):
    n = len(z)
    if n == 1:
        return z
    even, odd = dft(z[0::2], sign), dft(z[1::2], sign)
    low, high = [], []
    for k in range(n // 2):
        (er, ei), (zr, zi) = even[k], odd[k]
        if k == 0:
            tr, ti = zr, zi
        elif 4 * k == n:
            tr, ti = (-zi, zr) if sign > 0 else (zi, -zr)
        else:
            c, s = math.cos(2 * math.pi * k / n), sign * math.sin(2 * math.pi * k / n)
            if 8 * k == n:
                tr, ti = (c * (zr - zi), c * (zi + zr)) if sign > 0 else (c * (zr + zi), c * (zi - zr))
            elif 8 * k == 3 * n:
                tr, ti = (c * (zr + zi), c * (zi - zr)) if sign > 0 else (c * (zr - zi), c * (zi + zr))
            else:
                tr, ti = c * zr - s * zi, c * zi + s * zr
        low.append((er + tr, ei + ti))
        high.append((er - tr, ei - ti))
    return low + high


def times(x, f, conj):
    (xr, xi), (fr, fi) = x, f
    if conj:
        return xr * fr + xi * fi, xi * fr - xr * fi
    return xr * fr - xi * fi, xr * fi + xi * fr


def resident(x):
    return pltpu.with_memory_space_constraint(x, pltpu.VMEM)


def in_hbm(x):
    return pltpu.with_memory_space_constraint(x, pltpu.HBM)


def peer_columns(me, j, width):
    return pl.ds(pl.multiple_of((me[0] ^ j) * width, 128), width)


def product_kernel(n, me, key, value, query, grad, *refs):
    bufs, outs, sems = refs[:4], refs[4:-1], refs[-1]
    _, rows, width = outs[0].shape
    width *= HALVES
    step = rows // STEPS
    copies = []
    for i in range(STEPS):
        at = pl.ds(i * step, step)
        copies.append(
            [
                pltpu.make_async_copy(src.at[at], dst.at[at], sems.at[a, i])
                for a, (src, dst) in enumerate(zip((key, value, query, grad), bufs))
            ]
        )
        for copy in copies[i]:
            copy.start()
    for s in range(STEPS):
        at = pl.ds(s * step, step)
        for a, (left, right) in enumerate((bufs[:2], bufs[2:])):
            copies[s][2 * a].wait()
            copies[s][2 * a + 1].wait()
            for i, j in enumerate(peers(n)):
                cols = peer_columns(me, j, width)
                value = (left[at, cols].astype(F32) * right[at, cols].astype(F32)).astype(BF16)
                for half in range(HALVES):
                    outs[half * n + i][a, at] = value[:, half * width // HALVES :][:, : width // HALVES]


def products(n, me, key, value, query, grad):
    rows, total = key.shape
    width = total // n // HALVES
    out = pl.pallas_call(
        functools.partial(product_kernel, n),
        in_specs=[SMEM] + [HBM] * 4,
        out_specs=[VMEM] * (4 + HALVES * n),
        out_shape=[pltpu.VMEM(key.shape, BF16)] * 4
        + [pltpu.VMEM((2, rows, width), BF16)] * (HALVES * n),
        scratch_shapes=[pltpu.SemaphoreType.DMA((4, STEPS))],
        compiler_params=PARAMS,
        name="products",
    )(me, key, value, query, grad)
    return out[:4], [out[4 + h * n : 4 + (h + 1) * n] for h in range(HALVES)]


def lane_groups(width):
    return [slice(i, i + 128) for i in range(0, width, 128)]


def filter_kernel(filt, fwd, *refs):
    spec, x, u = refs[-3:]
    m2, width = x.shape[1] // CLASSES, u.shape[-1]
    groups = lane_groups(width)
    rows = m2 // CLASSES
    for half in range(HALVES):
        for g, lanes in enumerate(groups):
            x[g] = filt[half * width + lanes.start : half * width + lanes.stop, :].T
        for c in range(CLASSES):
            for g, lanes in enumerate(groups):
                hi, lo = parts(x[g, pl.ds(c, m2, stride=CLASSES), :])
                u[c, :, lanes] = dot(fwd[c], jnp.concatenate([hi, hi], 0)) + dot(fwd[c, :, :m2], lo)

        def step(i, carry):
            r = pl.multiple_of(i * rows, rows)
            re, im = pl.ds(r, rows), pl.ds(m2 + r, rows)
            for lanes in groups:
                z = dft([(u[c, re, lanes], u[c, im, lanes]) for c in range(CLASSES)], -1)
                for k in range(CLASSES):
                    spec[half, k, re, lanes], spec[half, k, im, lanes] = z[k]
            return carry

        lax.fori_loop(0, CLASSES, step, 0)


def filter_spectra(filters, fwd, arrived):
    chans, length = filters.shape
    width = chans // HALVES
    m2 = length // CLASSES
    return pl.pallas_call(
        filter_kernel,
        in_specs=[VMEM] * (2 + len(arrived)),
        out_specs=VMEM,
        out_shape=pltpu.VMEM((HALVES, CLASSES, 2 * m2, width), F32),
        scratch_shapes=[
            pltpu.VMEM((width // 128, length, 128), F32),
            pltpu.VMEM((CLASSES, 2 * m2, width), F32),
        ],
        compiler_params=PARAMS,
        name="filter_spectra",
    )(filters, fwd, *arrived)


def conv_kernel(n, d, half, me, *refs):
    got, (filt, fwd, back) = refs[:n], refs[n : n + 3]
    refs = refs[-(n + 2 + 6) :]
    out, (keep, send), (nat, x, u, y, turned, grad) = refs[:n], refs[n : n + 2], refs[n + 2 :]
    _, rows, width = got[0].shape
    m2 = x.shape[2]
    per = keep.shape[1] // CLASSES
    groups = lane_groups(width)
    step_rows = m2 // CLASSES
    part_rows = rows // CLASSES
    chans = slice(half * width, (half + 1) * width)

    for a in range(2):
        for g, lanes in enumerate(groups):
            for i, j in enumerate(peers(n)):
                at = pl.multiple_of((me[0] ^ j) * rows, rows)
                nat[a, g, pl.ds(at, rows)] = got[i][a, :, lanes].astype(F32)
            for c in range(CLASSES):
                x[a, c, :, lanes] = nat[a, g, pl.ds(c, m2, stride=CLASSES), :].astype(BF16)
        for c in range(CLASSES):
            data = x[a, c]
            u[a, c] = dot(fwd[c], jnp.concatenate([data, data], 0))

    def middle(i, carry):
        r = pl.multiple_of(i * step_rows, step_rows)
        re, im = pl.ds(r, step_rows), pl.ds(m2 + r, step_rows)
        for lanes in groups:
            kv = dft([(u[0, c, re, lanes], u[0, c, im, lanes]) for c in range(CLASSES)], -1)
            wt = dft([(u[1, c, re, lanes], u[1, c, im, lanes]) for c in range(CLASSES)], -1)
            fs = [(filt[half, k, re, lanes], filt[half, k, im, lanes]) for k in range(CLASSES)]
            for o, (left, right, conj) in enumerate([(kv, fs, False), (wt, fs, True), (wt, kv, True)]):
                z = dft([times(s, t, conj) for s, t in zip(left, right)], 1)
                for c in range(CLASSES):
                    y[o, c, re, lanes] = z[c][0].astype(BF16)
                    y[o, c, im, lanes] = z[c][1].astype(BF16)
        return carry

    lax.fori_loop(0, CLASSES, middle, 0)

    for c in range(CLASSES):
        grad[c] = dot(back[c], y[2, c])
        for o in range(2):
            turned[o, c] = dot(back[c], y[o, c]).astype(BF16)
    for i, j in enumerate(peers(n)):
        at = pl.multiple_of((me[0] ^ j) * part_rows, part_rows)
        for o in range(2):
            for c in range(CLASSES):
                out[i][half, o, c * part_rows : (c + 1) * part_rows] = turned[o, c, pl.ds(at, part_rows)]
    for j in range(d):
        at = pl.multiple_of((me[1] ^ j) * per, per)
        for c in range(CLASSES):
            part = grad[c, pl.ds(at, per)]
            if j % 2:
                send[j // 2, c * per : (c + 1) * per, chans] = part.astype(BF16)
            else:
                keep[j // 2, c * per : (c + 1) * per, chans] = part


def conv(n, d, half, me, got, filt, fwd, back, before):
    _, rows, width = got[0].shape
    length = n * rows
    m2 = length // CLASSES
    out = pl.pallas_call(
        functools.partial(conv_kernel, n, d, half),
        in_specs=[SMEM] + [VMEM] * (n + 3 + len(before)),
        out_specs=[VMEM] * (n + 2),
        out_shape=[pltpu.VMEM((HALVES, 2, rows, width), BF16)] * n
        + [pltpu.VMEM((d // 2, length // d, HALVES * width), dtype) for dtype in (F32, BF16)],
        scratch_shapes=[
            pltpu.VMEM((2, width // 128, length, 128), F32),
            pltpu.VMEM((2, CLASSES, m2, width), BF16),
            pltpu.VMEM((2, CLASSES, 2 * m2, width), F32),
            pltpu.VMEM((3, CLASSES, 2 * m2, width), BF16),
            pltpu.VMEM((2, CLASSES, m2, width), BF16),
            pltpu.VMEM((CLASSES, m2, width), F32),
        ],
        input_output_aliases={n + 4 + i: i for i in range(len(before))},
        compiler_params=CONV_PARAMS,
        name="conv",
    )(me, *got, filt, fwd, back, *before)
    return out


def natural(scratch, piece):
    rows = piece.shape[0] // CLASSES
    for c in range(CLASSES):
        scratch[pl.ds(c, rows, stride=CLASSES), :] = piece[c * rows : (c + 1) * rows]
    return scratch[...]


def gate_kernel(js, me, query, grad, value, key, gain, *refs):
    got, outs, (sent, sems, nat) = refs[: len(js)], refs[-7:-3], refs[-3:]
    _, _, rows, width = got[0].shape
    copies = []
    for i, j in enumerate(js):
        block = peer_columns(me, j, HALVES * width)
        for half in range(HALVES):
            for g, lanes in enumerate(lane_groups(width)):
                at = half * width + lanes.start
                start = pl.multiple_of((me[0] ^ j) * HALVES * width + at, 128)
                cols = pl.ds(start, 128)
                to = slice(at, at + 128)
                scale = gain[:, cols]
                q, g_, v, k = (x[:, cols].astype(F32) for x in (query, grad, value, key))
                conv_out, corr_back = (
                    natural(nat.at[i, o, half, g], got[i][half, o, :, lanes].astype(F32)) for o in range(2)
                )
                mixing = conv_out + scale * (k * v).astype(BF16).astype(F32)
                sent[0, i, :, to] = (q * mixing).astype(BF16)
                sent[1, i, :, to] = (g_ * mixing).astype(BF16)
                total = corr_back + scale * (g_ * q).astype(BF16).astype(F32)
                sent[2, i, :, to] = (total * v).astype(BF16)
                sent[3, i, :, to] = (total * k).astype(BF16)
        for a in range(4):
            copy = pltpu.make_async_copy(sent.at[a, i], outs[a].at[:, block], sems.at[a, i])
            copy.start()
            copies.append(copy)
    for copy in copies:
        copy.wait()


def gate(js, me, query, grad, value, key, gain, got, outs):
    _, _, rows, width = got[0].shape
    return pl.pallas_call(
        functools.partial(gate_kernel, js),
        in_specs=[SMEM] + [VMEM] * (5 + len(got)) + [HBM] * len(outs),
        out_specs=[HBM] * 4,
        out_shape=[jax.ShapeDtypeStruct(query.shape, BF16)] * 4,
        scratch_shapes=[
            pltpu.VMEM((4, len(js), rows, HALVES * width), BF16),
            pltpu.SemaphoreType.DMA((4, len(js))),
            pltpu.VMEM((len(js), 2, HALVES, width // 128, rows, 128), F32),
        ],
        input_output_aliases={6 + len(got) + i: i for i in range(len(outs))},
        compiler_params=PARAMS,
        name="gate",
    )(me, query, grad, value, key, gain, *got, *outs)


def add_kernel(keep, got, new_keep, new_send):
    for i in range(new_keep.shape[0]):
        new_keep[i] = keep[2 * i] + got[2 * i].astype(F32)
        new_send[i] = (keep[2 * i + 1] + got[2 * i + 1].astype(F32)).astype(BF16)


def turn_kernel(keep, got, out, nat):
    for g, lanes in enumerate(lane_groups(keep.shape[2])):
        total = keep[0, :, lanes] + got[0, :, lanes].astype(F32)
        out[lanes, :] = natural(nat.at[g], total).T


def sum_grads(d, keep, send):
    _, per, chans = keep.shape
    bit = 1
    while True:
        got = resident(lax.ppermute(send, "dp", [(i, i ^ bit) for i in range(d)]))
        if keep.shape[0] == 1:
            break
        shape = (keep.shape[0] // 2, per, chans)
        keep, send = pl.pallas_call(
            add_kernel,
            in_specs=[VMEM] * 2,
            out_specs=[VMEM] * 2,
            out_shape=[pltpu.VMEM(shape, F32), pltpu.VMEM(shape, BF16)],
            compiler_params=PARAMS,
            name="add_grads",
        )(keep, got)
        bit *= 2
    return pl.pallas_call(
        turn_kernel,
        in_specs=[VMEM] * 2,
        out_specs=VMEM,
        out_shape=jax.ShapeDtypeStruct((chans, per), F32),
        scratch_shapes=[pltpu.VMEM((chans // 128, per, 128), F32)],
        compiler_params=PARAMS,
        name="turn_grads",
    )(keep, got)


def peers(n):
    return [0, 1, *range(2, n, 2), *range(3, n, 2)]


def exchange(n, js, blocks):
    return [
        resident(lax.ppermute(block, "ctx", [(i, i ^ j) for i in range(n)])) if j else block
        for j, block in zip(js, blocks)
    ]


def after_kernel(*refs):
    pass


def after(arrived, blocks):
    count = len(arrived)
    return pl.pallas_call(
        after_kernel,
        in_specs=[VMEM] * (count + len(blocks)),
        out_specs=[VMEM] * len(blocks),
        out_shape=[pltpu.VMEM(b.shape, b.dtype) for b in blocks],
        input_output_aliases={count + i: i for i in range(len(blocks))},
        compiler_params=PARAMS,
        name="after",
    )(*arrived, *blocks)


def local(n, d, query_in, key_in, value_in, grad_out, filters, skip_gain):
    fwd, back = (resident(jnp.asarray(t)) for t in tables(filters.shape[1]))
    filters = resident(filters)
    gain = skip_gain[None, :]
    me = jnp.stack([lax.axis_index("ctx"), lax.axis_index("dp")]).astype(jnp.int32)

    arrays = [in_hbm(x[0]) for x in (key_in, value_in, query_in, grad_out)]
    (key, value, query, grad), got = products(n, me, *arrays)
    first = exchange(n, peers(n), got[0])
    second = exchange(n, peers(n), after([first[1]], got[1]))
    spec = filter_spectra(filters, fwd, [second[1]])
    results = conv(n, d, 0, me, first, spec, fwd, back, [])
    *mixed, keep, send = conv(n, d, 1, me, second, spec, fwd, back, results)
    mixed = exchange(n, peers(n), mixed)
    grad_filter = sum_grads(d, keep, *after([mixed[1]], [send]))

    outs = []
    early = n - 2
    for at in (slice(early), slice(early, n)):
        outs = gate(peers(n)[at], me, query, grad, value, key, gain, mixed[at], outs)
    return *(x[None] for x in outs), grad_filter


def solution(mesh):
    rows = P("dp", "ctx", None)
    return jax.shard_map(
        functools.partial(local, mesh.shape["ctx"], mesh.shape["dp"]),
        mesh=mesh,
        in_specs=(rows, rows, rows, rows, P("ctx", None), P()),
        out_specs=(rows, rows, rows, rows, P("ctx", "dp")),
        check_vma=False,
    )
```

```python
import functools
import math

import jax
import jax.numpy as jnp
import ml_dtypes
import numpy as np
from jax import lax
from jax.experimental import pallas as pl
from jax.experimental.pallas import tpu as pltpu
from jax.sharding import PartitionSpec as P

F32 = jnp.float32
BF16 = jnp.bfloat16
CLASSES = 8
HALVES = 2
STEPS = 4
PARAMS = pltpu.CompilerParams(vmem_limit_bytes=16 * 1024 * 1024)
CONV_PARAMS = pltpu.CompilerParams(vmem_limit_bytes=34 * 1024 * 1024)
SMEM = pl.BlockSpec(memory_space=pltpu.SMEM)
VMEM = pl.BlockSpec(memory_space=pltpu.VMEM)
SMALL_COST = pl.CostEstimate(flops=0, bytes_accessed=1024, transcendentals=0)
HBM = pl.BlockSpec(memory_space=pltpu.HBM)


def tables(length):
    m2 = length // CLASSES
    c = np.arange(CLASSES)[:, None, None]
    j = np.arange(m2)[None, :, None]
    m = np.arange(m2)[None, None, :]
    turn = ((CLASSES * m + c) * (2 * j + 1)) % (4 * length)
    angle = 2 * np.pi * turn / (4 * length)
    forward = np.concatenate([np.cos(angle), -np.sin(angle)], 1)
    back = np.swapaxes(forward, 1, 2) / length

    def parts(x):
        hi = x.astype(ml_dtypes.bfloat16)
        return hi, (x - hi.astype(np.float64)).astype(ml_dtypes.bfloat16)

    return np.concatenate(parts(forward), 2), back.astype(ml_dtypes.bfloat16)


def parts(x):
    hi = x.astype(BF16)
    return hi, (x - hi.astype(F32)).astype(BF16)


def dot(a, b):
    return jnp.dot(a, b, preferred_element_type=F32)


def dft(z, sign):
    n = len(z)
    if n == 1:
        return z
    even, odd = dft(z[0::2], sign), dft(z[1::2], sign)
    low, high = [], []
    for k in range(n // 2):
        (er, ei), (zr, zi) = even[k], odd[k]
        if k == 0:
            tr, ti = zr, zi
        elif 4 * k == n:
            tr, ti = (-zi, zr) if sign > 0 else (zi, -zr)
        else:
            c, s = math.cos(2 * math.pi * k / n), sign * math.sin(2 * math.pi * k / n)
            if 8 * k == n:
                tr, ti = (c * (zr - zi), c * (zi + zr)) if sign > 0 else (c * (zr + zi), c * (zi - zr))
            elif 8 * k == 3 * n:
                tr, ti = (c * (zr + zi), c * (zi - zr)) if sign > 0 else (c * (zr - zi), c * (zi + zr))
            else:
                tr, ti = c * zr - s * zi, c * zi + s * zr
        low.append((er + tr, ei + ti))
        high.append((er - tr, ei - ti))
    return low + high


def times(x, f, conj):
    (xr, xi), (fr, fi) = x, f
    if conj:
        return xr * fr + xi * fi, xi * fr - xr * fi
    return xr * fr - xi * fi, xr * fi + xi * fr


def resident(x):
    return pltpu.with_memory_space_constraint(x, pltpu.VMEM)


def in_hbm(x):
    return pltpu.with_memory_space_constraint(x, pltpu.HBM)


def chips(n):
    return range(0, n, 2)


def sources(n, got, passed):
    straight = [(chip, got[i].at[0]) for i, chip in enumerate(chips(n))]
    return straight + [(chip + 1, passed.at[i]) for i, chip in enumerate(chips(n))]


def peer_columns(me, j, half, width, lane=0, lanes=None):
    start = (HALVES * (me[0] ^ j) + half) * width + lane
    return pl.ds(pl.multiple_of(start, 128), lanes or width)


def product_kernel(n, me, key, value, query, grad, *refs):
    bufs, outs, sems = refs[:4], refs[4:-1], refs[-1]
    width = outs[0].shape[-1]
    rows = key.shape[0]
    step = rows // STEPS
    copies = []
    for i in range(STEPS):
        at = pl.ds(i * step, step)
        copies.append(
            [
                pltpu.make_async_copy(src.at[at], dst.at[at], sems.at[a, i])
                for a, (src, dst) in enumerate(zip((key, value, query, grad), bufs))
            ]
        )
        for copy in copies[i]:
            copy.start()
    for s in range(STEPS):
        at = pl.ds(s * step, step)
        for a, (left, right) in enumerate((bufs[:2], bufs[2:])):
            copies[s][2 * a].wait()
            copies[s][2 * a + 1].wait()
            for half in range(HALVES):
                for i, chip in enumerate(chips(n)):
                    for core in range(2):
                        cols = peer_columns(me, chip + core, half, width)
                        value = left[at, cols].astype(F32) * right[at, cols].astype(F32)
                        outs[half * (n // 2) + i][core, a, at] = value.astype(BF16)


def products(n, me, key, value, query, grad):
    rows, total = key.shape
    width = total // n // HALVES
    count = n // 2
    out = pl.pallas_call(
        functools.partial(product_kernel, n),
        in_specs=[SMEM] + [HBM] * 4,
        out_specs=[VMEM] * (4 + HALVES * count),
        out_shape=[pltpu.VMEM(key.shape, BF16)] * 4
        + [pltpu.VMEM((2, 2, rows, width), BF16)] * (HALVES * count),
        scratch_shapes=[pltpu.SemaphoreType.DMA((4, STEPS))],
        cost_estimate=SMALL_COST,
        compiler_params=PARAMS,
        name="products",
    )(me, key, value, query, grad)
    return out[:4], [out[4 + h * count : 4 + (h + 1) * count] for h in range(HALVES)]


def lane_groups(width):
    return [slice(i, i + 128) for i in range(0, width, 128)]


def filter_kernel(filt, fwd, *refs):
    spec, x, u = refs[-3:]
    m2, width = x.shape[1] // CLASSES, u.shape[-1]
    groups = lane_groups(width)
    rows = m2 // CLASSES
    for half in range(HALVES):
        for g, lanes in enumerate(groups):
            x[g] = filt[half * width + lanes.start : half * width + lanes.stop, :].T
        for c in range(CLASSES):
            for g, lanes in enumerate(groups):
                hi, lo = parts(x[g, pl.ds(c, m2, stride=CLASSES), :])
                u[c, :, lanes] = dot(fwd[c], jnp.concatenate([hi, hi], 0)) + dot(fwd[c, :, :m2], lo)

        def step(i, carry):
            r = pl.multiple_of(i * rows, rows)
            re, im = pl.ds(r, rows), pl.ds(m2 + r, rows)
            for lanes in groups:
                z = dft([(u[c, re, lanes], u[c, im, lanes]) for c in range(CLASSES)], -1)
                for k in range(CLASSES):
                    spec[half, k, re, lanes], spec[half, k, im, lanes] = z[k]
            return carry

        lax.fori_loop(0, CLASSES, step, 0)


def filter_spectra(filters, fwd, arrived):
    chans, length = filters.shape
    width = chans // HALVES
    m2 = length // CLASSES
    return pl.pallas_call(
        filter_kernel,
        in_specs=[VMEM] * (2 + len(arrived)),
        out_specs=VMEM,
        out_shape=pltpu.VMEM((HALVES, CLASSES, 2 * m2, width), F32),
        scratch_shapes=[
            pltpu.VMEM((width // 128, length, 128), F32),
            pltpu.VMEM((CLASSES, 2 * m2, width), F32),
        ],
        cost_estimate=SMALL_COST,
        compiler_params=PARAMS,
        name="filter_spectra",
    )(filters, fwd, *arrived)


def conv_kernel(n, d, half, me, *refs):
    count = n // 2
    got, (passed, filt, fwd, back) = refs[:count], refs[count : count + 4]
    refs = refs[-(count + 2 + 6) :]
    out, (keep, send), (nat, x, u, y, turned, grad) = refs[:count], refs[count : count + 2], refs[count + 2 :]
    rows, width = passed.shape[2:]
    blocks = sources(n, got, passed)
    m2 = x.shape[2]
    per = keep.shape[1] // CLASSES
    groups = lane_groups(width)
    step_rows = m2 // CLASSES
    part_rows = rows // CLASSES
    chans = slice(half * width, (half + 1) * width)

    for a in range(2):
        for g, lanes in enumerate(groups):
            for j, block in blocks:
                at = pl.multiple_of((me[0] ^ j) * rows, rows)
                nat[a, g, pl.ds(at, rows)] = block[a, :, lanes].astype(F32)
            for c in range(CLASSES):
                x[a, c, :, lanes] = nat[a, g, pl.ds(c, m2, stride=CLASSES), :].astype(BF16)
        for c in range(CLASSES):
            data = x[a, c]
            u[a, c] = dot(fwd[c], jnp.concatenate([data, data], 0))

    def middle(i, carry):
        r = pl.multiple_of(i * step_rows, step_rows)
        re, im = pl.ds(r, step_rows), pl.ds(m2 + r, step_rows)
        for lanes in groups:
            kv = dft([(u[0, c, re, lanes], u[0, c, im, lanes]) for c in range(CLASSES)], -1)
            wt = dft([(u[1, c, re, lanes], u[1, c, im, lanes]) for c in range(CLASSES)], -1)
            fs = [(filt[half, k, re, lanes], filt[half, k, im, lanes]) for k in range(CLASSES)]
            for o, (left, right, conj) in enumerate([(kv, fs, False), (wt, fs, True), (wt, kv, True)]):
                z = dft([times(s, t, conj) for s, t in zip(left, right)], 1)
                for c in range(CLASSES):
                    y[o, c, re, lanes] = z[c][0].astype(BF16)
                    y[o, c, im, lanes] = z[c][1].astype(BF16)
        return carry

    lax.fori_loop(0, CLASSES, middle, 0)

    for c in range(CLASSES):
        grad[c] = dot(back[c], y[2, c])
        for o in range(2):
            turned[o, c] = dot(back[c], y[o, c]).astype(BF16)
    for j in range(n):
        at = pl.multiple_of((me[0] ^ j) * part_rows, part_rows)
        for o in range(2):
            for c in range(CLASSES):
                out[j // 2][j % 2, o, c * part_rows : (c + 1) * part_rows] = turned[o, c, pl.ds(at, part_rows)]
    for j in range(d):
        at = pl.multiple_of((me[1] ^ j) * per, per)
        for c in range(CLASSES):
            part = grad[c, pl.ds(at, per)]
            if j % 2:
                send[j // 2, c * per : (c + 1) * per, chans] = part.astype(BF16)
            else:
                keep[j // 2, c * per : (c + 1) * per, chans] = part


def conv(n, d, half, me, got, passed, filt, fwd, back, before):
    _, _, rows, width = got[0].shape
    length = n * rows
    m2 = length // CLASSES
    count = n // 2
    out = pl.pallas_call(
        functools.partial(conv_kernel, n, d, half),
        in_specs=[SMEM] + [VMEM] * (count + 4 + len(before)),
        out_specs=[VMEM] * (count + 2),
        out_shape=[pltpu.VMEM((2, 2, rows, width), BF16)] * count
        + [pltpu.VMEM((d // 2, length // d, HALVES * width), dtype) for dtype in (F32, BF16)],
        scratch_shapes=[
            pltpu.VMEM((2, width // 128, length, 128), F32),
            pltpu.VMEM((2, CLASSES, m2, width), BF16),
            pltpu.VMEM((2, CLASSES, 2 * m2, width), F32),
            pltpu.VMEM((3, CLASSES, 2 * m2, width), BF16),
            pltpu.VMEM((2, CLASSES, m2, width), BF16),
            pltpu.VMEM((CLASSES, m2, width), F32),
        ],
        input_output_aliases={count + 5 + i: count + i for i in range(len(before))},
        cost_estimate=SMALL_COST,
        compiler_params=CONV_PARAMS,
        name="conv",
    )(me, *got, passed, filt, fwd, back, *before)
    return out[:count], out[count:]


def natural(scratch, piece):
    rows = piece.shape[0] // CLASSES
    for c in range(CLASSES):
        scratch[pl.ds(c, rows, stride=CLASSES), :] = piece[c * rows : (c + 1) * rows]
    return scratch[...]


def gate_kernel(half, js, picks, me, query, grad, value, key, gain, *refs):
    outs, (sent, sems, nat) = refs[-7:-3], refs[-3:]
    rows, width = sent.shape[2:]
    copies = []
    for i, (j, (array, place)) in enumerate(zip(js, picks)):
        block = refs[array].at[place]
        for g, lanes in enumerate(lane_groups(width)):
            cols = peer_columns(me, j, half, width, lanes.start, 128)
            scale = gain[:, cols]
            q, g_, v, k = (x[:, cols].astype(F32) for x in (query, grad, value, key))
            conv_out, corr_back = (
                natural(nat.at[i, o, g], block[o, :, lanes].astype(F32)) for o in range(2)
            )
            mixing = conv_out + scale * (k * v).astype(BF16).astype(F32)
            sent[0, i, :, lanes] = (q * mixing).astype(BF16)
            sent[1, i, :, lanes] = (g_ * mixing).astype(BF16)
            total = corr_back + scale * (g_ * q).astype(BF16).astype(F32)
            sent[2, i, :, lanes] = (total * v).astype(BF16)
            sent[3, i, :, lanes] = (total * k).astype(BF16)
        for a in range(4):
            to = outs[a].at[:, peer_columns(me, j, half, width)]
            copy = pltpu.make_async_copy(sent.at[a, i], to, sems.at[a, i])
            copy.start()
            copies.append(copy)
    for copy in copies:
        copy.wait()


def gate(half, js, picks, me, arrays, gain, got, outs):
    rows, width = got[0].shape[-2:]
    return pl.pallas_call(
        functools.partial(gate_kernel, half, js, picks),
        in_specs=[SMEM] + [VMEM] * (5 + len(got)) + [HBM] * len(outs),
        out_specs=[HBM] * 4,
        out_shape=[jax.ShapeDtypeStruct(arrays[0].shape, BF16)] * 4,
        scratch_shapes=[
            pltpu.VMEM((4, len(js), rows, width), BF16),
            pltpu.SemaphoreType.DMA((4, len(js))),
            pltpu.VMEM((len(js), 2, width // 128, rows, 128), F32),
        ],
        input_output_aliases={6 + len(got) + i: i for i in range(len(outs))},
        cost_estimate=SMALL_COST,
        compiler_params=PARAMS,
        name="gate",
    )(me, *arrays, gain, *got, *outs)


def add_kernel(keep, got, new_keep, new_send):
    for i in range(new_keep.shape[0]):
        new_keep[i] = keep[2 * i] + got[2 * i].astype(F32)
        new_send[i] = (keep[2 * i + 1] + got[2 * i + 1].astype(F32)).astype(BF16)


def turn_kernel(keep, got, out, nat):
    for g, lanes in enumerate(lane_groups(keep.shape[2])):
        total = keep[0, :, lanes] + got[0, :, lanes].astype(F32)
        out[lanes, :] = natural(nat.at[g], total).T


def sum_grads(d, keep, send):
    _, per, chans = keep.shape
    bit = 1
    while True:
        got = resident(lax.ppermute(send, "dp", [(i, i ^ bit) for i in range(d)]))
        if keep.shape[0] == 1:
            break
        shape = (keep.shape[0] // 2, per, chans)
        keep, send = pl.pallas_call(
            add_kernel,
            in_specs=[VMEM] * 2,
            out_specs=[VMEM] * 2,
            out_shape=[pltpu.VMEM(shape, F32), pltpu.VMEM(shape, BF16)],
            cost_estimate=SMALL_COST,
        compiler_params=PARAMS,
            name="add_grads",
        )(keep, got)
        bit *= 2
    return pl.pallas_call(
        turn_kernel,
        in_specs=[VMEM] * 2,
        out_specs=VMEM,
        out_shape=jax.ShapeDtypeStruct((chans, per), F32),
        scratch_shapes=[pltpu.VMEM((chans // 128, per, 128), F32)],
        cost_estimate=SMALL_COST,
        compiler_params=PARAMS,
        name="turn_grads",
    )(keep, got)


def across(n, blocks):
    return [blocks[0]] + [
        resident(lax.ppermute(block, "ctx", [(i, i ^ chip) for i in range(n)]))
        for chip, block in zip(chips(n)[1:], blocks[1:])
    ]


def pack_kernel(*refs):
    for i, ref in enumerate(refs[:-1]):
        refs[-1][i] = ref[1]


def inside(n, got):
    packed = pl.pallas_call(
        pack_kernel,
        in_specs=[VMEM] * len(got),
        out_specs=VMEM,
        out_shape=pltpu.VMEM((len(got), *got[0].shape[1:]), BF16),
        cost_estimate=SMALL_COST,
        compiler_params=PARAMS,
        name="pack",
    )(*got)
    return resident(lax.ppermute(packed, "ctx", [(i, i ^ 1) for i in range(n)]))


def after_kernel(*refs):
    pass


def after(arrived, blocks):
    count = len(arrived)
    return pl.pallas_call(
        after_kernel,
        in_specs=[VMEM] * (count + len(blocks)),
        out_specs=[VMEM] * len(blocks),
        out_shape=[pltpu.VMEM(b.shape, b.dtype) for b in blocks],
        input_output_aliases={count + i: i for i in range(len(blocks))},
        cost_estimate=SMALL_COST,
        compiler_params=PARAMS,
        name="after",
    )(*arrived, *blocks)


def local(n, d, query_in, key_in, value_in, grad_out, filters, skip_gain):
    fwd, back = (resident(jnp.asarray(t)) for t in tables(filters.shape[1]))
    filters = resident(filters)
    gain = skip_gain[None, :]
    me = jnp.stack([lax.axis_index("ctx"), lax.axis_index("dp")]).astype(jnp.int32)

    arrays = [in_hbm(x[0]) for x in (key_in, value_in, query_in, grad_out)]
    (key, value, query, grad), sent = products(n, me, *arrays)
    arrays = query, grad, value, key
    spec = filter_spectra(filters, fwd, [])
    got = [across(n, blocks) for blocks in sent]
    mixed, sums = [], []
    for half in range(HALVES):
        if mixed:
            got[half] = after(mixed[0][:1], got[half])
        passed = inside(n, got[half])
        blocks, sums = conv(n, d, half, me, got[half], passed, spec, fwd, back, sums)
        mixed.append(across(n, blocks))
    grad_filter = sum_grads(d, *sums)

    straight = [(i, 0) for i in range(n // 2)]
    outs = []
    for half in range(HALVES):
        passed = inside(n, mixed[half])
        outs = gate(half, chips(n), straight, me, arrays, gain, mixed[half], outs)
        handed = [(0, i) for i in range(n // 2)]
        outs = gate(half, [c + 1 for c in chips(n)], handed, me, arrays, gain, [passed], outs)
    return *(x[None] for x in outs), grad_filter


def solution(mesh):
    rows = P("dp", "ctx", None)
    return jax.shard_map(
        functools.partial(local, mesh.shape["ctx"], mesh.shape["dp"]),
        mesh=mesh,
        in_specs=(rows, rows, rows, rows, P("ctx", None), P()),
        out_specs=(rows, rows, rows, rows, P("ctx", "dp")),
        check_vma=False,
    )
```

```python
import functools
import math

import jax
import jax.numpy as jnp
import ml_dtypes
import numpy as np
from jax import lax
from jax.experimental import pallas as pl
from jax.experimental.pallas import tpu as pltpu
from jax.sharding import PartitionSpec as P

F32 = jnp.float32
BF16 = jnp.bfloat16
CLASSES = 8
HALVES = 2
STEPS = 4
PARAMS = pltpu.CompilerParams(vmem_limit_bytes=16 * 1024 * 1024)
CONV_PARAMS = pltpu.CompilerParams(vmem_limit_bytes=34 * 1024 * 1024)
SMEM = pl.BlockSpec(memory_space=pltpu.SMEM)
VMEM = pl.BlockSpec(memory_space=pltpu.VMEM)
SMALL_COST = pl.CostEstimate(flops=0, bytes_accessed=1024, transcendentals=0)
HBM = pl.BlockSpec(memory_space=pltpu.HBM)


def tables(length):
    m2 = length // CLASSES
    c = np.arange(CLASSES)[:, None, None]
    j = np.arange(m2)[None, :, None]
    m = np.arange(m2)[None, None, :]
    turn = ((CLASSES * m + c) * (2 * j + 1)) % (4 * length)
    angle = 2 * np.pi * turn / (4 * length)
    forward = np.concatenate([np.cos(angle), -np.sin(angle)], 1)
    back = np.swapaxes(forward, 1, 2) / length

    def parts(x):
        hi = x.astype(ml_dtypes.bfloat16)
        return hi, (x - hi.astype(np.float64)).astype(ml_dtypes.bfloat16)

    return np.concatenate(parts(forward), 2), back.astype(ml_dtypes.bfloat16)


def parts(x):
    hi = x.astype(BF16)
    return hi, (x - hi.astype(F32)).astype(BF16)


def dot(a, b):
    return jnp.dot(a, b, preferred_element_type=F32)


def dft(z, sign):
    n = len(z)
    if n == 1:
        return z
    even, odd = dft(z[0::2], sign), dft(z[1::2], sign)
    low, high = [], []
    for k in range(n // 2):
        (er, ei), (zr, zi) = even[k], odd[k]
        if k == 0:
            tr, ti = zr, zi
        elif 4 * k == n:
            tr, ti = (-zi, zr) if sign > 0 else (zi, -zr)
        else:
            c, s = math.cos(2 * math.pi * k / n), sign * math.sin(2 * math.pi * k / n)
            if 8 * k == n:
                tr, ti = (c * (zr - zi), c * (zi + zr)) if sign > 0 else (c * (zr + zi), c * (zi - zr))
            elif 8 * k == 3 * n:
                tr, ti = (c * (zr + zi), c * (zi - zr)) if sign > 0 else (c * (zr - zi), c * (zi + zr))
            else:
                tr, ti = c * zr - s * zi, c * zi + s * zr
        low.append((er + tr, ei + ti))
        high.append((er - tr, ei - ti))
    return low + high


def times(x, f, conj):
    (xr, xi), (fr, fi) = x, f
    if conj:
        return xr * fr + xi * fi, xi * fr - xr * fi
    return xr * fr - xi * fi, xr * fi + xi * fr


def resident(x):
    return pltpu.with_memory_space_constraint(x, pltpu.VMEM)


def in_hbm(x):
    return pltpu.with_memory_space_constraint(x, pltpu.HBM)


def chips(n):
    return range(0, n, 2)


def sources(n, got, passed):
    straight = [(chip, got[i].at[0]) for i, chip in enumerate(chips(n))]
    return straight + [(chip + 1, passed[i]) for i, chip in enumerate(chips(n))]


def peer_columns(me, j, half, width, lane=0, lanes=None):
    start = (HALVES * (me[0] ^ j) + half) * width + lane
    return pl.ds(pl.multiple_of(start, 128), lanes or width)


def product_kernel(n, me, key, value, query, grad, *refs):
    bufs, outs, sems = refs[:4], refs[4:-1], refs[-1]
    width = outs[0].shape[-1]
    rows = key.shape[0]
    step = rows // STEPS
    copies = []
    for i in range(STEPS):
        at = pl.ds(i * step, step)
        copies.append(
            [
                pltpu.make_async_copy(src.at[at], dst.at[at], sems.at[a, i])
                for a, (src, dst) in enumerate(zip((key, value, query, grad), bufs))
            ]
        )
        for copy in copies[i]:
            copy.start()
    for s in range(STEPS):
        at = pl.ds(s * step, step)
        for a, (left, right) in enumerate((bufs[:2], bufs[2:])):
            copies[s][2 * a].wait()
            copies[s][2 * a + 1].wait()
            for half in range(HALVES):
                for i, chip in enumerate(chips(n)):
                    for core in range(2):
                        cols = peer_columns(me, chip + core, half, width)
                        value = left[at, cols].astype(F32) * right[at, cols].astype(F32)
                        outs[half * (n // 2) + i][core, a, at] = value.astype(BF16)


def products(n, me, key, value, query, grad):
    rows, total = key.shape
    width = total // n // HALVES
    count = n // 2
    out = pl.pallas_call(
        functools.partial(product_kernel, n),
        in_specs=[SMEM] + [HBM] * 4,
        out_specs=[VMEM] * (4 + HALVES * count),
        out_shape=[pltpu.VMEM(key.shape, BF16)] * 4
        + [pltpu.VMEM((2, 2, rows, width), BF16)] * (HALVES * count),
        scratch_shapes=[pltpu.SemaphoreType.DMA((4, STEPS))],
        cost_estimate=SMALL_COST,
        compiler_params=PARAMS,
        name="products",
    )(me, key, value, query, grad)
    return out[:4], [out[4 + h * count : 4 + (h + 1) * count] for h in range(HALVES)]


def lane_groups(width):
    return [slice(i, i + 128) for i in range(0, width, 128)]


def filter_kernel(filt, fwd, *refs):
    spec, x, u = refs[-3:]
    m2, width = x.shape[1] // CLASSES, u.shape[-1]
    groups = lane_groups(width)
    rows = m2 // CLASSES
    for half in range(HALVES):
        for g, lanes in enumerate(groups):
            x[g] = filt[half * width + lanes.start : half * width + lanes.stop, :].T
        for c in range(CLASSES):
            for g, lanes in enumerate(groups):
                hi, lo = parts(x[g, pl.ds(c, m2, stride=CLASSES), :])
                u[c, :, lanes] = dot(fwd[c], jnp.concatenate([hi, hi], 0)) + dot(fwd[c, :, :m2], lo)

        def step(i, carry):
            r = pl.multiple_of(i * rows, rows)
            re, im = pl.ds(r, rows), pl.ds(m2 + r, rows)
            for lanes in groups:
                z = dft([(u[c, re, lanes], u[c, im, lanes]) for c in range(CLASSES)], -1)
                for k in range(CLASSES):
                    spec[half, k, re, lanes], spec[half, k, im, lanes] = z[k]
            return carry

        lax.fori_loop(0, CLASSES, step, 0)


def filter_spectra(filters, fwd, arrived):
    chans, length = filters.shape
    width = chans // HALVES
    m2 = length // CLASSES
    return pl.pallas_call(
        filter_kernel,
        in_specs=[VMEM] * (2 + len(arrived)),
        out_specs=VMEM,
        out_shape=pltpu.VMEM((HALVES, CLASSES, 2 * m2, width), F32),
        scratch_shapes=[
            pltpu.VMEM((width // 128, length, 128), F32),
            pltpu.VMEM((CLASSES, 2 * m2, width), F32),
        ],
        cost_estimate=SMALL_COST,
        compiler_params=PARAMS,
        name="filter_spectra",
    )(filters, fwd, *arrived)


def conv_kernel(n, d, half, me, *refs):
    count = n // 2
    got, passed, (filt, fwd, back) = refs[:count], refs[count:n], refs[n : n + 3]
    refs = refs[-(count + 2 + 6) :]
    out, (keep, send), (nat, x, u, y, turned, grad) = refs[:count], refs[count : count + 2], refs[count + 2 :]
    rows, width = passed[0].shape[1:]
    blocks = sources(n, got, passed)
    m2 = x.shape[2]
    per = keep.shape[1] // CLASSES
    groups = lane_groups(width)
    step_rows = m2 // CLASSES
    part_rows = rows // CLASSES

    for a in range(2):
        for g, lanes in enumerate(groups):
            for j, block in blocks:
                at = pl.multiple_of((me[0] ^ j) * rows, rows)
                nat[a, g, pl.ds(at, rows)] = block[a, :, lanes].astype(F32)
            for c in range(CLASSES):
                x[a, c, :, lanes] = nat[a, g, pl.ds(c, m2, stride=CLASSES), :].astype(BF16)
        for c in range(CLASSES):
            data = x[a, c]
            u[a, c] = dot(fwd[c], jnp.concatenate([data, data], 0))

    def middle(i, carry):
        r = pl.multiple_of(i * step_rows, step_rows)
        re, im = pl.ds(r, step_rows), pl.ds(m2 + r, step_rows)
        for lanes in groups:
            kv = dft([(u[0, c, re, lanes], u[0, c, im, lanes]) for c in range(CLASSES)], -1)
            wt = dft([(u[1, c, re, lanes], u[1, c, im, lanes]) for c in range(CLASSES)], -1)
            fs = [(filt[half, k, re, lanes], filt[half, k, im, lanes]) for k in range(CLASSES)]
            for o, (left, right, conj) in enumerate([(kv, fs, False), (wt, fs, True), (wt, kv, True)]):
                z = dft([times(s, t, conj) for s, t in zip(left, right)], 1)
                for c in range(CLASSES):
                    y[o, c, re, lanes] = z[c][0].astype(BF16)
                    y[o, c, im, lanes] = z[c][1].astype(BF16)
        return carry

    lax.fori_loop(0, CLASSES, middle, 0)

    for c in range(CLASSES):
        grad[c] = dot(back[c], y[2, c])
        for o in range(2):
            turned[o, c] = dot(back[c], y[o, c]).astype(BF16)
    for j in range(n):
        at = pl.multiple_of((me[0] ^ j) * part_rows, part_rows)
        for o in range(2):
            for c in range(CLASSES):
                out[j // 2][j % 2, o, c * part_rows : (c + 1) * part_rows] = turned[o, c, pl.ds(at, part_rows)]
    for j in range(d):
        at = pl.multiple_of((me[1] ^ j) * per, per)
        for c in range(CLASSES):
            part = grad[c, pl.ds(at, per)]
            if j % 2:
                send[j // 2, c * per : (c + 1) * per] = part.astype(BF16)
            else:
                keep[j // 2, c * per : (c + 1) * per] = part


def conv(n, d, half, me, got, passed, filt, fwd, back):
    _, _, rows, width = got[0].shape
    length = n * rows
    m2 = length // CLASSES
    count = n // 2
    out = pl.pallas_call(
        functools.partial(conv_kernel, n, d, half),
        in_specs=[SMEM] + [VMEM] * (n + 3),
        out_specs=[VMEM] * (count + 2),
        out_shape=[pltpu.VMEM((2, 2, rows, width), BF16)] * count
        + [pltpu.VMEM((d // 2, length // d, width), dtype) for dtype in (F32, BF16)],
        scratch_shapes=[
            pltpu.VMEM((2, width // 128, length, 128), F32),
            pltpu.VMEM((2, CLASSES, m2, width), BF16),
            pltpu.VMEM((2, CLASSES, 2 * m2, width), F32),
            pltpu.VMEM((3, CLASSES, 2 * m2, width), BF16),
            pltpu.VMEM((2, CLASSES, m2, width), BF16),
            pltpu.VMEM((CLASSES, m2, width), F32),
        ],
        cost_estimate=SMALL_COST,
        compiler_params=CONV_PARAMS,
        name="conv",
    )(me, *got, *passed, filt, fwd, back)
    return out[:count], out[count:]


def natural(scratch, piece):
    rows = piece.shape[0] // CLASSES
    for c in range(CLASSES):
        scratch[pl.ds(c, rows, stride=CLASSES), :] = piece[c * rows : (c + 1) * rows]
    return scratch[...]


def gate_kernel(half, js, straight, me, query, grad, value, key, gain, *refs):
    outs, (sent, sems, nat) = refs[-7:-3], refs[-3:]
    rows, width = sent.shape[2:]
    copies = []
    for i, j in enumerate(js):
        block = refs[i].at[0] if straight else refs[i]
        for g, lanes in enumerate(lane_groups(width)):
            cols = peer_columns(me, j, half, width, lanes.start, 128)
            scale = gain[:, cols]
            q, g_, v, k = (x[:, cols].astype(F32) for x in (query, grad, value, key))
            conv_out, corr_back = (
                natural(nat.at[i, o, g], block[o, :, lanes].astype(F32)) for o in range(2)
            )
            mixing = conv_out + scale * (k * v).astype(BF16).astype(F32)
            sent[0, i, :, lanes] = (q * mixing).astype(BF16)
            sent[1, i, :, lanes] = (g_ * mixing).astype(BF16)
            total = corr_back + scale * (g_ * q).astype(BF16).astype(F32)
            sent[2, i, :, lanes] = (total * v).astype(BF16)
            sent[3, i, :, lanes] = (total * k).astype(BF16)
        for a in range(4):
            to = outs[a].at[:, peer_columns(me, j, half, width)]
            copy = pltpu.make_async_copy(sent.at[a, i], to, sems.at[a, i])
            copy.start()
            copies.append(copy)
    for copy in copies:
        copy.wait()


def gate(half, js, me, arrays, gain, got, outs):
    rows, width = got[0].shape[-2:]
    straight = got[0].ndim == 4
    return pl.pallas_call(
        functools.partial(gate_kernel, half, js, straight),
        in_specs=[SMEM] + [VMEM] * (5 + len(got)) + [HBM] * len(outs),
        out_specs=[HBM] * 4,
        out_shape=[jax.ShapeDtypeStruct(arrays[0].shape, BF16)] * 4,
        scratch_shapes=[
            pltpu.VMEM((4, len(js), rows, width), BF16),
            pltpu.SemaphoreType.DMA((4, len(js))),
            pltpu.VMEM((len(js), 2, width // 128, rows, 128), F32),
        ],
        input_output_aliases={6 + len(got) + i: i for i in range(len(outs))},
        cost_estimate=SMALL_COST,
        compiler_params=PARAMS,
        name="gate",
    )(me, *arrays, gain, *got, *outs)


def add_kernel(keep, got, new_keep, new_send):
    for i in range(new_keep.shape[0]):
        new_keep[i] = keep[2 * i] + got[2 * i].astype(F32)
        new_send[i] = (keep[2 * i + 1] + got[2 * i + 1].astype(F32)).astype(BF16)


def trade(d, bit, send):
    return resident(lax.ppermute(send, "dp", [(i, i ^ bit) for i in range(d)]))


def add_grads(keep, got):
    shape = (keep.shape[0] // 2, *keep.shape[1:])
    return pl.pallas_call(
        add_kernel,
        in_specs=[VMEM] * 2,
        out_specs=[VMEM] * 2,
        out_shape=[pltpu.VMEM(shape, F32), pltpu.VMEM(shape, BF16)],
        cost_estimate=SMALL_COST,
        compiler_params=PARAMS,
        name="add_grads",
    )(keep, got)


def turn_kernel(*refs):
    out, nat = refs[-2:]
    width = refs[0].shape[2]
    for half in range(HALVES):
        keep, got = refs[2 * half : 2 * half + 2]
        for g, lanes in enumerate(lane_groups(width)):
            total = keep[0, :, lanes] + got[0, :, lanes].astype(F32)
            to = slice(half * width + lanes.start, half * width + lanes.stop)
            out[to, :] = natural(nat.at[half, g], total).T


def turn_grads(halves):
    _, per, width = halves[0][0].shape
    return pl.pallas_call(
        turn_kernel,
        in_specs=[VMEM] * (2 * HALVES),
        out_specs=VMEM,
        out_shape=jax.ShapeDtypeStruct((HALVES * width, per), F32),
        scratch_shapes=[pltpu.VMEM((HALVES, width // 128, per, 128), F32)],
        cost_estimate=SMALL_COST,
        compiler_params=PARAMS,
        name="turn_grads",
    )(*halves[0], *halves[1])


def across(n, blocks):
    return [blocks[0]] + [
        resident(lax.ppermute(block, "ctx", [(i, i ^ chip) for i in range(n)]))
        for chip, block in zip(chips(n)[1:], blocks[1:])
    ]


def pack_kernel(*refs):
    count = len(refs) // 2
    for ref, out in zip(refs[:count], refs[count:]):
        out[...] = ref[1]


def inside(n, got):
    packed = pl.pallas_call(
        pack_kernel,
        in_specs=[VMEM] * len(got),
        out_specs=[VMEM] * len(got),
        out_shape=[pltpu.VMEM(got[0].shape[1:], BF16)] * len(got),
        cost_estimate=SMALL_COST,
        compiler_params=PARAMS,
        name="pack",
    )(*got)
    return [resident(lax.ppermute(x, "ctx", [(i, i ^ 1) for i in range(n)])) for x in packed]


def after_kernel(*refs):
    pass


def after(arrived, blocks):
    count = len(arrived)
    return pl.pallas_call(
        after_kernel,
        in_specs=[VMEM] * (count + len(blocks)),
        out_specs=[VMEM] * len(blocks),
        out_shape=[pltpu.VMEM(b.shape, b.dtype) for b in blocks],
        input_output_aliases={count + i: i for i in range(len(blocks))},
        cost_estimate=SMALL_COST,
        compiler_params=PARAMS,
        name="after",
    )(*arrived, *blocks)


def local(n, d, query_in, key_in, value_in, grad_out, filters, skip_gain):
    fwd, back = (resident(jnp.asarray(t)) for t in tables(filters.shape[1]))
    filters = resident(filters)
    gain = skip_gain[None, :]
    me = jnp.stack([lax.axis_index("ctx"), lax.axis_index("dp")]).astype(jnp.int32)

    arrays = [in_hbm(x[0]) for x in (key_in, value_in, query_in, grad_out)]
    (key, value, query, grad), sent = products(n, me, *arrays)
    arrays = query, grad, value, key
    spec = filter_spectra(filters, fwd, [])
    got = [across(n, blocks) for blocks in sent]
    bits = [1 << b for b in range(d.bit_length() - 1)]
    blocks, (keep, send) = conv(n, d, 0, me, got[0], inside(n, got[0]), spec, fwd, back)
    first = across(n, blocks)
    keep, send = add_grads(keep, trade(d, 1, send))
    for bit in bits[1:-1]:
        keep, send = add_grads(keep, trade(d, bit, send))
    sums = [(keep, trade(d, bits[-1], send))]

    got[1] = after(blocks[:1], got[1])
    blocks, (keep, send) = conv(n, d, 1, me, got[1], inside(n, got[1]), spec, fwd, back)
    second = across(n, after(sums[0][:1], blocks))
    keep, send = add_grads(keep, trade(d, 1, send))
    for bit in bits[1:-1]:
        keep, send = add_grads(keep, trade(d, bit, send))
    sums.append((keep, trade(d, bits[-1], send)))

    odd = [c + 1 for c in chips(n)]
    passed = inside(n, first)
    outs = gate(0, chips(n), me, arrays, gain, after([keep, sums[0][1]], first), [])
    outs = gate(0, odd, me, arrays, gain, passed, outs)
    grad_filter = turn_grads(sums)
    passed = inside(n, second)
    outs = gate(1, chips(n), me, arrays, gain, second, outs)
    outs = gate(1, odd, me, arrays, gain, passed, outs)
    return *(x[None] for x in outs), grad_filter


def solution(mesh):
    rows = P("dp", "ctx", None)
    return jax.shard_map(
        functools.partial(local, mesh.shape["ctx"], mesh.shape["dp"]),
        mesh=mesh,
        in_specs=(rows, rows, rows, rows, P("ctx", None), P()),
        out_specs=(rows, rows, rows, rows, P("ctx", "dp")),
        check_vma=False,
    )
```

```python
import functools
import math

import jax
import jax.numpy as jnp
import ml_dtypes
import numpy as np
from jax import lax
from jax.experimental import pallas as pl
from jax.experimental.pallas import tpu as pltpu
from jax.sharding import PartitionSpec as P

F32 = jnp.float32
BF16 = jnp.bfloat16
CLASSES = 8
HALVES = 2
STEPS = 4
PARAMS = pltpu.CompilerParams(vmem_limit_bytes=16 * 1024 * 1024)
CONV_PARAMS = pltpu.CompilerParams(vmem_limit_bytes=34 * 1024 * 1024)
SMEM = pl.BlockSpec(memory_space=pltpu.SMEM)
VMEM = pl.BlockSpec(memory_space=pltpu.VMEM)
HBM = pl.BlockSpec(memory_space=pltpu.HBM)


def tables(length):
    m2 = length // CLASSES
    c = np.arange(CLASSES)[:, None, None]
    j = np.arange(m2)[None, :, None]
    m = np.arange(m2)[None, None, :]
    turn = ((CLASSES * m + c) * (2 * j + 1)) % (4 * length)
    angle = 2 * np.pi * turn / (4 * length)
    forward = np.concatenate([np.cos(angle), -np.sin(angle)], 1)
    back = np.swapaxes(forward, 1, 2) / length

    def parts(x):
        hi = x.astype(ml_dtypes.bfloat16)
        return hi, (x - hi.astype(np.float64)).astype(ml_dtypes.bfloat16)

    return np.concatenate(parts(forward), 2), back.astype(ml_dtypes.bfloat16)


def parts(x):
    hi = x.astype(BF16)
    return hi, (x - hi.astype(F32)).astype(BF16)


def dot(a, b):
    return jnp.dot(a, b, preferred_element_type=F32)


def dft(z, sign):
    n = len(z)
    if n == 1:
        return z
    even, odd = dft(z[0::2], sign), dft(z[1::2], sign)
    low, high = [], []
    for k in range(n // 2):
        (er, ei), (zr, zi) = even[k], odd[k]
        if k == 0:
            tr, ti = zr, zi
        elif 4 * k == n:
            tr, ti = (-zi, zr) if sign > 0 else (zi, -zr)
        else:
            c, s = math.cos(2 * math.pi * k / n), sign * math.sin(2 * math.pi * k / n)
            if 8 * k == n:
                tr, ti = (c * (zr - zi), c * (zi + zr)) if sign > 0 else (c * (zr + zi), c * (zi - zr))
            elif 8 * k == 3 * n:
                tr, ti = (c * (zr + zi), c * (zi - zr)) if sign > 0 else (c * (zr - zi), c * (zi + zr))
            else:
                tr, ti = c * zr - s * zi, c * zi + s * zr
        low.append((er + tr, ei + ti))
        high.append((er - tr, ei - ti))
    return low + high


def times(x, f, conj):
    (xr, xi), (fr, fi) = x, f
    if conj:
        return xr * fr + xi * fi, xi * fr - xr * fi
    return xr * fr - xi * fi, xr * fi + xi * fr


def resident(x):
    return pltpu.with_memory_space_constraint(x, pltpu.VMEM)


def in_hbm(x):
    return pltpu.with_memory_space_constraint(x, pltpu.HBM)


def peer_columns(me, j, width):
    return pl.ds(pl.multiple_of((me[0] ^ j) * width, 128), width)


def product_kernel(n, me, key, value, query, grad, *refs):
    bufs, outs, sems = refs[:4], refs[4:-1], refs[-1]
    _, rows, width = outs[0].shape
    step = rows // STEPS
    copies = []
    for i in range(STEPS):
        at = pl.ds(i * step, step)
        copies.append(
            [
                pltpu.make_async_copy(src.at[at], dst.at[at], sems.at[a, i])
                for a, (src, dst) in enumerate(zip((key, value, query, grad), bufs))
            ]
        )
        for copy in copies[i]:
            copy.start()
    for s in range(STEPS):
        at = pl.ds(s * step, step)
        for a, (left, right) in enumerate((bufs[:2], bufs[2:])):
            copies[s][2 * a].wait()
            copies[s][2 * a + 1].wait()
            for j in range(n):
                cols = peer_columns(me, j, HALVES * width)
                value = (left[at, cols].astype(F32) * right[at, cols].astype(F32)).astype(BF16)
                outs[peers(n).index(j)][a, at] = value[:, :width]
                outs[n + j // 2][j % 2, a, at] = value[:, width:]


def products(n, me, key, value, query, grad):
    rows, total = key.shape
    width = total // n // HALVES
    out = pl.pallas_call(
        functools.partial(product_kernel, n),
        in_specs=[SMEM] + [HBM] * 4,
        out_specs=[VMEM] * (4 + n + n // 2),
        out_shape=[pltpu.VMEM(key.shape, BF16)] * 4
        + [pltpu.VMEM((2, rows, width), BF16)] * n
        + [pltpu.VMEM((2, 2, rows, width), BF16)] * (n // 2),
        scratch_shapes=[pltpu.SemaphoreType.DMA((4, STEPS))],
        compiler_params=PARAMS,
        name="products",
    )(me, key, value, query, grad)
    return out[:4], out[4 : 4 + n], out[4 + n :]


def lane_groups(width):
    return [slice(i, i + 128) for i in range(0, width, 128)]


def filter_kernel(filt, fwd, *refs):
    spec, x, u = refs[-3:]
    m2, width = x.shape[1] // CLASSES, u.shape[-1]
    groups = lane_groups(width)
    rows = m2 // CLASSES
    for half in range(HALVES):
        for g, lanes in enumerate(groups):
            x[g] = filt[half * width + lanes.start : half * width + lanes.stop, :].T
        for c in range(CLASSES):
            for g, lanes in enumerate(groups):
                hi, lo = parts(x[g, pl.ds(c, m2, stride=CLASSES), :])
                u[c, :, lanes] = dot(fwd[c], jnp.concatenate([hi, hi], 0)) + dot(fwd[c, :, :m2], lo)

        def step(i, carry):
            r = pl.multiple_of(i * rows, rows)
            re, im = pl.ds(r, rows), pl.ds(m2 + r, rows)
            for lanes in groups:
                z = dft([(u[c, re, lanes], u[c, im, lanes]) for c in range(CLASSES)], -1)
                for k in range(CLASSES):
                    spec[half, k, re, lanes], spec[half, k, im, lanes] = z[k]
            return carry

        lax.fori_loop(0, CLASSES, step, 0)


def filter_spectra(filters, fwd, arrived):
    chans, length = filters.shape
    width = chans // HALVES
    m2 = length // CLASSES
    return pl.pallas_call(
        filter_kernel,
        in_specs=[VMEM] * (2 + len(arrived)),
        out_specs=VMEM,
        out_shape=pltpu.VMEM((HALVES, CLASSES, 2 * m2, width), F32),
        scratch_shapes=[
            pltpu.VMEM((width // 128, length, 128), F32),
            pltpu.VMEM((CLASSES, 2 * m2, width), F32),
        ],
        compiler_params=PARAMS,
        name="filter_spectra",
    )(filters, fwd, *arrived)


def conv_kernel(n, d, half, me, *refs):
    taken = n // 2 + 1 if half else n
    got, (filt, fwd, back) = refs[:taken], refs[taken : taken + 3]
    refs = refs[-(n - 1 + 2 + 6) :]
    *near, far, keep, send, nat, x, u, y, turned, grad = refs
    rows, width = got[0].shape[-2:]
    if half:
        blocks = [(chip, got[chip // 2].at[0]) for chip in range(0, n, 2)]
        blocks += [(chip + 1, got[-1].at[chip // 2]) for chip in range(0, n, 2)]
    else:
        blocks = list(zip(peers(n), got))
    m2 = x.shape[2]
    per = keep.shape[1] // CLASSES
    groups = lane_groups(width)
    step_rows = m2 // CLASSES
    part_rows = rows // CLASSES
    chans = slice(half * width, (half + 1) * width)

    for a in range(2):
        for g, lanes in enumerate(groups):
            for j, block in blocks:
                at = pl.multiple_of((me[0] ^ j) * rows, rows)
                nat[a, g, pl.ds(at, rows)] = block[a, :, lanes].astype(F32)
            for c in range(CLASSES):
                x[a, c, :, lanes] = nat[a, g, pl.ds(c, m2, stride=CLASSES), :].astype(BF16)
        for c in range(CLASSES):
            data = x[a, c]
            u[a, c] = dot(fwd[c], jnp.concatenate([data, data], 0))

    def middle(i, carry):
        r = pl.multiple_of(i * step_rows, step_rows)
        re, im = pl.ds(r, step_rows), pl.ds(m2 + r, step_rows)
        for lanes in groups:
            kv = dft([(u[0, c, re, lanes], u[0, c, im, lanes]) for c in range(CLASSES)], -1)
            wt = dft([(u[1, c, re, lanes], u[1, c, im, lanes]) for c in range(CLASSES)], -1)
            fs = [(filt[half, k, re, lanes], filt[half, k, im, lanes]) for k in range(CLASSES)]
            for o, (left, right, conj) in enumerate([(kv, fs, False), (wt, fs, True), (wt, kv, True)]):
                z = dft([times(s, t, conj) for s, t in zip(left, right)], 1)
                for c in range(CLASSES):
                    y[o, c, re, lanes] = z[c][0].astype(BF16)
                    y[o, c, im, lanes] = z[c][1].astype(BF16)
        return carry

    lax.fori_loop(0, CLASSES, middle, 0)

    for c in range(CLASSES):
        grad[c] = dot(back[c], y[2, c])
        for o in range(2):
            turned[o, c] = dot(back[c], y[o, c]).astype(BF16)
    ends = [*zip(near_peers(n), near), (n - 2, far.at[0]), (n - 1, far.at[1])]
    for j, block in ends:
        at = pl.multiple_of((me[0] ^ j) * part_rows, part_rows)
        for o in range(2):
            for c in range(CLASSES):
                block[half, o, c * part_rows : (c + 1) * part_rows] = turned[o, c, pl.ds(at, part_rows)]
    for j in range(d):
        at = pl.multiple_of((me[1] ^ j) * per, per)
        for c in range(CLASSES):
            part = grad[c, pl.ds(at, per)]
            if j % 2:
                send[j // 2, c * per : (c + 1) * per, chans] = part.astype(BF16)
            else:
                keep[j // 2, c * per : (c + 1) * per, chans] = part


def conv(n, d, half, me, got, filt, fwd, back, before):
    rows, width = got[0].shape[-2:]
    length = n * rows
    m2 = length // CLASSES
    first = 4 + len(got)
    out = pl.pallas_call(
        functools.partial(conv_kernel, n, d, half),
        in_specs=[SMEM] + [VMEM] * (len(got) + 3 + len(before)),
        out_specs=[VMEM] * (n - 1 + 2),
        out_shape=[pltpu.VMEM((HALVES, 2, rows, width), BF16)] * (n - 2)
        + [pltpu.VMEM((2, HALVES, 2, rows, width), BF16)]
        + [pltpu.VMEM((d // 2, length // d, HALVES * width), dtype) for dtype in (F32, BF16)],
        scratch_shapes=[
            pltpu.VMEM((2, width // 128, length, 128), F32),
            pltpu.VMEM((2, CLASSES, m2, width), BF16),
            pltpu.VMEM((2, CLASSES, 2 * m2, width), F32),
            pltpu.VMEM((3, CLASSES, 2 * m2, width), BF16),
            pltpu.VMEM((2, CLASSES, m2, width), BF16),
            pltpu.VMEM((CLASSES, m2, width), F32),
        ],
        input_output_aliases={first + i: i for i in range(len(before))},
        compiler_params=CONV_PARAMS,
        name="conv",
    )(me, *got, filt, fwd, back, *before)
    return out


def natural(scratch, piece):
    rows = piece.shape[0] // CLASSES
    for c in range(CLASSES):
        scratch[pl.ds(c, rows, stride=CLASSES), :] = piece[c * rows : (c + 1) * rows]
    return scratch[...]


def gate_kernel(js, me, query, grad, value, key, gain, *refs):
    got, outs, (sent, sems, nat) = refs[: len(js)], refs[-7:-3], refs[-3:]
    got = [ref.at[0] if len(ref.shape) == 5 else ref for ref in got]
    _, _, rows, width = got[0].shape
    copies = []
    for i, j in enumerate(js):
        block = peer_columns(me, j, HALVES * width)
        for half in range(HALVES):
            for g, lanes in enumerate(lane_groups(width)):
                at = half * width + lanes.start
                start = pl.multiple_of((me[0] ^ j) * HALVES * width + at, 128)
                cols = pl.ds(start, 128)
                to = slice(at, at + 128)
                scale = gain[:, cols]
                q, g_, v, k = (x[:, cols].astype(F32) for x in (query, grad, value, key))
                conv_out, corr_back = (
                    natural(nat.at[i, o, half, g], got[i][half, o, :, lanes].astype(F32)) for o in range(2)
                )
                mixing = conv_out + scale * (k * v).astype(BF16).astype(F32)
                sent[0, i, :, to] = (q * mixing).astype(BF16)
                sent[1, i, :, to] = (g_ * mixing).astype(BF16)
                total = corr_back + scale * (g_ * q).astype(BF16).astype(F32)
                sent[2, i, :, to] = (total * v).astype(BF16)
                sent[3, i, :, to] = (total * k).astype(BF16)
        for a in range(4):
            copy = pltpu.make_async_copy(sent.at[a, i], outs[a].at[:, block], sems.at[a, i])
            copy.start()
            copies.append(copy)
    for copy in copies:
        copy.wait()


def gate(js, me, query, grad, value, key, gain, got, outs):
    _, _, rows, width = got[0].shape
    return pl.pallas_call(
        functools.partial(gate_kernel, js),
        in_specs=[SMEM] + [VMEM] * (5 + len(got)) + [HBM] * len(outs),
        out_specs=[HBM] * 4,
        out_shape=[jax.ShapeDtypeStruct(query.shape, BF16)] * 4,
        scratch_shapes=[
            pltpu.VMEM((4, len(js), rows, HALVES * width), BF16),
            pltpu.SemaphoreType.DMA((4, len(js))),
            pltpu.VMEM((len(js), 2, HALVES, width // 128, rows, 128), F32),
        ],
        input_output_aliases={6 + len(got) + i: i for i in range(len(outs))},
        compiler_params=PARAMS,
        name="gate",
    )(me, query, grad, value, key, gain, *got, *outs)


def add_kernel(keep, got, new_keep, new_send):
    for i in range(new_keep.shape[0]):
        new_keep[i] = keep[2 * i] + got[2 * i].astype(F32)
        new_send[i] = (keep[2 * i + 1] + got[2 * i + 1].astype(F32)).astype(BF16)


def turn_kernel(keep, got, out, nat):
    for g, lanes in enumerate(lane_groups(keep.shape[2])):
        total = keep[0, :, lanes] + got[0, :, lanes].astype(F32)
        out[lanes, :] = natural(nat.at[g], total).T


def sum_grads(d, keep, send, arrived):
    _, per, chans = keep.shape
    bit = 1
    while True:
        got = resident(lax.ppermute(send, "dp", [(i, i ^ bit) for i in range(d)]))
        if keep.shape[0] == 1:
            break
        got, = after(arrived, [got])
        shape = (keep.shape[0] // 2, per, chans)
        keep, send = pl.pallas_call(
            add_kernel,
            in_specs=[VMEM] * 2,
            out_specs=[VMEM] * 2,
            out_shape=[pltpu.VMEM(shape, F32), pltpu.VMEM(shape, BF16)],
            compiler_params=PARAMS,
            name="add_grads",
        )(keep, got)
        bit *= 2
    return pl.pallas_call(
        turn_kernel,
        in_specs=[VMEM] * 2,
        out_specs=VMEM,
        out_shape=jax.ShapeDtypeStruct((chans, per), F32),
        scratch_shapes=[pltpu.VMEM((chans // 128, per, 128), F32)],
        compiler_params=PARAMS,
        name="turn_grads",
    )(keep, got)


def peers(n):
    return [0, 1, *range(2, n, 2), *range(3, n, 2)]


def near_peers(n):
    return [j for j in peers(n) if j < n - 2]


def swap(n, j, block):
    return resident(lax.ppermute(block, "ctx", [(i, i ^ j) for i in range(n)]))


def pack_kernel(*refs):
    for i, ref in enumerate(refs[:-1]):
        refs[-1][i] = ref[1]


def hand_over(n, got):
    packed = pl.pallas_call(
        pack_kernel,
        in_specs=[VMEM] * len(got),
        out_specs=VMEM,
        out_shape=pltpu.VMEM((len(got), *got[0].shape[1:]), BF16),
        compiler_params=PARAMS,
        name="pack",
    )(*got)
    return swap(n, 1, packed)


def after_kernel(*refs):
    pass


def after(arrived, blocks):
    count = len(arrived)
    return pl.pallas_call(
        after_kernel,
        in_specs=[VMEM] * (count + len(blocks)),
        out_specs=[VMEM] * len(blocks),
        out_shape=[pltpu.VMEM(b.shape, b.dtype) for b in blocks],
        input_output_aliases={count + i: i for i in range(len(blocks))},
        compiler_params=PARAMS,
        name="after",
    )(*arrived, *blocks)


def local(n, d, query_in, key_in, value_in, grad_out, filters, skip_gain):
    fwd, back = (resident(jnp.asarray(t)) for t in tables(filters.shape[1]))
    filters = resident(filters)
    gain = skip_gain[None, :]
    me = jnp.stack([lax.axis_index("ctx"), lax.axis_index("dp")]).astype(jnp.int32)

    arrays = [in_hbm(x[0]) for x in (key_in, value_in, query_in, grad_out)]
    (key, value, query, grad), first, second = products(n, me, *arrays)
    first = [first[0], *(swap(n, j, x) for j, x in zip(peers(n)[1:], first[1:]))]
    second = [second[0], *(swap(n, 2 * i, x) for i, x in enumerate(second[1:], 1))]
    spec = filter_spectra(filters, fwd, [])
    results = conv(n, d, 0, me, first, spec, fwd, back, [])
    second = after(results[:1], second)
    second = [*second, hand_over(n, second)]
    *mixed, keep, send = conv(n, d, 1, me, second, spec, fwd, back, results)
    near = [mixed[0], *(swap(n, j, x) for j, x in zip(near_peers(n)[1:], mixed[1:-1]))]
    far = swap(n, n - 2, mixed[-1])
    grad_filter = sum_grads(d, keep, send, near[2:4])
    passed = hand_over(n, [far])
    js = [*near_peers(n)[:-2], n - 2, n - 1]
    outs = gate(js, me, query, grad, value, key, gain, [*near[:-2], far, passed], [])
    outs = gate(near_peers(n)[-2:], me, query, grad, value, key, gain, near[-2:], outs)
    return *(x[None] for x in outs), grad_filter


def solution(mesh):
    rows = P("dp", "ctx", None)
    return jax.shard_map(
        functools.partial(local, mesh.shape["ctx"], mesh.shape["dp"]),
        mesh=mesh,
        in_specs=(rows, rows, rows, rows, P("ctx", None), P()),
        out_specs=(rows, rows, rows, rows, P("ctx", "dp")),
        check_vma=False,
    )
```

```python
import functools
import math

import jax
import jax.numpy as jnp
import ml_dtypes
import numpy as np
from jax import lax
from jax.experimental import pallas as pl
from jax.experimental.pallas import tpu as pltpu
from jax.sharding import PartitionSpec as P

F32 = jnp.float32
BF16 = jnp.bfloat16
CLASSES = 8
HALVES = 2
STEPS = 4
PARAMS = pltpu.CompilerParams(vmem_limit_bytes=16 * 1024 * 1024)
CONV_PARAMS = pltpu.CompilerParams(vmem_limit_bytes=34 * 1024 * 1024)
SMEM = pl.BlockSpec(memory_space=pltpu.SMEM)
VMEM = pl.BlockSpec(memory_space=pltpu.VMEM)
HBM = pl.BlockSpec(memory_space=pltpu.HBM)


def tables(length):
    m2 = length // CLASSES
    c = np.arange(CLASSES)[:, None, None]
    j = np.arange(m2)[None, :, None]
    m = np.arange(m2)[None, None, :]
    turn = ((CLASSES * m + c) * (2 * j + 1)) % (4 * length)
    angle = 2 * np.pi * turn / (4 * length)
    forward = np.concatenate([np.cos(angle), -np.sin(angle)], 1)
    back = np.swapaxes(forward, 1, 2) / length

    def parts(x):
        hi = x.astype(ml_dtypes.bfloat16)
        return hi, (x - hi.astype(np.float64)).astype(ml_dtypes.bfloat16)

    return np.concatenate(parts(forward), 2), back.astype(ml_dtypes.bfloat16)


def parts(x):
    hi = x.astype(BF16)
    return hi, (x - hi.astype(F32)).astype(BF16)


def dot(a, b):
    return jnp.dot(a, b, preferred_element_type=F32)


def dft(z, sign):
    n = len(z)
    if n == 1:
        return z
    even, odd = dft(z[0::2], sign), dft(z[1::2], sign)
    low, high = [], []
    for k in range(n // 2):
        (er, ei), (zr, zi) = even[k], odd[k]
        if k == 0:
            tr, ti = zr, zi
        elif 4 * k == n:
            tr, ti = (-zi, zr) if sign > 0 else (zi, -zr)
        else:
            c, s = math.cos(2 * math.pi * k / n), sign * math.sin(2 * math.pi * k / n)
            if 8 * k == n:
                tr, ti = (c * (zr - zi), c * (zi + zr)) if sign > 0 else (c * (zr + zi), c * (zi - zr))
            elif 8 * k == 3 * n:
                tr, ti = (c * (zr + zi), c * (zi - zr)) if sign > 0 else (c * (zr - zi), c * (zi + zr))
            else:
                tr, ti = c * zr - s * zi, c * zi + s * zr
        low.append((er + tr, ei + ti))
        high.append((er - tr, ei - ti))
    return low + high


def times(x, f, conj):
    (xr, xi), (fr, fi) = x, f
    if conj:
        return xr * fr + xi * fi, xi * fr - xr * fi
    return xr * fr - xi * fi, xr * fi + xi * fr


def resident(x):
    return pltpu.with_memory_space_constraint(x, pltpu.VMEM)


def in_hbm(x):
    return pltpu.with_memory_space_constraint(x, pltpu.HBM)


def peer_columns(me, j, width):
    return pl.ds(pl.multiple_of((me[0] ^ j) * width, 128), width)


def product_kernel(n, me, key, value, query, grad, *refs):
    bufs, outs, sems = refs[:4], refs[4:-1], refs[-1]
    _, rows, width = outs[0].shape
    width *= HALVES
    step = rows // STEPS
    copies = []
    for i in range(STEPS):
        at = pl.ds(i * step, step)
        copies.append(
            [
                pltpu.make_async_copy(src.at[at], dst.at[at], sems.at[a, i])
                for a, (src, dst) in enumerate(zip((key, value, query, grad), bufs))
            ]
        )
        for copy in copies[i]:
            copy.start()
    for s in range(STEPS):
        at = pl.ds(s * step, step)
        for a, (left, right) in enumerate((bufs[:2], bufs[2:])):
            copies[s][2 * a].wait()
            copies[s][2 * a + 1].wait()
            for i, j in enumerate(peers(n)):
                cols = peer_columns(me, j, width)
                value = (left[at, cols].astype(F32) * right[at, cols].astype(F32)).astype(BF16)
                for half in range(HALVES):
                    outs[half * n + i][a, at] = value[:, half * width // HALVES :][:, : width // HALVES]


def products(n, me, key, value, query, grad):
    rows, total = key.shape
    width = total // n // HALVES
    out = pl.pallas_call(
        functools.partial(product_kernel, n),
        in_specs=[SMEM] + [HBM] * 4,
        out_specs=[VMEM] * (4 + HALVES * n),
        out_shape=[pltpu.VMEM(key.shape, BF16)] * 4
        + [pltpu.VMEM((2, rows, width), BF16)] * (HALVES * n),
        scratch_shapes=[pltpu.SemaphoreType.DMA((4, STEPS))],
        compiler_params=PARAMS,
        name="products",
    )(me, key, value, query, grad)
    return out[:4], [out[4 + h * n : 4 + (h + 1) * n] for h in range(HALVES)]


def lane_groups(width):
    return [slice(i, i + 128) for i in range(0, width, 128)]


def filter_kernel(half, filt, fwd, *refs):
    spec, x, u = refs[-3:]
    m2, width = x.shape[1] // CLASSES, u.shape[-1]
    groups = lane_groups(width)
    rows = m2 // CLASSES
    for g, lanes in enumerate(groups):
        x[g] = filt[half * width + lanes.start : half * width + lanes.stop, :].T
    for c in range(CLASSES):
        for g, lanes in enumerate(groups):
            hi, lo = parts(x[g, pl.ds(c, m2, stride=CLASSES), :])
            u[c, :, lanes] = dot(fwd[c], jnp.concatenate([hi, hi], 0)) + dot(fwd[c, :, :m2], lo)

    def step(i, carry):
        r = pl.multiple_of(i * rows, rows)
        re, im = pl.ds(r, rows), pl.ds(m2 + r, rows)
        for lanes in groups:
            z = dft([(u[c, re, lanes], u[c, im, lanes]) for c in range(CLASSES)], -1)
            for k in range(CLASSES):
                spec[k, re, lanes], spec[k, im, lanes] = z[k]
        return carry

    lax.fori_loop(0, CLASSES, step, 0)


def filter_spectrum(half, filters, fwd, arrived):
    chans, length = filters.shape
    width = chans // HALVES
    m2 = length // CLASSES
    return pl.pallas_call(
        functools.partial(filter_kernel, half),
        in_specs=[VMEM] * (2 + len(arrived)),
        out_specs=VMEM,
        out_shape=pltpu.VMEM((CLASSES, 2 * m2, width), F32),
        scratch_shapes=[
            pltpu.VMEM((width // 128, length, 128), F32),
            pltpu.VMEM((CLASSES, 2 * m2, width), F32),
        ],
        compiler_params=PARAMS,
        name="filter_spectrum",
    )(filters, fwd, *arrived)


def conv_kernel(n, d, half, me, *refs):
    got, (filt, fwd, back) = refs[:n], refs[n : n + 3]
    refs = refs[-(n + 2 + 6) :]
    out, (keep, send), (nat, x, u, y, turned, grad) = refs[:n], refs[n : n + 2], refs[n + 2 :]
    _, rows, width = got[0].shape
    m2 = x.shape[2]
    per = keep.shape[1] // CLASSES
    groups = lane_groups(width)
    step_rows = m2 // CLASSES
    part_rows = rows // CLASSES
    chans = slice(half * width, (half + 1) * width)

    for a in range(2):
        for g, lanes in enumerate(groups):
            for i, j in enumerate(peers(n)):
                at = pl.multiple_of((me[0] ^ j) * rows, rows)
                nat[a, g, pl.ds(at, rows)] = got[i][a, :, lanes].astype(F32)
            for c in range(CLASSES):
                x[a, c, :, lanes] = nat[a, g, pl.ds(c, m2, stride=CLASSES), :].astype(BF16)
        for c in range(CLASSES):
            data = x[a, c]
            u[a, c] = dot(fwd[c], jnp.concatenate([data, data], 0))

    def middle(i, carry):
        r = pl.multiple_of(i * step_rows, step_rows)
        re, im = pl.ds(r, step_rows), pl.ds(m2 + r, step_rows)
        for lanes in groups:
            kv = dft([(u[0, c, re, lanes], u[0, c, im, lanes]) for c in range(CLASSES)], -1)
            wt = dft([(u[1, c, re, lanes], u[1, c, im, lanes]) for c in range(CLASSES)], -1)
            fs = [(filt[k, re, lanes], filt[k, im, lanes]) for k in range(CLASSES)]
            for o, (left, right, conj) in enumerate([(kv, fs, False), (wt, fs, True), (wt, kv, True)]):
                z = dft([times(s, t, conj) for s, t in zip(left, right)], 1)
                for c in range(CLASSES):
                    y[o, c, re, lanes] = z[c][0].astype(BF16)
                    y[o, c, im, lanes] = z[c][1].astype(BF16)
        return carry

    lax.fori_loop(0, CLASSES, middle, 0)

    for c in range(CLASSES):
        grad[c] = dot(back[c], y[2, c])
        for o in range(2):
            turned[o, c] = dot(back[c], y[o, c]).astype(BF16)
    for i, j in enumerate(peers(n)):
        at = pl.multiple_of((me[0] ^ j) * part_rows, part_rows)
        for o in range(2):
            for c in range(CLASSES):
                out[i][half, o, c * part_rows : (c + 1) * part_rows] = turned[o, c, pl.ds(at, part_rows)]
    for j in range(d):
        at = pl.multiple_of((me[1] ^ j) * per, per)
        for c in range(CLASSES):
            part = grad[c, pl.ds(at, per)]
            if j % 2:
                send[j // 2, c * per : (c + 1) * per, chans] = part.astype(BF16)
            else:
                keep[j // 2, c * per : (c + 1) * per, chans] = part


def conv(n, d, half, me, got, filt, fwd, back, before):
    _, rows, width = got[0].shape
    length = n * rows
    m2 = length // CLASSES
    out = pl.pallas_call(
        functools.partial(conv_kernel, n, d, half),
        in_specs=[SMEM] + [VMEM] * (n + 3 + len(before)),
        out_specs=[VMEM] * (n + 2),
        out_shape=[pltpu.VMEM((HALVES, 2, rows, width), BF16)] * n
        + [pltpu.VMEM((d // 2, length // d, HALVES * width), dtype) for dtype in (F32, BF16)],
        scratch_shapes=[
            pltpu.VMEM((2, width // 128, length, 128), F32),
            pltpu.VMEM((2, CLASSES, m2, width), BF16),
            pltpu.VMEM((2, CLASSES, 2 * m2, width), F32),
            pltpu.VMEM((3, CLASSES, 2 * m2, width), BF16),
            pltpu.VMEM((2, CLASSES, m2, width), BF16),
            pltpu.VMEM((CLASSES, m2, width), F32),
        ],
        input_output_aliases={n + 4 + i: i for i in range(len(before))},
        compiler_params=CONV_PARAMS,
        name="conv",
    )(me, *got, filt, fwd, back, *before)
    return out


def natural(scratch, piece):
    rows = piece.shape[0] // CLASSES
    for c in range(CLASSES):
        scratch[pl.ds(c, rows, stride=CLASSES), :] = piece[c * rows : (c + 1) * rows]
    return scratch[...]


def gate_kernel(js, me, query, grad, value, key, gain, *refs):
    got, outs, (sent, sems, nat) = refs[: len(js)], refs[-7:-3], refs[-3:]
    _, _, rows, width = got[0].shape
    copies = []
    for i, j in enumerate(js):
        block = peer_columns(me, j, HALVES * width)
        for half in range(HALVES):
            for g, lanes in enumerate(lane_groups(width)):
                at = half * width + lanes.start
                start = pl.multiple_of((me[0] ^ j) * HALVES * width + at, 128)
                cols = pl.ds(start, 128)
                to = slice(at, at + 128)
                scale = gain[:, cols]
                q, g_, v, k = (x[:, cols].astype(F32) for x in (query, grad, value, key))
                conv_out, corr_back = (
                    natural(nat.at[i, o, half, g], got[i][half, o, :, lanes].astype(F32)) for o in range(2)
                )
                mixing = conv_out + scale * (k * v).astype(BF16).astype(F32)
                sent[0, i, :, to] = (q * mixing).astype(BF16)
                sent[1, i, :, to] = (g_ * mixing).astype(BF16)
                total = corr_back + scale * (g_ * q).astype(BF16).astype(F32)
                sent[2, i, :, to] = (total * v).astype(BF16)
                sent[3, i, :, to] = (total * k).astype(BF16)
        for a in range(4):
            copy = pltpu.make_async_copy(sent.at[a, i], outs[a].at[:, block], sems.at[a, i])
            copy.start()
            copies.append(copy)
    for copy in copies:
        copy.wait()


def gate(js, me, query, grad, value, key, gain, got, outs):
    _, _, rows, width = got[0].shape
    return pl.pallas_call(
        functools.partial(gate_kernel, js),
        in_specs=[SMEM] + [VMEM] * (5 + len(got)) + [HBM] * len(outs),
        out_specs=[HBM] * 4,
        out_shape=[jax.ShapeDtypeStruct(query.shape, BF16)] * 4,
        scratch_shapes=[
            pltpu.VMEM((4, len(js), rows, HALVES * width), BF16),
            pltpu.SemaphoreType.DMA((4, len(js))),
            pltpu.VMEM((len(js), 2, HALVES, width // 128, rows, 128), F32),
        ],
        input_output_aliases={6 + len(got) + i: i for i in range(len(outs))},
        compiler_params=PARAMS,
        name="gate",
    )(me, query, grad, value, key, gain, *got, *outs)


def add_kernel(keep, got, new_keep, new_send):
    for i in range(new_keep.shape[0]):
        new_keep[i] = keep[2 * i] + got[2 * i].astype(F32)
        new_send[i] = (keep[2 * i + 1] + got[2 * i + 1].astype(F32)).astype(BF16)


def turn_kernel(keep, got, out, nat):
    for g, lanes in enumerate(lane_groups(keep.shape[2])):
        total = keep[0, :, lanes] + got[0, :, lanes].astype(F32)
        out[lanes, :] = natural(nat.at[g], total).T


def trade(d, bit, send):
    return resident(lax.ppermute(send, "dp", [(i, i ^ bit) for i in range(d)]))


def add_grads(keep, got):
    shape = (keep.shape[0] // 2, *keep.shape[1:])
    return pl.pallas_call(
        add_kernel,
        in_specs=[VMEM] * 2,
        out_specs=[VMEM] * 2,
        out_shape=[pltpu.VMEM(shape, F32), pltpu.VMEM(shape, BF16)],
        compiler_params=PARAMS,
        name="add_grads",
    )(keep, got)


def turn_grads(keep, got):
    _, per, chans = keep.shape
    return pl.pallas_call(
        turn_kernel,
        in_specs=[VMEM] * 2,
        out_specs=VMEM,
        out_shape=jax.ShapeDtypeStruct((chans, per), F32),
        scratch_shapes=[pltpu.VMEM((chans // 128, per, 128), F32)],
        compiler_params=PARAMS,
        name="turn_grads",
    )(keep, got)


def peers(n):
    return [0, 1, *range(2, n, 2), *range(3, n, 2)]


def exchange(n, js, blocks):
    return [
        resident(lax.ppermute(block, "ctx", [(i, i ^ j) for i in range(n)])) if j else block
        for j, block in zip(js, blocks)
    ]


def after_kernel(*refs):
    pass


def after(arrived, blocks):
    count = len(arrived)
    return pl.pallas_call(
        after_kernel,
        in_specs=[VMEM] * (count + len(blocks)),
        out_specs=[VMEM] * len(blocks),
        out_shape=[pltpu.VMEM(b.shape, b.dtype) for b in blocks],
        input_output_aliases={count + i: i for i in range(len(blocks))},
        compiler_params=PARAMS,
        name="after",
    )(*arrived, *blocks)


def local(n, d, query_in, key_in, value_in, grad_out, filters, skip_gain):
    fwd, back = (resident(jnp.asarray(t)) for t in tables(filters.shape[1]))
    filters = resident(filters)
    gain = skip_gain[None, :]
    me = jnp.stack([lax.axis_index("ctx"), lax.axis_index("dp")]).astype(jnp.int32)

    arrays = [in_hbm(x[0]) for x in (key_in, value_in, query_in, grad_out)]
    (key, value, query, grad), got = products(n, me, *arrays)
    js = peers(n)
    cut = n // 2
    first = exchange(n, js, got[0])
    spec = filter_spectrum(0, filters, fwd, first[1:3])
    second = exchange(n, js[:cut], after([spec], got[1][:cut]))
    spec_other = filter_spectrum(1, filters, fwd, [spec])
    second += exchange(n, js[cut:], after([spec_other], got[1][cut:]))
    results = conv(n, d, 0, me, first, spec, fwd, back, [])
    *mixed, keep, send = conv(n, d, 1, me, second, spec_other, fwd, back, results)

    bits = [1 << b for b in range(d.bit_length() - 1)]
    traded = trade(d, 1, send)
    early = exchange(n, js[:-1], mixed[:-1])
    for bit in bits[1:]:
        keep, send = add_grads(keep, traded)
        traded = trade(d, bit, send)
    grad_filter = turn_grads(keep, traded)
    mixed = early + exchange(n, js[-1:], after([keep], mixed[-1:]))

    outs = []
    early = n - 2
    for at in (slice(early), slice(early, n)):
        outs = gate(peers(n)[at], me, query, grad, value, key, gain, mixed[at], outs)
    return *(x[None] for x in outs), grad_filter


def solution(mesh):
    rows = P("dp", "ctx", None)
    return jax.shard_map(
        functools.partial(local, mesh.shape["ctx"], mesh.shape["dp"]),
        mesh=mesh,
        in_specs=(rows, rows, rows, rows, P("ctx", None), P()),
        out_specs=(rows, rows, rows, rows, P("ctx", "dp")),
        check_vma=False,
    )
```

```python
import functools
import math

import jax
import jax.numpy as jnp
import ml_dtypes
import numpy as np
from jax import lax
from jax.experimental import pallas as pl
from jax.experimental.pallas import tpu as pltpu
from jax.sharding import PartitionSpec as P

F32 = jnp.float32
BF16 = jnp.bfloat16
CLASSES = 8
HALVES = 2
STEPS = 4
PARAMS = pltpu.CompilerParams(vmem_limit_bytes=16 * 1024 * 1024)
CONV_PARAMS = pltpu.CompilerParams(vmem_limit_bytes=34 * 1024 * 1024)
SMEM = pl.BlockSpec(memory_space=pltpu.SMEM)
VMEM = pl.BlockSpec(memory_space=pltpu.VMEM)
HBM = pl.BlockSpec(memory_space=pltpu.HBM)


def tables(length):
    m2 = length // CLASSES
    c = np.arange(CLASSES)[:, None, None]
    j = np.arange(m2)[None, :, None]
    m = np.arange(m2)[None, None, :]
    turn = ((CLASSES * m + c) * (2 * j + 1)) % (4 * length)
    angle = 2 * np.pi * turn / (4 * length)
    forward = np.concatenate([np.cos(angle), -np.sin(angle)], 1)
    back = np.swapaxes(forward, 1, 2) / length

    def parts(x):
        hi = x.astype(ml_dtypes.bfloat16)
        return hi, (x - hi.astype(np.float64)).astype(ml_dtypes.bfloat16)

    return np.concatenate(parts(forward), 2), back.astype(ml_dtypes.bfloat16)


def parts(x):
    hi = x.astype(BF16)
    return hi, (x - hi.astype(F32)).astype(BF16)


def dot(a, b):
    return jnp.dot(a, b, preferred_element_type=F32)


def dft(z, sign):
    n = len(z)
    if n == 1:
        return z
    even, odd = dft(z[0::2], sign), dft(z[1::2], sign)
    low, high = [], []
    for k in range(n // 2):
        (er, ei), (zr, zi) = even[k], odd[k]
        if k == 0:
            tr, ti = zr, zi
        elif 4 * k == n:
            tr, ti = (-zi, zr) if sign > 0 else (zi, -zr)
        else:
            c, s = math.cos(2 * math.pi * k / n), sign * math.sin(2 * math.pi * k / n)
            if 8 * k == n:
                tr, ti = (c * (zr - zi), c * (zi + zr)) if sign > 0 else (c * (zr + zi), c * (zi - zr))
            elif 8 * k == 3 * n:
                tr, ti = (c * (zr + zi), c * (zi - zr)) if sign > 0 else (c * (zr - zi), c * (zi + zr))
            else:
                tr, ti = c * zr - s * zi, c * zi + s * zr
        low.append((er + tr, ei + ti))
        high.append((er - tr, ei - ti))
    return low + high


def times(x, f, conj):
    (xr, xi), (fr, fi) = x, f
    if conj:
        return xr * fr + xi * fi, xi * fr - xr * fi
    return xr * fr - xi * fi, xr * fi + xi * fr


def resident(x):
    return pltpu.with_memory_space_constraint(x, pltpu.VMEM)


def in_hbm(x):
    return pltpu.with_memory_space_constraint(x, pltpu.HBM)


def peer_columns(me, j, width):
    return pl.ds(pl.multiple_of((me[0] ^ j) * width, 128), width)


def product_kernel(n, me, key, value, query, grad, *refs):
    bufs, outs, sems = refs[:4], refs[4:-1], refs[-1]
    _, rows, width = outs[0].shape
    width *= HALVES
    step = rows // STEPS
    copies = []
    for i in range(STEPS):
        at = pl.ds(i * step, step)
        copies.append(
            [
                pltpu.make_async_copy(src.at[at], dst.at[at], sems.at[a, i])
                for a, (src, dst) in enumerate(zip((key, value, query, grad), bufs))
            ]
        )
        for copy in copies[i]:
            copy.start()
    for s in range(STEPS):
        at = pl.ds(s * step, step)
        for a, (left, right) in enumerate((bufs[:2], bufs[2:])):
            copies[s][2 * a].wait()
            copies[s][2 * a + 1].wait()
            for i, j in enumerate(peers(n)):
                cols = peer_columns(me, j, width)
                value = (left[at, cols].astype(F32) * right[at, cols].astype(F32)).astype(BF16)
                for half in range(HALVES):
                    outs[half * n + i][a, at] = value[:, half * width // HALVES :][:, : width // HALVES]


def products(n, me, key, value, query, grad):
    rows, total = key.shape
    width = total // n // HALVES
    out = pl.pallas_call(
        functools.partial(product_kernel, n),
        in_specs=[SMEM] + [HBM] * 4,
        out_specs=[VMEM] * (4 + HALVES * n),
        out_shape=[pltpu.VMEM(key.shape, BF16)] * 4
        + [pltpu.VMEM((2, rows, width), BF16)] * (HALVES * n),
        scratch_shapes=[pltpu.SemaphoreType.DMA((4, STEPS))],
        compiler_params=PARAMS,
        name="products",
    )(me, key, value, query, grad)
    return out[:4], [out[4 + h * n : 4 + (h + 1) * n] for h in range(HALVES)]


def lane_groups(width):
    return [slice(i, i + 128) for i in range(0, width, 128)]


def filter_kernel(half, filt, fwd, *refs):
    spec, x, u = refs[-3:]
    m2, width = x.shape[1] // CLASSES, u.shape[-1]
    groups = lane_groups(width)
    rows = m2 // CLASSES
    for g, lanes in enumerate(groups):
        x[g] = filt[half * width + lanes.start : half * width + lanes.stop, :].T
    for c in range(CLASSES):
        for g, lanes in enumerate(groups):
            hi, lo = parts(x[g, pl.ds(c, m2, stride=CLASSES), :])
            u[c, :, lanes] = dot(fwd[c], jnp.concatenate([hi, hi], 0)) + dot(fwd[c, :, :m2], lo)

    def step(i, carry):
        r = pl.multiple_of(i * rows, rows)
        re, im = pl.ds(r, rows), pl.ds(m2 + r, rows)
        for lanes in groups:
            z = dft([(u[c, re, lanes], u[c, im, lanes]) for c in range(CLASSES)], -1)
            for k in range(CLASSES):
                spec[k, re, lanes], spec[k, im, lanes] = z[k]
        return carry

    lax.fori_loop(0, CLASSES, step, 0)


def filter_spectrum(half, filters, fwd, arrived):
    chans, length = filters.shape
    width = chans // HALVES
    m2 = length // CLASSES
    return pl.pallas_call(
        functools.partial(filter_kernel, half),
        in_specs=[VMEM] * (2 + len(arrived)),
        out_specs=VMEM,
        out_shape=pltpu.VMEM((CLASSES, 2 * m2, width), F32),
        scratch_shapes=[
            pltpu.VMEM((width // 128, length, 128), F32),
            pltpu.VMEM((CLASSES, 2 * m2, width), F32),
        ],
        compiler_params=PARAMS,
        name="filter_spectrum",
    )(filters, fwd, *arrived)


def conv_kernel(n, d, half, me, *refs):
    got, (filt, fwd, back) = refs[:n], refs[n : n + 3]
    refs = refs[-(n + 2 + 6) :]
    out, (keep, send), (nat, x, u, y, turned, grad) = refs[:n], refs[n : n + 2], refs[n + 2 :]
    _, rows, width = got[0].shape
    m2 = x.shape[2]
    per = keep.shape[1] // CLASSES
    groups = lane_groups(width)
    step_rows = m2 // CLASSES
    part_rows = rows // CLASSES

    for a in range(2):
        for g, lanes in enumerate(groups):
            for i, j in enumerate(peers(n)):
                at = pl.multiple_of((me[0] ^ j) * rows, rows)
                nat[a, g, pl.ds(at, rows)] = got[i][a, :, lanes].astype(F32)
            for c in range(CLASSES):
                x[a, c, :, lanes] = nat[a, g, pl.ds(c, m2, stride=CLASSES), :].astype(BF16)
        for c in range(CLASSES):
            data = x[a, c]
            u[a, c] = dot(fwd[c], jnp.concatenate([data, data], 0))

    def middle(i, carry):
        r = pl.multiple_of(i * step_rows, step_rows)
        re, im = pl.ds(r, step_rows), pl.ds(m2 + r, step_rows)
        for lanes in groups:
            kv = dft([(u[0, c, re, lanes], u[0, c, im, lanes]) for c in range(CLASSES)], -1)
            wt = dft([(u[1, c, re, lanes], u[1, c, im, lanes]) for c in range(CLASSES)], -1)
            fs = [(filt[k, re, lanes], filt[k, im, lanes]) for k in range(CLASSES)]
            for o, (left, right, conj) in enumerate([(kv, fs, False), (wt, fs, True), (wt, kv, True)]):
                z = dft([times(s, t, conj) for s, t in zip(left, right)], 1)
                for c in range(CLASSES):
                    y[o, c, re, lanes] = z[c][0].astype(BF16)
                    y[o, c, im, lanes] = z[c][1].astype(BF16)
        return carry

    lax.fori_loop(0, CLASSES, middle, 0)

    for c in range(CLASSES):
        grad[c] = dot(back[c], y[2, c])
        for o in range(2):
            turned[o, c] = dot(back[c], y[o, c]).astype(BF16)
    for i, j in enumerate(peers(n)):
        at = pl.multiple_of((me[0] ^ j) * part_rows, part_rows)
        for o in range(2):
            for c in range(CLASSES):
                out[i][half, o, c * part_rows : (c + 1) * part_rows] = turned[o, c, pl.ds(at, part_rows)]
    for j in range(d):
        at = pl.multiple_of((me[1] ^ j) * per, per)
        for c in range(CLASSES):
            part = grad[c, pl.ds(at, per)]
            if j % 2:
                send[j // 2, c * per : (c + 1) * per] = part.astype(BF16)
            else:
                keep[j // 2, c * per : (c + 1) * per] = part


def conv(n, d, half, me, got, filt, fwd, back, before):
    _, rows, width = got[0].shape
    length = n * rows
    m2 = length // CLASSES
    out = pl.pallas_call(
        functools.partial(conv_kernel, n, d, half),
        in_specs=[SMEM] + [VMEM] * (n + 3 + len(before)),
        out_specs=[VMEM] * (n + 2),
        out_shape=[pltpu.VMEM((HALVES, 2, rows, width), BF16)] * n
        + [pltpu.VMEM((d // 2, length // d, width), dtype) for dtype in (F32, BF16)],
        scratch_shapes=[
            pltpu.VMEM((2, width // 128, length, 128), F32),
            pltpu.VMEM((2, CLASSES, m2, width), BF16),
            pltpu.VMEM((2, CLASSES, 2 * m2, width), F32),
            pltpu.VMEM((3, CLASSES, 2 * m2, width), BF16),
            pltpu.VMEM((2, CLASSES, m2, width), BF16),
            pltpu.VMEM((CLASSES, m2, width), F32),
        ],
        input_output_aliases={n + 4 + i: i for i in range(len(before))},
        compiler_params=CONV_PARAMS,
        name="conv",
    )(me, *got, filt, fwd, back, *before)
    return out


def natural(scratch, piece):
    rows = piece.shape[0] // CLASSES
    for c in range(CLASSES):
        scratch[pl.ds(c, rows, stride=CLASSES), :] = piece[c * rows : (c + 1) * rows]
    return scratch[...]


def gate_kernel(js, me, query, grad, value, key, gain, *refs):
    got, outs, token, (sent, sems, nat) = refs[: len(js)], refs[-8:-4], refs[-4], refs[-3:]
    token[...] = jnp.zeros_like(token)
    _, _, rows, width = got[0].shape
    copies = []
    for i, j in enumerate(js):
        block = peer_columns(me, j, HALVES * width)
        for half in range(HALVES):
            for g, lanes in enumerate(lane_groups(width)):
                at = half * width + lanes.start
                start = pl.multiple_of((me[0] ^ j) * HALVES * width + at, 128)
                cols = pl.ds(start, 128)
                to = slice(at, at + 128)
                scale = gain[:, cols]
                q, g_, v, k = (x[:, cols].astype(F32) for x in (query, grad, value, key))
                conv_out, corr_back = (
                    natural(nat.at[i, o, half, g], got[i][half, o, :, lanes].astype(F32)) for o in range(2)
                )
                mixing = conv_out + scale * (k * v).astype(BF16).astype(F32)
                sent[0, i, :, to] = (q * mixing).astype(BF16)
                sent[1, i, :, to] = (g_ * mixing).astype(BF16)
                total = corr_back + scale * (g_ * q).astype(BF16).astype(F32)
                sent[2, i, :, to] = (total * v).astype(BF16)
                sent[3, i, :, to] = (total * k).astype(BF16)
        for a in range(4):
            copy = pltpu.make_async_copy(sent.at[a, i], outs[a].at[:, block], sems.at[a, i])
            copy.start()
            copies.append(copy)
    for copy in copies:
        copy.wait()


def gate(js, me, query, grad, value, key, gain, got, outs):
    _, _, rows, width = got[0].shape
    return pl.pallas_call(
        functools.partial(gate_kernel, js),
        in_specs=[SMEM] + [VMEM] * (5 + len(got)) + [HBM] * len(outs),
        out_specs=[HBM] * 4 + [VMEM],
        out_shape=[jax.ShapeDtypeStruct(query.shape, BF16)] * 4 + [pltpu.VMEM((8, 128), F32)],
        scratch_shapes=[
            pltpu.VMEM((4, len(js), rows, HALVES * width), BF16),
            pltpu.SemaphoreType.DMA((4, len(js))),
            pltpu.VMEM((len(js), 2, HALVES, width // 128, rows, 128), F32),
        ],
        input_output_aliases={6 + len(got) + i: i for i in range(len(outs))},
        compiler_params=PARAMS,
        name="gate",
    )(me, query, grad, value, key, gain, *got, *outs)


def add_kernel(*refs):
    parts, (new_keep, new_send) = refs[:-2], refs[-2:]
    width = parts[0].shape[2]
    for h in range(len(parts) // 2):
        keep, got = parts[2 * h : 2 * h + 2]
        chans = slice(h * width, (h + 1) * width)
        for i in range(new_keep.shape[0]):
            new_keep[i, :, chans] = keep[2 * i] + got[2 * i].astype(F32)
            new_send[i, :, chans] = (keep[2 * i + 1] + got[2 * i + 1].astype(F32)).astype(BF16)


def turn_kernel(keep, got, out, nat):
    for g, lanes in enumerate(lane_groups(keep.shape[2])):
        total = keep[0, :, lanes] + got[0, :, lanes].astype(F32)
        out[lanes, :] = natural(nat.at[g], total).T


def trade(d, bit, send):
    return resident(lax.ppermute(send, "dp", [(i, i ^ bit) for i in range(d)]))


def add_grads(*parts):
    count, per, width = parts[0].shape
    shape = (count // 2, per, width * len(parts) // 2)
    return pl.pallas_call(
        add_kernel,
        in_specs=[VMEM] * len(parts),
        out_specs=[VMEM] * 2,
        out_shape=[pltpu.VMEM(shape, F32), pltpu.VMEM(shape, BF16)],
        compiler_params=PARAMS,
        name="add_grads",
    )(*parts)


def turn_grads(keep, got):
    _, per, chans = keep.shape
    return pl.pallas_call(
        turn_kernel,
        in_specs=[VMEM] * 2,
        out_specs=VMEM,
        out_shape=jax.ShapeDtypeStruct((chans, per), F32),
        scratch_shapes=[pltpu.VMEM((chans // 128, per, 128), F32)],
        compiler_params=PARAMS,
        name="turn_grads",
    )(keep, got)


def peers(n):
    return [0, n - 2, 1, *range(2, n - 2, 2), *range(3, n, 2)]


def exchange(n, js, blocks):
    return [
        resident(lax.ppermute(block, "ctx", [(i, i ^ j) for i in range(n)])) if j else block
        for j, block in zip(js, blocks)
    ]


def after_kernel(*refs):
    pass


def after(arrived, blocks):
    count = len(arrived)
    return pl.pallas_call(
        after_kernel,
        in_specs=[VMEM] * (count + len(blocks)),
        out_specs=[VMEM] * len(blocks),
        out_shape=[pltpu.VMEM(b.shape, b.dtype) for b in blocks],
        input_output_aliases={count + i: i for i in range(len(blocks))},
        compiler_params=PARAMS,
        name="after",
    )(*arrived, *blocks)


def local(n, d, query_in, key_in, value_in, grad_out, filters, skip_gain):
    fwd, back = (resident(jnp.asarray(t)) for t in tables(filters.shape[1]))
    filters = resident(filters)
    gain = skip_gain[None, :]
    me = jnp.stack([lax.axis_index("ctx"), lax.axis_index("dp")]).astype(jnp.int32)

    arrays = [in_hbm(x[0]) for x in (key_in, value_in, query_in, grad_out)]
    (key, value, query, grad), got = products(n, me, *arrays)
    js = peers(n)
    cut = n // 2
    first = exchange(n, js, got[0])
    spec = filter_spectrum(0, filters, fwd, first[1:3])
    second = exchange(n, js[:cut], after([spec], got[1][:cut]))
    spec_other = filter_spectrum(1, filters, fwd, [spec])
    second += exchange(n, js[cut:], after([spec_other], got[1][cut:]))
    *mixed, keep, send = conv(n, d, 0, me, first, spec, fwd, back, [])
    traded = trade(d, 1, send)
    *mixed, keep_other, send = conv(n, d, 1, me, second, spec_other, fwd, back, mixed)

    bits = [1 << b for b in range(d.bit_length() - 1)]
    parts_ = keep, traded, keep_other, trade(d, 1, send)
    early = exchange(n, js[:-1], mixed[:-1])
    for bit in bits[1:]:
        keep, send = add_grads(*parts_)
        parts_ = keep, trade(d, bit, send)
    mixed = early + exchange(n, js[-1:], after([keep], mixed[-1:]))

    outs = []
    early = n - 2
    for at in (slice(early), slice(early, n)):
        *outs, gated = gate(peers(n)[at], me, query, grad, value, key, gain, mixed[at], outs)
    grad_filter = turn_grads(*parts_)
    return *(x[None] for x in outs), grad_filter


def solution(mesh):
    rows = P("dp", "ctx", None)
    return jax.shard_map(
        functools.partial(local, mesh.shape["ctx"], mesh.shape["dp"]),
        mesh=mesh,
        in_specs=(rows, rows, rows, rows, P("ctx", None), P()),
        out_specs=(rows, rows, rows, rows, P("ctx", "dp")),
        check_vma=False,
    )
```

```python
import functools
import math

import jax
import jax.numpy as jnp
import ml_dtypes
import numpy as np
from jax import lax
from jax.experimental import pallas as pl
from jax.experimental.pallas import tpu as pltpu
from jax.sharding import PartitionSpec as P

F32 = jnp.float32
BF16 = jnp.bfloat16
CLASSES = 8
HALVES = 2
STEPS = 4
PARAMS = pltpu.CompilerParams(vmem_limit_bytes=16 * 1024 * 1024)
CONV_PARAMS = pltpu.CompilerParams(vmem_limit_bytes=34 * 1024 * 1024)
SMEM = pl.BlockSpec(memory_space=pltpu.SMEM)
VMEM = pl.BlockSpec(memory_space=pltpu.VMEM)
HBM = pl.BlockSpec(memory_space=pltpu.HBM)


def tables(length):
    m2 = length // CLASSES
    c = np.arange(CLASSES)[:, None, None]
    j = np.arange(m2)[None, :, None]
    m = np.arange(m2)[None, None, :]
    turn = ((CLASSES * m + c) * (2 * j + 1)) % (4 * length)
    angle = 2 * np.pi * turn / (4 * length)
    forward = np.concatenate([np.cos(angle), -np.sin(angle)], 1)
    back = np.swapaxes(forward, 1, 2) / length

    def parts(x):
        hi = x.astype(ml_dtypes.bfloat16)
        return hi, (x - hi.astype(np.float64)).astype(ml_dtypes.bfloat16)

    return np.concatenate(parts(forward), 2), back.astype(ml_dtypes.bfloat16)


def parts(x):
    hi = x.astype(BF16)
    return hi, (x - hi.astype(F32)).astype(BF16)


def dot(a, b):
    return jnp.dot(a, b, preferred_element_type=F32)


def dft(z, sign):
    n = len(z)
    if n == 1:
        return z
    even, odd = dft(z[0::2], sign), dft(z[1::2], sign)
    low, high = [], []
    for k in range(n // 2):
        (er, ei), (zr, zi) = even[k], odd[k]
        if k == 0:
            tr, ti = zr, zi
        elif 4 * k == n:
            tr, ti = (-zi, zr) if sign > 0 else (zi, -zr)
        else:
            c, s = math.cos(2 * math.pi * k / n), sign * math.sin(2 * math.pi * k / n)
            if 8 * k == n:
                tr, ti = (c * (zr - zi), c * (zi + zr)) if sign > 0 else (c * (zr + zi), c * (zi - zr))
            elif 8 * k == 3 * n:
                tr, ti = (c * (zr + zi), c * (zi - zr)) if sign > 0 else (c * (zr - zi), c * (zi + zr))
            else:
                tr, ti = c * zr - s * zi, c * zi + s * zr
        low.append((er + tr, ei + ti))
        high.append((er - tr, ei - ti))
    return low + high


def times(x, f, conj):
    (xr, xi), (fr, fi) = x, f
    if conj:
        return xr * fr + xi * fi, xi * fr - xr * fi
    return xr * fr - xi * fi, xr * fi + xi * fr


def resident(x):
    return pltpu.with_memory_space_constraint(x, pltpu.VMEM)


def in_hbm(x):
    return pltpu.with_memory_space_constraint(x, pltpu.HBM)


def peer_columns(me, j, width):
    return pl.ds(pl.multiple_of((me[0] ^ j) * width, 128), width)


def product_kernel(n, me, key, value, query, grad, *refs):
    bufs, outs, sems = refs[:4], refs[4:-1], refs[-1]
    _, rows, width = outs[0].shape
    width *= HALVES
    step = rows // STEPS
    copies = []
    for i in range(STEPS):
        at = pl.ds(i * step, step)
        copies.append(
            [
                pltpu.make_async_copy(src.at[at], dst.at[at], sems.at[a, i])
                for a, (src, dst) in enumerate(zip((key, value, query, grad), bufs))
            ]
        )
        for copy in copies[i]:
            copy.start()
    for s in range(STEPS):
        at = pl.ds(s * step, step)
        for a, (left, right) in enumerate((bufs[:2], bufs[2:])):
            copies[s][2 * a].wait()
            copies[s][2 * a + 1].wait()
            for i, j in enumerate(peers(n)):
                cols = peer_columns(me, j, width)
                value = (left[at, cols].astype(F32) * right[at, cols].astype(F32)).astype(BF16)
                for half in range(HALVES):
                    outs[half * n + i][a, at] = value[:, half * width // HALVES :][:, : width // HALVES]


def products(n, me, key, value, query, grad):
    rows, total = key.shape
    width = total // n // HALVES
    out = pl.pallas_call(
        functools.partial(product_kernel, n),
        in_specs=[SMEM] + [HBM] * 4,
        out_specs=[VMEM] * (4 + HALVES * n),
        out_shape=[pltpu.VMEM(key.shape, BF16)] * 4
        + [pltpu.VMEM((2, rows, width), BF16)] * (HALVES * n),
        scratch_shapes=[pltpu.SemaphoreType.DMA((4, STEPS))],
        compiler_params=PARAMS,
        name="products",
    )(me, key, value, query, grad)
    return out[:4], [out[4 + h * n : 4 + (h + 1) * n] for h in range(HALVES)]


def lane_groups(width):
    return [slice(i, i + 128) for i in range(0, width, 128)]


def filter_kernel(half, filt, fwd, *refs):
    spec, x, u = refs[-3:]
    m2, width = x.shape[1] // CLASSES, u.shape[-1]
    groups = lane_groups(width)
    rows = m2 // CLASSES
    for g, lanes in enumerate(groups):
        x[g] = filt[half * width + lanes.start : half * width + lanes.stop, :].T
    for c in range(CLASSES):
        for g, lanes in enumerate(groups):
            hi, lo = parts(x[g, pl.ds(c, m2, stride=CLASSES), :])
            u[c, :, lanes] = dot(fwd[c], jnp.concatenate([hi, hi], 0)) + dot(fwd[c, :, :m2], lo)

    def step(i, carry):
        r = pl.multiple_of(i * rows, rows)
        re, im = pl.ds(r, rows), pl.ds(m2 + r, rows)
        for lanes in groups:
            z = dft([(u[c, re, lanes], u[c, im, lanes]) for c in range(CLASSES)], -1)
            for k in range(CLASSES):
                spec[k, re, lanes], spec[k, im, lanes] = z[k]
        return carry

    lax.fori_loop(0, CLASSES, step, 0)


def filter_spectrum(half, filters, fwd, arrived):
    chans, length = filters.shape
    width = chans // HALVES
    m2 = length // CLASSES
    return pl.pallas_call(
        functools.partial(filter_kernel, half),
        in_specs=[VMEM] * (2 + len(arrived)),
        out_specs=VMEM,
        out_shape=pltpu.VMEM((CLASSES, 2 * m2, width), F32),
        scratch_shapes=[
            pltpu.VMEM((width // 128, length, 128), F32),
            pltpu.VMEM((CLASSES, 2 * m2, width), F32),
        ],
        compiler_params=PARAMS,
        name="filter_spectrum",
    )(filters, fwd, *arrived)


def conv_kernel(n, d, half, me, *refs):
    got, (filt, fwd, back) = refs[:n], refs[n : n + 3]
    refs = refs[-(n + 2 + 6) :]
    out, (keep, send), (nat, x, u, y, turned, grad) = refs[:n], refs[n : n + 2], refs[n + 2 :]
    _, rows, width = got[0].shape
    m2 = x.shape[2]
    per = keep.shape[1] // CLASSES
    groups = lane_groups(width)
    step_rows = m2 // CLASSES
    part_rows = rows // CLASSES

    for a in range(2):
        for g, lanes in enumerate(groups):
            for i, j in enumerate(peers(n)):
                at = pl.multiple_of((me[0] ^ j) * rows, rows)
                nat[a, g, pl.ds(at, rows)] = got[i][a, :, lanes].astype(F32)
            for c in range(CLASSES):
                x[a, c, :, lanes] = nat[a, g, pl.ds(c, m2, stride=CLASSES), :].astype(BF16)
        for c in range(CLASSES):
            data = x[a, c]
            u[a, c] = dot(fwd[c], jnp.concatenate([data, data], 0))

    def middle(i, carry):
        r = pl.multiple_of(i * step_rows, step_rows)
        re, im = pl.ds(r, step_rows), pl.ds(m2 + r, step_rows)
        for lanes in groups:
            kv = dft([(u[0, c, re, lanes], u[0, c, im, lanes]) for c in range(CLASSES)], -1)
            wt = dft([(u[1, c, re, lanes], u[1, c, im, lanes]) for c in range(CLASSES)], -1)
            fs = [(filt[k, re, lanes], filt[k, im, lanes]) for k in range(CLASSES)]
            for o, (left, right, conj) in enumerate([(kv, fs, False), (wt, fs, True), (wt, kv, True)]):
                z = dft([times(s, t, conj) for s, t in zip(left, right)], 1)
                for c in range(CLASSES):
                    y[o, c, re, lanes] = z[c][0].astype(BF16)
                    y[o, c, im, lanes] = z[c][1].astype(BF16)
        return carry

    lax.fori_loop(0, CLASSES, middle, 0)

    for c in range(CLASSES):
        grad[c] = dot(back[c], y[2, c])
        for o in range(2):
            turned[o, c] = dot(back[c], y[o, c]).astype(BF16)
    for i, j in enumerate(back_peers(n)):
        at = pl.multiple_of((me[0] ^ j) * part_rows, part_rows)
        for o in range(2):
            for c in range(CLASSES):
                out[i][half, o, c * part_rows : (c + 1) * part_rows] = turned[o, c, pl.ds(at, part_rows)]
    for j in range(d):
        at = pl.multiple_of((me[1] ^ j) * per, per)
        for c in range(CLASSES):
            part = grad[c, pl.ds(at, per)]
            if j % 2:
                send[j // 2, c * per : (c + 1) * per] = part.astype(BF16)
            else:
                keep[j // 2, c * per : (c + 1) * per] = part


def conv(n, d, half, me, got, filt, fwd, back, before):
    _, rows, width = got[0].shape
    length = n * rows
    m2 = length // CLASSES
    out = pl.pallas_call(
        functools.partial(conv_kernel, n, d, half),
        in_specs=[SMEM] + [VMEM] * (n + 3 + len(before)),
        out_specs=[VMEM] * (n + 2),
        out_shape=[pltpu.VMEM((HALVES, 2, rows, width), BF16)] * n
        + [pltpu.VMEM((d // 2, length // d, width), dtype) for dtype in (F32, BF16)],
        scratch_shapes=[
            pltpu.VMEM((2, width // 128, length, 128), F32),
            pltpu.VMEM((2, CLASSES, m2, width), BF16),
            pltpu.VMEM((2, CLASSES, 2 * m2, width), F32),
            pltpu.VMEM((3, CLASSES, 2 * m2, width), BF16),
            pltpu.VMEM((2, CLASSES, m2, width), BF16),
            pltpu.VMEM((CLASSES, m2, width), F32),
        ],
        input_output_aliases={n + 4 + i: i for i in range(len(before))},
        compiler_params=CONV_PARAMS,
        name="conv",
    )(me, *got, filt, fwd, back, *before)
    return out


def natural(scratch, piece):
    rows = piece.shape[0] // CLASSES
    for c in range(CLASSES):
        scratch[pl.ds(c, rows, stride=CLASSES), :] = piece[c * rows : (c + 1) * rows]
    return scratch[...]


def gate_kernel(js, me, query, grad, value, key, gain, *refs):
    got, outs, token, (sent, sems, nat) = refs[: len(js)], refs[-8:-4], refs[-4], refs[-3:]
    token[...] = jnp.zeros_like(token)
    _, _, rows, width = got[0].shape
    copies = []
    for i, j in enumerate(js):
        block = peer_columns(me, j, HALVES * width)
        for half in range(HALVES):
            for g, lanes in enumerate(lane_groups(width)):
                at = half * width + lanes.start
                start = pl.multiple_of((me[0] ^ j) * HALVES * width + at, 128)
                cols = pl.ds(start, 128)
                to = slice(at, at + 128)
                scale = gain[:, cols]
                q, g_, v, k = (x[:, cols].astype(F32) for x in (query, grad, value, key))
                conv_out, corr_back = (
                    natural(nat.at[i, o, half, g], got[i][half, o, :, lanes].astype(F32)) for o in range(2)
                )
                mixing = conv_out + scale * (k * v).astype(BF16).astype(F32)
                sent[0, i, :, to] = (q * mixing).astype(BF16)
                sent[1, i, :, to] = (g_ * mixing).astype(BF16)
                total = corr_back + scale * (g_ * q).astype(BF16).astype(F32)
                sent[2, i, :, to] = (total * v).astype(BF16)
                sent[3, i, :, to] = (total * k).astype(BF16)
        for a in range(4):
            copy = pltpu.make_async_copy(sent.at[a, i], outs[a].at[:, block], sems.at[a, i])
            copy.start()
            copies.append(copy)
    for copy in copies:
        copy.wait()


def gate(js, me, query, grad, value, key, gain, got, outs):
    _, _, rows, width = got[0].shape
    return pl.pallas_call(
        functools.partial(gate_kernel, js),
        in_specs=[SMEM] + [VMEM] * (5 + len(got)) + [HBM] * len(outs),
        out_specs=[HBM] * 4 + [VMEM],
        out_shape=[jax.ShapeDtypeStruct(query.shape, BF16)] * 4 + [pltpu.VMEM((8, 128), F32)],
        scratch_shapes=[
            pltpu.VMEM((4, len(js), rows, HALVES * width), BF16),
            pltpu.SemaphoreType.DMA((4, len(js))),
            pltpu.VMEM((len(js), 2, HALVES, width // 128, rows, 128), F32),
        ],
        input_output_aliases={6 + len(got) + i: i for i in range(len(outs))},
        compiler_params=PARAMS,
        name="gate",
    )(me, query, grad, value, key, gain, *got, *outs)


def add_kernel(*refs):
    parts, (new_keep, new_send) = refs[:-2], refs[-2:]
    width = parts[0].shape[2]
    for h in range(len(parts) // 2):
        keep, got = parts[2 * h : 2 * h + 2]
        chans = slice(h * width, (h + 1) * width)
        for i in range(new_keep.shape[0]):
            new_keep[i, :, chans] = keep[2 * i] + got[2 * i].astype(F32)
            new_send[i, :, chans] = (keep[2 * i + 1] + got[2 * i + 1].astype(F32)).astype(BF16)


def turn_kernel(keep, got, out, nat):
    for g, lanes in enumerate(lane_groups(keep.shape[2])):
        total = keep[0, :, lanes] + got[0, :, lanes].astype(F32)
        out[lanes, :] = natural(nat.at[g], total).T


def trade(d, bit, send):
    return resident(lax.ppermute(send, "dp", [(i, i ^ bit) for i in range(d)]))


def add_grads(*parts):
    count, per, width = parts[0].shape
    shape = (count // 2, per, width * len(parts) // 2)
    return pl.pallas_call(
        add_kernel,
        in_specs=[VMEM] * len(parts),
        out_specs=[VMEM] * 2,
        out_shape=[pltpu.VMEM(shape, F32), pltpu.VMEM(shape, BF16)],
        compiler_params=PARAMS,
        name="add_grads",
    )(*parts)


def turn_grads(keep, got):
    _, per, chans = keep.shape
    return pl.pallas_call(
        turn_kernel,
        in_specs=[VMEM] * 2,
        out_specs=VMEM,
        out_shape=jax.ShapeDtypeStruct((chans, per), F32),
        scratch_shapes=[pltpu.VMEM((chans // 128, per, 128), F32)],
        compiler_params=PARAMS,
        name="turn_grads",
    )(keep, got)


def peers(n):
    return [0, 1, *range(2, n, 2), *range(3, n, 2)]


def back_peers(n):
    return [0, n - 2, 1, *range(2, n - 2, 2), *range(3, n, 2)]


def exchange(n, js, blocks):
    return [
        resident(lax.ppermute(block, "ctx", [(i, i ^ j) for i in range(n)])) if j else block
        for j, block in zip(js, blocks)
    ]


def after_kernel(*refs):
    pass


def after(arrived, blocks):
    count = len(arrived)
    return pl.pallas_call(
        after_kernel,
        in_specs=[VMEM] * (count + len(blocks)),
        out_specs=[VMEM] * len(blocks),
        out_shape=[pltpu.VMEM(b.shape, b.dtype) for b in blocks],
        input_output_aliases={count + i: i for i in range(len(blocks))},
        compiler_params=PARAMS,
        name="after",
    )(*arrived, *blocks)


def local(n, d, query_in, key_in, value_in, grad_out, filters, skip_gain):
    fwd, back = (resident(jnp.asarray(t)) for t in tables(filters.shape[1]))
    filters = resident(filters)
    gain = skip_gain[None, :]
    me = jnp.stack([lax.axis_index("ctx"), lax.axis_index("dp")]).astype(jnp.int32)

    arrays = [in_hbm(x[0]) for x in (key_in, value_in, query_in, grad_out)]
    (key, value, query, grad), got = products(n, me, *arrays)
    js = peers(n)
    cut = n // 2
    first = exchange(n, js, got[0])
    spec = filter_spectrum(0, filters, fwd, first[1:3])
    second = exchange(n, js[:cut], after([spec], got[1][:cut]))
    spec_other = filter_spectrum(1, filters, fwd, [spec])
    second += exchange(n, js[cut:], after([spec_other], got[1][cut:]))
    *mixed, keep, send = conv(n, d, 0, me, first, spec, fwd, back, [])
    traded = trade(d, 1, send)
    *mixed, keep_other, send = conv(n, d, 1, me, second, spec_other, fwd, back, mixed)

    bits = [1 << b for b in range(d.bit_length() - 1)]
    parts_ = keep, traded, keep_other, trade(d, 1, send)
    js = back_peers(n)
    mixed = exchange(n, js, mixed)
    for bit in bits[1:]:
        keep, send = add_grads(*parts_)
        parts_ = keep, trade(d, bit, send)

    outs = []
    early = n - 2
    for at in (slice(early), slice(early, n)):
        *outs, _ = gate(js[at], me, query, grad, value, key, gain, mixed[at], outs)
    grad_filter = turn_grads(*parts_)
    return *(x[None] for x in outs), grad_filter


def solution(mesh):
    rows = P("dp", "ctx", None)
    return jax.shard_map(
        functools.partial(local, mesh.shape["ctx"], mesh.shape["dp"]),
        mesh=mesh,
        in_specs=(rows, rows, rows, rows, P("ctx", None), P()),
        out_specs=(rows, rows, rows, rows, P("ctx", "dp")),
        check_vma=False,
    )
```

```python
import functools
import math

import jax
import jax.numpy as jnp
import ml_dtypes
import numpy as np
from jax import lax
from jax.experimental import pallas as pl
from jax.experimental.pallas import tpu as pltpu
from jax.sharding import PartitionSpec as P

F32 = jnp.float32
BF16 = jnp.bfloat16
CLASSES = 8
HALVES = 2
PARAMS = pltpu.CompilerParams(vmem_limit_bytes=16 * 1024 * 1024)
CONV_PARAMS = pltpu.CompilerParams(vmem_limit_bytes=34 * 1024 * 1024)
SMEM = pl.BlockSpec(memory_space=pltpu.SMEM)
VMEM = pl.BlockSpec(memory_space=pltpu.VMEM)
HBM = pl.BlockSpec(memory_space=pltpu.HBM)


def tables(length):
    m2 = length // CLASSES
    c = np.arange(CLASSES)[:, None, None]
    j = np.arange(m2)[None, :, None]
    m = np.arange(m2)[None, None, :]
    turn = ((CLASSES * m + c) * (2 * j + 1)) % (4 * length)
    angle = 2 * np.pi * turn / (4 * length)
    forward = np.concatenate([np.cos(angle), -np.sin(angle)], 1)
    back = np.swapaxes(forward, 1, 2) / length

    def parts(x):
        hi = x.astype(ml_dtypes.bfloat16)
        return hi, (x - hi.astype(np.float64)).astype(ml_dtypes.bfloat16)

    return np.concatenate(parts(forward), 2), back.astype(ml_dtypes.bfloat16)


def parts(x):
    hi = x.astype(BF16)
    return hi, (x - hi.astype(F32)).astype(BF16)


def dot(a, b):
    return jnp.dot(a, b, preferred_element_type=F32)


def dft(z, sign):
    n = len(z)
    if n == 1:
        return z
    even, odd = dft(z[0::2], sign), dft(z[1::2], sign)
    low, high = [], []
    for k in range(n // 2):
        (er, ei), (zr, zi) = even[k], odd[k]
        if k == 0:
            tr, ti = zr, zi
        elif 4 * k == n:
            tr, ti = (-zi, zr) if sign > 0 else (zi, -zr)
        else:
            c, s = math.cos(2 * math.pi * k / n), sign * math.sin(2 * math.pi * k / n)
            if 8 * k == n:
                tr, ti = (c * (zr - zi), c * (zi + zr)) if sign > 0 else (c * (zr + zi), c * (zi - zr))
            elif 8 * k == 3 * n:
                tr, ti = (c * (zr + zi), c * (zi - zr)) if sign > 0 else (c * (zr - zi), c * (zi + zr))
            else:
                tr, ti = c * zr - s * zi, c * zi + s * zr
        low.append((er + tr, ei + ti))
        high.append((er - tr, ei - ti))
    return low + high


def times(x, f, conj):
    (xr, xi), (fr, fi) = x, f
    if conj:
        return xr * fr + xi * fi, xi * fr - xr * fi
    return xr * fr - xi * fi, xr * fi + xi * fr


def resident(x):
    return pltpu.with_memory_space_constraint(x, pltpu.VMEM)


def in_hbm(x):
    return pltpu.with_memory_space_constraint(x, pltpu.HBM)


def peer_columns(me, j, width):
    return pl.ds(pl.multiple_of((me[0] ^ j) * width, 128), width)


def half_columns(me, j, half, width):
    return pl.ds(pl.multiple_of((HALVES * (me[0] ^ j) + half) * width, 128), width)


def first_kernel(n, me, key, value, query, grad, *refs):
    outs, (bufs, sems) = refs[:n], refs[n:]
    width = outs[0].shape[2]
    copies = []
    for i, j in enumerate(peers(n)):
        cols = half_columns(me, j, 0, width)
        copies.append(
            [
                pltpu.make_async_copy(src.at[:, cols], bufs.at[a, i], sems.at[a, i])
                for a, src in enumerate((key, value, query, grad))
            ]
        )
        for copy in copies[i]:
            copy.start()
    for i, out in enumerate(outs):
        for copy in copies[i]:
            copy.wait()
        for a in range(2):
            left, right = bufs[2 * a, i].astype(F32), bufs[2 * a + 1, i].astype(F32)
            out[a] = (left * right).astype(BF16)


def second_kernel(n, me, key, value, query, grad, *refs):
    outs = refs[-n:]
    width = outs[0].shape[2]
    for out, j in zip(outs, peers(n)):
        cols = half_columns(me, j, 1, width)
        for a, (left, right) in enumerate(((key, value), (query, grad))):
            out[a] = (left[:, cols].astype(F32) * right[:, cols].astype(F32)).astype(BF16)


def products(half, n, me, arrays, arrived):
    rows, total = arrays[0].shape
    width = total // n // HALVES
    scratch = [pltpu.VMEM((4, n, rows, width), BF16), pltpu.SemaphoreType.DMA((4, n))]
    return pl.pallas_call(
        functools.partial(second_kernel if half else first_kernel, n),
        in_specs=[SMEM] + [VMEM if half else HBM] * 4 + [VMEM] * len(arrived),
        out_specs=[VMEM] * n,
        out_shape=[pltpu.VMEM((2, rows, width), BF16)] * n,
        scratch_shapes=[] if half else scratch,
        compiler_params=PARAMS,
        name="products",
    )(me, *arrays, *arrived)


def lane_groups(width):
    return [slice(i, i + 128) for i in range(0, width, 128)]


def filter_kernel(half, filt, fwd, *refs):
    spec, x, u = refs[-3:]
    m2, width = x.shape[1] // CLASSES, u.shape[-1]
    groups = lane_groups(width)
    rows = m2 // CLASSES
    for g, lanes in enumerate(groups):
        x[g] = filt[half * width + lanes.start : half * width + lanes.stop, :].T
    for c in range(CLASSES):
        for g, lanes in enumerate(groups):
            hi, lo = parts(x[g, pl.ds(c, m2, stride=CLASSES), :])
            u[c, :, lanes] = dot(fwd[c], jnp.concatenate([hi, hi], 0)) + dot(fwd[c, :, :m2], lo)

    def step(i, carry):
        r = pl.multiple_of(i * rows, rows)
        re, im = pl.ds(r, rows), pl.ds(m2 + r, rows)
        for lanes in groups:
            z = dft([(u[c, re, lanes], u[c, im, lanes]) for c in range(CLASSES)], -1)
            for k in range(CLASSES):
                spec[k, re, lanes], spec[k, im, lanes] = z[k]
        return carry

    lax.fori_loop(0, CLASSES, step, 0)


def filter_spectrum(half, filters, fwd, arrived):
    chans, length = filters.shape
    width = chans // HALVES
    m2 = length // CLASSES
    return pl.pallas_call(
        functools.partial(filter_kernel, half),
        in_specs=[VMEM] * (2 + len(arrived)),
        out_specs=VMEM,
        out_shape=pltpu.VMEM((CLASSES, 2 * m2, width), F32),
        scratch_shapes=[
            pltpu.VMEM((width // 128, length, 128), F32),
            pltpu.VMEM((CLASSES, 2 * m2, width), F32),
        ],
        compiler_params=PARAMS,
        name="filter_spectrum",
    )(filters, fwd, *arrived)


def conv_kernel(n, d, half, me, *refs):
    got, (filt, fwd, back) = refs[:n], refs[n : n + 3]
    refs = refs[-(n + 2 + 6) :]
    out, (keep, send), (nat, x, u, y, turned, grad) = refs[:n], refs[n : n + 2], refs[n + 2 :]
    _, rows, width = got[0].shape
    m2 = x.shape[2]
    per = keep.shape[1] // CLASSES
    groups = lane_groups(width)
    step_rows = m2 // CLASSES
    part_rows = rows // CLASSES

    for a in range(2):
        for g, lanes in enumerate(groups):
            for i, j in enumerate(peers(n)):
                at = pl.multiple_of((me[0] ^ j) * rows, rows)
                nat[a, g, pl.ds(at, rows)] = got[i][a, :, lanes].astype(F32)
            for c in range(CLASSES):
                x[a, c, :, lanes] = nat[a, g, pl.ds(c, m2, stride=CLASSES), :].astype(BF16)
        for c in range(CLASSES):
            data = x[a, c]
            u[a, c] = dot(fwd[c], jnp.concatenate([data, data], 0))

    def middle(i, carry):
        r = pl.multiple_of(i * step_rows, step_rows)
        re, im = pl.ds(r, step_rows), pl.ds(m2 + r, step_rows)
        for lanes in groups:
            kv = dft([(u[0, c, re, lanes], u[0, c, im, lanes]) for c in range(CLASSES)], -1)
            wt = dft([(u[1, c, re, lanes], u[1, c, im, lanes]) for c in range(CLASSES)], -1)
            fs = [(filt[k, re, lanes], filt[k, im, lanes]) for k in range(CLASSES)]
            for o, (left, right, conj) in enumerate([(kv, fs, False), (wt, fs, True), (wt, kv, True)]):
                z = dft([times(s, t, conj) for s, t in zip(left, right)], 1)
                for c in range(CLASSES):
                    y[o, c, re, lanes] = z[c][0].astype(BF16)
                    y[o, c, im, lanes] = z[c][1].astype(BF16)
        return carry

    lax.fori_loop(0, CLASSES, middle, 0)

    for c in range(CLASSES):
        grad[c] = dot(back[c], y[2, c])
        for o in range(2):
            turned[o, c] = dot(back[c], y[o, c]).astype(BF16)
    for i, j in enumerate(back_peers(n)):
        at = pl.multiple_of((me[0] ^ j) * part_rows, part_rows)
        for o in range(2):
            for c in range(CLASSES):
                out[i][half, o, c * part_rows : (c + 1) * part_rows] = turned[o, c, pl.ds(at, part_rows)]
    for j in range(d):
        at = pl.multiple_of((me[1] ^ j) * per, per)
        for c in range(CLASSES):
            part = grad[c, pl.ds(at, per)]
            if j % 2:
                send[j // 2, c * per : (c + 1) * per] = part.astype(BF16)
            else:
                keep[j // 2, c * per : (c + 1) * per] = part


def conv(n, d, half, me, got, filt, fwd, back, before):
    _, rows, width = got[0].shape
    length = n * rows
    m2 = length // CLASSES
    out = pl.pallas_call(
        functools.partial(conv_kernel, n, d, half),
        in_specs=[SMEM] + [VMEM] * (n + 3 + len(before)),
        out_specs=[VMEM] * (n + 2),
        out_shape=[pltpu.VMEM((HALVES, 2, rows, width), BF16)] * n
        + [pltpu.VMEM((d // 2, length // d, width), dtype) for dtype in (F32, BF16)],
        scratch_shapes=[
            pltpu.VMEM((2, width // 128, length, 128), F32),
            pltpu.VMEM((2, CLASSES, m2, width), BF16),
            pltpu.VMEM((2, CLASSES, 2 * m2, width), F32),
            pltpu.VMEM((3, CLASSES, 2 * m2, width), BF16),
            pltpu.VMEM((2, CLASSES, m2, width), BF16),
            pltpu.VMEM((CLASSES, m2, width), F32),
        ],
        input_output_aliases={n + 4 + i: i for i in range(len(before))},
        compiler_params=CONV_PARAMS,
        name="conv",
    )(me, *got, filt, fwd, back, *before)
    return out


def natural(scratch, piece):
    rows = piece.shape[0] // CLASSES
    for c in range(CLASSES):
        scratch[pl.ds(c, rows, stride=CLASSES), :] = piece[c * rows : (c + 1) * rows]
    return scratch[...]


def gate_kernel(js, me, query, grad, value, key, gain, *refs):
    got, outs, token, (sent, sems, nat) = refs[: len(js)], refs[-8:-4], refs[-4], refs[-3:]
    token[...] = jnp.zeros_like(token)
    _, _, rows, width = got[0].shape
    copies = []
    for i, j in enumerate(js):
        block = peer_columns(me, j, HALVES * width)
        for half in range(HALVES):
            for g, lanes in enumerate(lane_groups(width)):
                at = half * width + lanes.start
                start = pl.multiple_of((me[0] ^ j) * HALVES * width + at, 128)
                cols = pl.ds(start, 128)
                to = slice(at, at + 128)
                scale = gain[:, cols]
                q, g_, v, k = (x[:, cols].astype(F32) for x in (query, grad, value, key))
                conv_out, corr_back = (
                    natural(nat.at[i, o, half, g], got[i][half, o, :, lanes].astype(F32)) for o in range(2)
                )
                mixing = conv_out + scale * (k * v).astype(BF16).astype(F32)
                sent[0, i, :, to] = (q * mixing).astype(BF16)
                sent[1, i, :, to] = (g_ * mixing).astype(BF16)
                total = corr_back + scale * (g_ * q).astype(BF16).astype(F32)
                sent[2, i, :, to] = (total * v).astype(BF16)
                sent[3, i, :, to] = (total * k).astype(BF16)
        for a in range(4):
            copy = pltpu.make_async_copy(sent.at[a, i], outs[a].at[:, block], sems.at[a, i])
            copy.start()
            copies.append(copy)
    for copy in copies:
        copy.wait()


def gate(js, me, query, grad, value, key, gain, got, outs):
    _, _, rows, width = got[0].shape
    return pl.pallas_call(
        functools.partial(gate_kernel, js),
        in_specs=[SMEM] + [VMEM] * (5 + len(got)) + [HBM] * len(outs),
        out_specs=[HBM] * 4 + [VMEM],
        out_shape=[jax.ShapeDtypeStruct(query.shape, BF16)] * 4 + [pltpu.VMEM((8, 128), F32)],
        scratch_shapes=[
            pltpu.VMEM((4, len(js), rows, HALVES * width), BF16),
            pltpu.SemaphoreType.DMA((4, len(js))),
            pltpu.VMEM((len(js), 2, HALVES, width // 128, rows, 128), F32),
        ],
        input_output_aliases={6 + len(got) + i: i for i in range(len(outs))},
        compiler_params=PARAMS,
        name="gate",
    )(me, query, grad, value, key, gain, *got, *outs)


def add_kernel(*refs):
    parts, (new_keep, new_send) = refs[:-2], refs[-2:]
    width = parts[0].shape[2]
    for h in range(len(parts) // 2):
        keep, got = parts[2 * h : 2 * h + 2]
        chans = slice(h * width, (h + 1) * width)
        for i in range(new_keep.shape[0]):
            new_keep[i, :, chans] = keep[2 * i] + got[2 * i].astype(F32)
            new_send[i, :, chans] = (keep[2 * i + 1] + got[2 * i + 1].astype(F32)).astype(BF16)


def turn_kernel(keep, got, out, nat):
    for g, lanes in enumerate(lane_groups(keep.shape[2])):
        total = keep[0, :, lanes] + got[0, :, lanes].astype(F32)
        out[lanes, :] = natural(nat.at[g], total).T


def trade(d, bit, send):
    return resident(lax.ppermute(send, "dp", [(i, i ^ bit) for i in range(d)]))


def add_grads(*parts):
    count, per, width = parts[0].shape
    shape = (count // 2, per, width * len(parts) // 2)
    return pl.pallas_call(
        add_kernel,
        in_specs=[VMEM] * len(parts),
        out_specs=[VMEM] * 2,
        out_shape=[pltpu.VMEM(shape, F32), pltpu.VMEM(shape, BF16)],
        compiler_params=PARAMS,
        name="add_grads",
    )(*parts)


def turn_grads(keep, got):
    _, per, chans = keep.shape
    return pl.pallas_call(
        turn_kernel,
        in_specs=[VMEM] * 2,
        out_specs=VMEM,
        out_shape=jax.ShapeDtypeStruct((chans, per), F32),
        scratch_shapes=[pltpu.VMEM((chans // 128, per, 128), F32)],
        compiler_params=PARAMS,
        name="turn_grads",
    )(keep, got)


def peers(n):
    return [0, 1, *range(2, n, 2), *range(3, n, 2)]


def back_peers(n):
    return [0, n - 2, 1, *range(2, n - 2, 2), *range(3, n, 2)]


def exchange(n, js, blocks):
    return [
        resident(lax.ppermute(block, "ctx", [(i, i ^ j) for i in range(n)])) if j else block
        for j, block in zip(js, blocks)
    ]


def after_kernel(*refs):
    pass


def after(arrived, blocks):
    count = len(arrived)
    return pl.pallas_call(
        after_kernel,
        in_specs=[VMEM] * (count + len(blocks)),
        out_specs=[VMEM] * len(blocks),
        out_shape=[pltpu.VMEM(b.shape, b.dtype) for b in blocks],
        input_output_aliases={count + i: i for i in range(len(blocks))},
        compiler_params=PARAMS,
        name="after",
    )(*arrived, *blocks)


def local(n, d, query_in, key_in, value_in, grad_out, filters, skip_gain):
    fwd, back = (resident(jnp.asarray(t)) for t in tables(filters.shape[1]))
    filters = resident(filters)
    gain = skip_gain[None, :]
    me = jnp.stack([lax.axis_index("ctx"), lax.axis_index("dp")]).astype(jnp.int32)

    arrays = [x[0] for x in (key_in, value_in, query_in, grad_out)]
    js = peers(n)
    cut = n // 2
    first = products(0, n, me, [in_hbm(x) for x in arrays], [])
    first = exchange(n, js, first)
    key, value, query, grad = arrays = [resident(x) for x in arrays]
    other = products(1, n, me, arrays, first[1:2])
    spec = filter_spectrum(0, filters, fwd, first[1:3])
    second = exchange(n, js[:cut], after([spec], other[:cut]))
    spec_other = filter_spectrum(1, filters, fwd, [spec])
    second += exchange(n, js[cut:], after([spec_other], other[cut:]))
    *mixed, keep, send = conv(n, d, 0, me, first, spec, fwd, back, [])
    traded = trade(d, 1, send)
    *mixed, keep_other, send = conv(n, d, 1, me, second, spec_other, fwd, back, mixed)

    bits = [1 << b for b in range(d.bit_length() - 1)]
    parts_ = keep, traded, keep_other, trade(d, 1, send)
    js = back_peers(n)
    mixed = exchange(n, js, mixed)
    for bit in bits[1:]:
        keep, send = add_grads(*parts_)
        parts_ = keep, trade(d, bit, send)

    outs = []
    early = n - 2
    for at in (slice(early), slice(early, n)):
        *outs, _ = gate(js[at], me, query, grad, value, key, gain, mixed[at], outs)
    grad_filter = turn_grads(*parts_)
    return *(x[None] for x in outs), grad_filter


def solution(mesh):
    rows = P("dp", "ctx", None)
    return jax.shard_map(
        functools.partial(local, mesh.shape["ctx"], mesh.shape["dp"]),
        mesh=mesh,
        in_specs=(rows, rows, rows, rows, P("ctx", None), P()),
        out_specs=(rows, rows, rows, rows, P("ctx", "dp")),
        check_vma=False,
    )
```

```python
import functools
import math

import jax
import jax.numpy as jnp
import ml_dtypes
import numpy as np
from jax import lax
from jax.experimental import pallas as pl
from jax.experimental.pallas import tpu as pltpu
from jax.sharding import PartitionSpec as P

F32 = jnp.float32
BF16 = jnp.bfloat16
CLASSES = 8
HALVES = 2
PARAMS = pltpu.CompilerParams(vmem_limit_bytes=16 * 1024 * 1024)
CONV_PARAMS = pltpu.CompilerParams(vmem_limit_bytes=34 * 1024 * 1024)
SMEM = pl.BlockSpec(memory_space=pltpu.SMEM)
VMEM = pl.BlockSpec(memory_space=pltpu.VMEM)
HBM = pl.BlockSpec(memory_space=pltpu.HBM)


def tables(length):
    m2 = length // CLASSES
    c = np.arange(CLASSES)[:, None, None]
    j = np.arange(m2)[None, :, None]
    m = np.arange(m2)[None, None, :]
    turn = ((CLASSES * m + c) * (2 * j + 1)) % (4 * length)
    angle = 2 * np.pi * turn / (4 * length)
    forward = np.concatenate([np.cos(angle), -np.sin(angle)], 1)
    back = np.swapaxes(forward, 1, 2) / length

    def parts(x):
        hi = x.astype(ml_dtypes.bfloat16)
        return hi, (x - hi.astype(np.float64)).astype(ml_dtypes.bfloat16)

    return np.concatenate(parts(forward), 2), back.astype(ml_dtypes.bfloat16)


def parts(x):
    hi = x.astype(BF16)
    return hi, (x - hi.astype(F32)).astype(BF16)


def dot(a, b):
    return jnp.dot(a, b, preferred_element_type=F32)


def dft(z, sign):
    n = len(z)
    if n == 1:
        return z
    even, odd = dft(z[0::2], sign), dft(z[1::2], sign)
    low, high = [], []
    for k in range(n // 2):
        (er, ei), (zr, zi) = even[k], odd[k]
        if k == 0:
            tr, ti = zr, zi
        elif 4 * k == n:
            tr, ti = (-zi, zr) if sign > 0 else (zi, -zr)
        else:
            c, s = math.cos(2 * math.pi * k / n), sign * math.sin(2 * math.pi * k / n)
            if 8 * k == n:
                tr, ti = (c * (zr - zi), c * (zi + zr)) if sign > 0 else (c * (zr + zi), c * (zi - zr))
            elif 8 * k == 3 * n:
                tr, ti = (c * (zr + zi), c * (zi - zr)) if sign > 0 else (c * (zr - zi), c * (zi + zr))
            else:
                tr, ti = c * zr - s * zi, c * zi + s * zr
        low.append((er + tr, ei + ti))
        high.append((er - tr, ei - ti))
    return low + high


def times(x, f, conj):
    (xr, xi), (fr, fi) = x, f
    if conj:
        return xr * fr + xi * fi, xi * fr - xr * fi
    return xr * fr - xi * fi, xr * fi + xi * fr


def resident(x):
    return pltpu.with_memory_space_constraint(x, pltpu.VMEM)


def in_hbm(x):
    return pltpu.with_memory_space_constraint(x, pltpu.HBM)


def peer_columns(me, j, width):
    return pl.ds(pl.multiple_of((me[0] ^ j) * width, 128), width)


def half_columns(me, j, half, width):
    return pl.ds(pl.multiple_of((HALVES * (me[0] ^ j) + half) * width, 128), width)


def first_kernel(n, me, key, value, query, grad, *refs):
    outs, (bufs, sems) = refs[:n], refs[n:]
    width = outs[0].shape[2]
    copies = []
    for i, j in enumerate(peers(n)):
        cols = half_columns(me, j, 0, width)
        copies.append(
            [
                pltpu.make_async_copy(src.at[:, cols], bufs.at[a, i], sems.at[a, i])
                for a, src in enumerate((key, value, query, grad))
            ]
        )
        for copy in copies[i]:
            copy.start()
    for i, out in enumerate(outs):
        for copy in copies[i]:
            copy.wait()
        for a in range(2):
            left, right = bufs[2 * a, i].astype(F32), bufs[2 * a + 1, i].astype(F32)
            out[a] = (left * right).astype(BF16)


def second_kernel(n, me, key, value, query, grad, *refs):
    outs = refs[-n:]
    width = outs[0].shape[2]
    for out, j in zip(outs, peers(n)):
        cols = half_columns(me, j, 1, width)
        for a, (left, right) in enumerate(((key, value), (query, grad))):
            out[a] = (left[:, cols].astype(F32) * right[:, cols].astype(F32)).astype(BF16)


def products(half, n, me, arrays, arrived):
    rows, total = arrays[0].shape
    width = total // n // HALVES
    scratch = [pltpu.VMEM((4, n, rows, width), BF16), pltpu.SemaphoreType.DMA((4, n))]
    return pl.pallas_call(
        functools.partial(second_kernel if half else first_kernel, n),
        in_specs=[SMEM] + [VMEM if half else HBM] * 4 + [VMEM] * len(arrived),
        out_specs=[VMEM] * n,
        out_shape=[pltpu.VMEM((2, rows, width), BF16)] * n,
        scratch_shapes=[] if half else scratch,
        compiler_params=PARAMS,
        name="products",
    )(me, *arrays, *arrived)


def lane_groups(width):
    return [slice(i, i + 128) for i in range(0, width, 128)]


def filter_kernel(half, filt, fwd, *refs):
    spec, x, u = refs[-3:]
    m2, width = x.shape[1] // CLASSES, u.shape[-1]
    groups = lane_groups(width)
    rows = m2 // CLASSES
    for g, lanes in enumerate(groups):
        x[g] = filt[half * width + lanes.start : half * width + lanes.stop, :].T
    for c in range(CLASSES):
        for g, lanes in enumerate(groups):
            hi, lo = parts(x[g, pl.ds(c, m2, stride=CLASSES), :])
            u[c, :, lanes] = dot(fwd[c], jnp.concatenate([hi, hi], 0)) + dot(fwd[c, :, :m2], lo)

    def step(i, carry):
        r = pl.multiple_of(i * rows, rows)
        re, im = pl.ds(r, rows), pl.ds(m2 + r, rows)
        for lanes in groups:
            z = dft([(u[c, re, lanes], u[c, im, lanes]) for c in range(CLASSES)], -1)
            for k in range(CLASSES):
                spec[k, re, lanes], spec[k, im, lanes] = z[k]
        return carry

    lax.fori_loop(0, CLASSES, step, 0)


def filter_spectrum(half, filters, fwd, arrived):
    chans, length = filters.shape
    width = chans // HALVES
    m2 = length // CLASSES
    return pl.pallas_call(
        functools.partial(filter_kernel, half),
        in_specs=[VMEM] * (2 + len(arrived)),
        out_specs=VMEM,
        out_shape=pltpu.VMEM((CLASSES, 2 * m2, width), F32),
        scratch_shapes=[
            pltpu.VMEM((width // 128, length, 128), F32),
            pltpu.VMEM((CLASSES, 2 * m2, width), F32),
        ],
        compiler_params=PARAMS,
        name="filter_spectrum",
    )(filters, fwd, *arrived)


def conv_kernel(n, d, half, me, *refs):
    got, (filt, fwd, back) = refs[:n], refs[n : n + 3]
    refs = refs[-(n + 2 + 6) :]
    out, (keep, send), (nat, x, u, y, turned, grad) = refs[:n], refs[n : n + 2], refs[n + 2 :]
    _, rows, width = got[0].shape
    m2 = x.shape[2]
    per = keep.shape[1] // CLASSES
    groups = lane_groups(width)
    step_rows = m2 // CLASSES
    part_rows = rows // CLASSES

    for a in range(2):
        for g, lanes in enumerate(groups):
            for i, j in enumerate(peers(n)):
                at = pl.multiple_of((me[0] ^ j) * rows, rows)
                nat[a, g, pl.ds(at, rows)] = got[i][a, :, lanes].astype(F32)
            for c in range(CLASSES):
                x[a, c, :, lanes] = nat[a, g, pl.ds(c, m2, stride=CLASSES), :].astype(BF16)
        for c in range(CLASSES):
            data = x[a, c]
            u[a, c] = dot(fwd[c], jnp.concatenate([data, data], 0))

    def middle(i, carry):
        r = pl.multiple_of(i * step_rows, step_rows)
        re, im = pl.ds(r, step_rows), pl.ds(m2 + r, step_rows)
        for lanes in groups:
            kv = dft([(u[0, c, re, lanes], u[0, c, im, lanes]) for c in range(CLASSES)], -1)
            wt = dft([(u[1, c, re, lanes], u[1, c, im, lanes]) for c in range(CLASSES)], -1)
            fs = [(filt[k, re, lanes], filt[k, im, lanes]) for k in range(CLASSES)]
            for o, (left, right, conj) in enumerate([(kv, fs, False), (wt, fs, True), (wt, kv, True)]):
                z = dft([times(s, t, conj) for s, t in zip(left, right)], 1)
                for c in range(CLASSES):
                    y[o, c, re, lanes] = z[c][0].astype(BF16)
                    y[o, c, im, lanes] = z[c][1].astype(BF16)
        return carry

    lax.fori_loop(0, CLASSES, middle, 0, unroll=2)

    for c in range(CLASSES):
        grad[c] = dot(back[c], y[2, c])
        for o in range(2):
            turned[o, c] = dot(back[c], y[o, c]).astype(BF16)
    for i, j in enumerate(back_peers(n)):
        at = pl.multiple_of((me[0] ^ j) * part_rows, part_rows)
        for o in range(2):
            for c in range(CLASSES):
                out[i][half, o, c * part_rows : (c + 1) * part_rows] = turned[o, c, pl.ds(at, part_rows)]
    for j in range(d):
        at = pl.multiple_of((me[1] ^ j) * per, per)
        for c in range(CLASSES):
            part = grad[c, pl.ds(at, per)]
            if j % 2:
                send[j // 2, c * per : (c + 1) * per] = part.astype(BF16)
            else:
                keep[j // 2, c * per : (c + 1) * per] = part


def conv(n, d, half, me, got, filt, fwd, back, before):
    _, rows, width = got[0].shape
    length = n * rows
    m2 = length // CLASSES
    out = pl.pallas_call(
        functools.partial(conv_kernel, n, d, half),
        in_specs=[SMEM] + [VMEM] * (n + 3 + len(before)),
        out_specs=[VMEM] * (n + 2),
        out_shape=[pltpu.VMEM((HALVES, 2, rows, width), BF16)] * n
        + [pltpu.VMEM((d // 2, length // d, width), dtype) for dtype in (F32, BF16)],
        scratch_shapes=[
            pltpu.VMEM((2, width // 128, length, 128), F32),
            pltpu.VMEM((2, CLASSES, m2, width), BF16),
            pltpu.VMEM((2, CLASSES, 2 * m2, width), F32),
            pltpu.VMEM((3, CLASSES, 2 * m2, width), BF16),
            pltpu.VMEM((2, CLASSES, m2, width), BF16),
            pltpu.VMEM((CLASSES, m2, width), F32),
        ],
        input_output_aliases={n + 4 + i: i for i in range(len(before))},
        compiler_params=CONV_PARAMS,
        name="conv",
    )(me, *got, filt, fwd, back, *before)
    return out


def natural(scratch, piece):
    rows = piece.shape[0] // CLASSES
    for c in range(CLASSES):
        scratch[pl.ds(c, rows, stride=CLASSES), :] = piece[c * rows : (c + 1) * rows]
    return scratch[...]


def gate_kernel(js, me, query, grad, value, key, gain, *refs):
    got, outs, token, (sent, sems, nat) = refs[: len(js)], refs[-8:-4], refs[-4], refs[-3:]
    token[...] = jnp.zeros_like(token)
    _, _, rows, width = got[0].shape
    copies = []
    for i, j in enumerate(js):
        block = peer_columns(me, j, HALVES * width)
        for half in range(HALVES):
            for g, lanes in enumerate(lane_groups(width)):
                at = half * width + lanes.start
                start = pl.multiple_of((me[0] ^ j) * HALVES * width + at, 128)
                cols = pl.ds(start, 128)
                to = slice(at, at + 128)
                scale = gain[:, cols]
                q, g_, v, k = (x[:, cols].astype(F32) for x in (query, grad, value, key))
                conv_out, corr_back = (
                    natural(nat.at[i, o, half, g], got[i][half, o, :, lanes].astype(F32)) for o in range(2)
                )
                mixing = conv_out + scale * (k * v).astype(BF16).astype(F32)
                sent[0, i, :, to] = (q * mixing).astype(BF16)
                sent[1, i, :, to] = (g_ * mixing).astype(BF16)
                total = corr_back + scale * (g_ * q).astype(BF16).astype(F32)
                sent[2, i, :, to] = (total * v).astype(BF16)
                sent[3, i, :, to] = (total * k).astype(BF16)
        for a in range(4):
            copy = pltpu.make_async_copy(sent.at[a, i], outs[a].at[:, block], sems.at[a, i])
            copy.start()
            copies.append(copy)
    for copy in copies:
        copy.wait()


def gate(js, me, query, grad, value, key, gain, got, outs):
    _, _, rows, width = got[0].shape
    return pl.pallas_call(
        functools.partial(gate_kernel, js),
        in_specs=[SMEM] + [VMEM] * (5 + len(got)) + [HBM] * len(outs),
        out_specs=[HBM] * 4 + [VMEM],
        out_shape=[jax.ShapeDtypeStruct(query.shape, BF16)] * 4 + [pltpu.VMEM((8, 128), F32)],
        scratch_shapes=[
            pltpu.VMEM((4, len(js), rows, HALVES * width), BF16),
            pltpu.SemaphoreType.DMA((4, len(js))),
            pltpu.VMEM((len(js), 2, HALVES, width // 128, rows, 128), F32),
        ],
        input_output_aliases={6 + len(got) + i: i for i in range(len(outs))},
        compiler_params=PARAMS,
        name="gate",
    )(me, query, grad, value, key, gain, *got, *outs)


def add_kernel(*refs):
    parts, (new_keep, new_send) = refs[:-2], refs[-2:]
    width = parts[0].shape[2]
    for h in range(len(parts) // 2):
        keep, got = parts[2 * h : 2 * h + 2]
        chans = slice(h * width, (h + 1) * width)
        for i in range(new_keep.shape[0]):
            new_keep[i, :, chans] = keep[2 * i] + got[2 * i].astype(F32)
            new_send[i, :, chans] = (keep[2 * i + 1] + got[2 * i + 1].astype(F32)).astype(BF16)


def turn_kernel(keep, got, out, nat):
    for g, lanes in enumerate(lane_groups(keep.shape[2])):
        total = keep[0, :, lanes] + got[0, :, lanes].astype(F32)
        out[lanes, :] = natural(nat.at[g], total).T


def trade(d, bit, send):
    return resident(lax.ppermute(send, "dp", [(i, i ^ bit) for i in range(d)]))


def add_grads(*parts):
    count, per, width = parts[0].shape
    shape = (count // 2, per, width * len(parts) // 2)
    return pl.pallas_call(
        add_kernel,
        in_specs=[VMEM] * len(parts),
        out_specs=[VMEM] * 2,
        out_shape=[pltpu.VMEM(shape, F32), pltpu.VMEM(shape, BF16)],
        compiler_params=PARAMS,
        name="add_grads",
    )(*parts)


def turn_grads(keep, got):
    _, per, chans = keep.shape
    return pl.pallas_call(
        turn_kernel,
        in_specs=[VMEM] * 2,
        out_specs=VMEM,
        out_shape=jax.ShapeDtypeStruct((chans, per), F32),
        scratch_shapes=[pltpu.VMEM((chans // 128, per, 128), F32)],
        compiler_params=PARAMS,
        name="turn_grads",
    )(keep, got)


def peers(n):
    return [0, 1, *range(2, n, 2), *range(3, n, 2)]


def back_peers(n):
    return [0, n - 2, 1, *range(2, n - 2, 2), *range(3, n, 2)]


def exchange(n, js, blocks):
    return [
        resident(lax.ppermute(block, "ctx", [(i, i ^ j) for i in range(n)])) if j else block
        for j, block in zip(js, blocks)
    ]


def after_kernel(*refs):
    pass


def after(arrived, blocks):
    count = len(arrived)
    return pl.pallas_call(
        after_kernel,
        in_specs=[VMEM] * (count + len(blocks)),
        out_specs=[VMEM] * len(blocks),
        out_shape=[pltpu.VMEM(b.shape, b.dtype) for b in blocks],
        input_output_aliases={count + i: i for i in range(len(blocks))},
        compiler_params=PARAMS,
        name="after",
    )(*arrived, *blocks)


def local(n, d, query_in, key_in, value_in, grad_out, filters, skip_gain):
    fwd, back = (resident(jnp.asarray(t)) for t in tables(filters.shape[1]))
    filters = resident(filters)
    gain = skip_gain[None, :]
    me = jnp.stack([lax.axis_index("ctx"), lax.axis_index("dp")]).astype(jnp.int32)

    arrays = [x[0] for x in (key_in, value_in, query_in, grad_out)]
    js = peers(n)
    cut = n // 2
    first = products(0, n, me, [in_hbm(x) for x in arrays], [])
    first = exchange(n, js, first)
    key, value, query, grad = arrays = [resident(x) for x in arrays]
    other = products(1, n, me, arrays, first[1:2])
    spec = filter_spectrum(0, filters, fwd, first[1:3])
    second = exchange(n, js[:cut], after([spec], other[:cut]))
    spec_other = filter_spectrum(1, filters, fwd, [spec])
    second += exchange(n, js[cut:], after([spec_other], other[cut:]))
    *mixed, keep, send = conv(n, d, 0, me, first, spec, fwd, back, [])
    traded = trade(d, 1, send)
    *mixed, keep_other, send = conv(n, d, 1, me, second, spec_other, fwd, back, mixed)

    bits = [1 << b for b in range(d.bit_length() - 1)]
    parts_ = keep, traded, keep_other, trade(d, 1, send)
    js = back_peers(n)
    mixed = exchange(n, js, mixed)
    for bit in bits[1:]:
        keep, send = add_grads(*parts_)
        parts_ = keep, trade(d, bit, send)

    outs = []
    early = n - 2
    for at in (slice(early), slice(early, n)):
        *outs, _ = gate(js[at], me, query, grad, value, key, gain, mixed[at], outs)
    grad_filter = turn_grads(*parts_)
    return *(x[None] for x in outs), grad_filter


def solution(mesh):
    rows = P("dp", "ctx", None)
    return jax.shard_map(
        functools.partial(local, mesh.shape["ctx"], mesh.shape["dp"]),
        mesh=mesh,
        in_specs=(rows, rows, rows, rows, P("ctx", None), P()),
        out_specs=(rows, rows, rows, rows, P("ctx", "dp")),
        check_vma=False,
    )
```

```python
import functools
import math

import jax
import jax.numpy as jnp
import ml_dtypes
import numpy as np
from jax import lax
from jax.experimental import pallas as pl
from jax.experimental.pallas import tpu as pltpu
from jax.sharding import PartitionSpec as P

F32 = jnp.float32
BF16 = jnp.bfloat16
CLASSES = 8
HALVES = 2
PARAMS = pltpu.CompilerParams(vmem_limit_bytes=16 * 1024 * 1024)
CONV_PARAMS = pltpu.CompilerParams(vmem_limit_bytes=34 * 1024 * 1024)
SMEM = pl.BlockSpec(memory_space=pltpu.SMEM)
VMEM = pl.BlockSpec(memory_space=pltpu.VMEM)
HBM = pl.BlockSpec(memory_space=pltpu.HBM)


def tables(length):
    m2 = length // CLASSES
    c = np.arange(CLASSES)[:, None, None]
    j = np.arange(m2)[None, :, None]
    m = np.arange(m2)[None, None, :]
    turn = ((CLASSES * m + c) * (2 * j + 1)) % (4 * length)
    angle = 2 * np.pi * turn / (4 * length)
    forward = np.concatenate([np.cos(angle), -np.sin(angle)], 1)
    back = np.swapaxes(forward, 1, 2) / length

    def parts(x):
        hi = x.astype(ml_dtypes.bfloat16)
        return hi, (x - hi.astype(np.float64)).astype(ml_dtypes.bfloat16)

    return np.concatenate(parts(forward), 2), back.astype(ml_dtypes.bfloat16)


def parts(x):
    hi = x.astype(BF16)
    return hi, (x - hi.astype(F32)).astype(BF16)


def dot(a, b):
    return jnp.dot(a, b, preferred_element_type=F32)


def dft(z, sign):
    n = len(z)
    if n == 1:
        return z
    even, odd = dft(z[0::2], sign), dft(z[1::2], sign)
    low, high = [], []
    for k in range(n // 2):
        (er, ei), (zr, zi) = even[k], odd[k]
        if k == 0:
            tr, ti = zr, zi
        elif 4 * k == n:
            tr, ti = (-zi, zr) if sign > 0 else (zi, -zr)
        else:
            c, s = math.cos(2 * math.pi * k / n), sign * math.sin(2 * math.pi * k / n)
            if 8 * k == n:
                tr, ti = (c * (zr - zi), c * (zi + zr)) if sign > 0 else (c * (zr + zi), c * (zi - zr))
            elif 8 * k == 3 * n:
                tr, ti = (c * (zr + zi), c * (zi - zr)) if sign > 0 else (c * (zr - zi), c * (zi + zr))
            else:
                tr, ti = c * zr - s * zi, c * zi + s * zr
        low.append((er + tr, ei + ti))
        high.append((er - tr, ei - ti))
    return low + high


def times(x, f, conj):
    (xr, xi), (fr, fi) = x, f
    if conj:
        return xr * fr + xi * fi, xi * fr - xr * fi
    return xr * fr - xi * fi, xr * fi + xi * fr


def resident(x):
    return pltpu.with_memory_space_constraint(x, pltpu.VMEM)


def in_hbm(x):
    return pltpu.with_memory_space_constraint(x, pltpu.HBM)


def peer_columns(me, j, width):
    return pl.ds(pl.multiple_of((me[0] ^ j) * width, 128), width)


def half_columns(me, j, half, width):
    return pl.ds(pl.multiple_of((HALVES * (me[0] ^ j) + half) * width, 128), width)


def first_kernel(n, me, key, value, query, grad, *refs):
    outs, (bufs, sems) = refs[:n], refs[n:]
    width = outs[0].shape[2]
    copies = []
    for i, j in enumerate(peers(n)):
        cols = half_columns(me, j, 0, width)
        copies.append(
            [
                pltpu.make_async_copy(src.at[:, cols], bufs.at[a, i], sems.at[a, i])
                for a, src in enumerate((key, value, query, grad))
            ]
        )
        for copy in copies[i]:
            copy.start()
    for i, out in enumerate(outs):
        for copy in copies[i]:
            copy.wait()
        for a in range(2):
            left, right = bufs[2 * a, i].astype(F32), bufs[2 * a + 1, i].astype(F32)
            out[a] = (left * right).astype(BF16)


def second_kernel(n, me, key, value, query, grad, *refs):
    outs = refs[-n:]
    width = outs[0].shape[2]
    for out, j in zip(outs, peers(n)):
        cols = half_columns(me, j, 1, width)
        for a, (left, right) in enumerate(((key, value), (query, grad))):
            out[a] = (left[:, cols].astype(F32) * right[:, cols].astype(F32)).astype(BF16)


def products(half, n, me, arrays, arrived):
    rows, total = arrays[0].shape
    width = total // n // HALVES
    scratch = [pltpu.VMEM((4, n, rows, width), BF16), pltpu.SemaphoreType.DMA((4, n))]
    return pl.pallas_call(
        functools.partial(second_kernel if half else first_kernel, n),
        in_specs=[SMEM] + [VMEM if half else HBM] * 4 + [VMEM] * len(arrived),
        out_specs=[VMEM] * n,
        out_shape=[pltpu.VMEM((2, rows, width), BF16)] * n,
        scratch_shapes=[] if half else scratch,
        compiler_params=PARAMS,
        name="products",
    )(me, *arrays, *arrived)


def lane_groups(width):
    return [slice(i, i + 128) for i in range(0, width, 128)]


def filter_kernel(half, filt, fwd, *refs):
    spec, x, u = refs[-3:]
    m2, width = x.shape[1] // CLASSES, u.shape[-1]
    groups = lane_groups(width)
    rows = m2 // CLASSES
    for g, lanes in enumerate(groups):
        x[g] = filt[half * width + lanes.start : half * width + lanes.stop, :].T
    for c in range(CLASSES):
        for g, lanes in enumerate(groups):
            hi, lo = parts(x[g, pl.ds(c, m2, stride=CLASSES), :])
            u[c, :, lanes] = dot(fwd[c], jnp.concatenate([hi, hi], 0)) + dot(fwd[c, :, :m2], lo)

    def step(i, carry):
        r = pl.multiple_of(i * rows, rows)
        re, im = pl.ds(r, rows), pl.ds(m2 + r, rows)
        for lanes in groups:
            z = dft([(u[c, re, lanes], u[c, im, lanes]) for c in range(CLASSES)], -1)
            for k in range(CLASSES):
                spec[k, re, lanes], spec[k, im, lanes] = z[k]
        return carry

    lax.fori_loop(0, CLASSES, step, 0)


def filter_spectrum(half, filters, fwd, arrived):
    chans, length = filters.shape
    width = chans // HALVES
    m2 = length // CLASSES
    return pl.pallas_call(
        functools.partial(filter_kernel, half),
        in_specs=[VMEM] * (2 + len(arrived)),
        out_specs=VMEM,
        out_shape=pltpu.VMEM((CLASSES, 2 * m2, width), F32),
        scratch_shapes=[
            pltpu.VMEM((width // 128, length, 128), F32),
            pltpu.VMEM((CLASSES, 2 * m2, width), F32),
        ],
        compiler_params=PARAMS,
        name="filter_spectrum",
    )(filters, fwd, *arrived)


def conv_kernel(n, d, half, me, *refs):
    got, (filt, fwd, back) = refs[:n], refs[n : n + 3]
    refs = refs[-(n + 2 + 6) :]
    out, (keep, send), (nat, x, u, y, turned, grad) = refs[:n], refs[n : n + 2], refs[n + 2 :]
    _, rows, width = got[0].shape
    m2 = x.shape[2]
    per = keep.shape[1] // CLASSES
    groups = lane_groups(width)
    step_rows = m2 // CLASSES
    part_rows = rows // CLASSES

    for a in range(2):
        for g, lanes in enumerate(groups):
            for i, j in enumerate(peers(n)):
                at = pl.multiple_of((me[0] ^ j) * rows, rows)
                nat[a, g, pl.ds(at, rows)] = got[i][a, :, lanes].astype(F32)
            for c in range(CLASSES):
                x[a, c, :, lanes] = nat[a, g, pl.ds(c, m2, stride=CLASSES), :].astype(BF16)
        for c in range(CLASSES):
            data = x[a, c]
            u[a, c] = dot(fwd[c], jnp.concatenate([data, data], 0))

    def middle(i, carry):
        r = pl.multiple_of(i * step_rows, step_rows)
        re, im = pl.ds(r, step_rows), pl.ds(m2 + r, step_rows)
        for lanes in groups:
            kv = dft([(u[0, c, re, lanes], u[0, c, im, lanes]) for c in range(CLASSES)], -1)
            wt = dft([(u[1, c, re, lanes], u[1, c, im, lanes]) for c in range(CLASSES)], -1)
            fs = [(filt[k, re, lanes], filt[k, im, lanes]) for k in range(CLASSES)]
            for o, (left, right, conj) in enumerate([(kv, fs, False), (wt, fs, True), (wt, kv, True)]):
                z = dft([times(s, t, conj) for s, t in zip(left, right)], 1)
                for c in range(CLASSES):
                    y[o, c, re, lanes] = z[c][0].astype(BF16)
                    y[o, c, im, lanes] = z[c][1].astype(BF16)
        return carry

    lax.fori_loop(0, CLASSES, middle, 0, unroll=2)

    for c in range(CLASSES):
        grad[c] = dot(back[c], y[2, c])
        for o in range(2):
            turned[o, c] = dot(back[c], y[o, c]).astype(BF16)
    for i, j in enumerate(back_peers(n)):
        at = pl.multiple_of((me[0] ^ j) * part_rows, part_rows)
        for o in range(2):
            for c in range(CLASSES):
                out[i][half, o, c * part_rows : (c + 1) * part_rows] = turned[o, c, pl.ds(at, part_rows)]
    for j in range(d):
        at = pl.multiple_of((me[1] ^ j) * per, per)
        for c in range(CLASSES):
            part = grad[c, pl.ds(at, per)]
            if j % 2:
                send[j // 2, c * per : (c + 1) * per] = part.astype(BF16)
            else:
                keep[j // 2, c * per : (c + 1) * per] = part


def conv(n, d, half, me, got, filt, fwd, back, before):
    _, rows, width = got[0].shape
    length = n * rows
    m2 = length // CLASSES
    out = pl.pallas_call(
        functools.partial(conv_kernel, n, d, half),
        in_specs=[SMEM] + [VMEM] * (n + 3 + len(before)),
        out_specs=[VMEM] * (n + 2),
        out_shape=[pltpu.VMEM((HALVES, 2, rows, width), BF16)] * n
        + [pltpu.VMEM((d // 2, length // d, width), dtype) for dtype in (F32, BF16)],
        scratch_shapes=[
            pltpu.VMEM((2, width // 128, length, 128), F32),
            pltpu.VMEM((2, CLASSES, m2, width), BF16),
            pltpu.VMEM((2, CLASSES, 2 * m2, width), F32),
            pltpu.VMEM((3, CLASSES, 2 * m2, width), BF16),
            pltpu.VMEM((2, CLASSES, m2, width), BF16),
            pltpu.VMEM((CLASSES, m2, width), F32),
        ],
        input_output_aliases={n + 4 + i: i for i in range(len(before))},
        compiler_params=CONV_PARAMS,
        name="conv",
    )(me, *got, filt, fwd, back, *before)
    return out


def natural(scratch, piece):
    rows = piece.shape[0] // CLASSES
    for c in range(CLASSES):
        scratch[pl.ds(c, rows, stride=CLASSES), :] = piece[c * rows : (c + 1) * rows]
    return scratch[...]


def gate_kernel(js, me, query, grad, value, key, gain, *refs):
    got, outs, token, (sent, sems, nat) = refs[: len(js)], refs[-8:-4], refs[-4], refs[-3:]
    token[...] = jnp.zeros_like(token)
    _, _, rows, width = got[0].shape
    copies = []
    for i, j in enumerate(js):
        block = peer_columns(me, j, HALVES * width)
        for half in range(HALVES):
            for g, lanes in enumerate(lane_groups(width)):
                at = half * width + lanes.start
                start = pl.multiple_of((me[0] ^ j) * HALVES * width + at, 128)
                cols = pl.ds(start, 128)
                to = slice(at, at + 128)
                scale = gain[:, cols]
                q, g_, v, k = (x[:, cols].astype(F32) for x in (query, grad, value, key))
                conv_out, corr_back = (
                    natural(nat.at[i, o, half, g], got[i][half, o, :, lanes].astype(F32)) for o in range(2)
                )
                mixing = conv_out + scale * (k * v).astype(BF16).astype(F32)
                sent[0, i, :, to] = (q * mixing).astype(BF16)
                sent[1, i, :, to] = (g_ * mixing).astype(BF16)
                total = corr_back + scale * (g_ * q).astype(BF16).astype(F32)
                sent[2, i, :, to] = (total * v).astype(BF16)
                sent[3, i, :, to] = (total * k).astype(BF16)
        for a in range(4):
            copy = pltpu.make_async_copy(sent.at[a, i], outs[a].at[:, block], sems.at[a, i])
            copy.start()
            copies.append(copy)
    for copy in copies:
        copy.wait()


def gate(js, me, query, grad, value, key, gain, got, outs):
    _, _, rows, width = got[0].shape
    return pl.pallas_call(
        functools.partial(gate_kernel, js),
        in_specs=[SMEM] + [VMEM] * (5 + len(got)) + [HBM] * len(outs),
        out_specs=[HBM] * 4 + [VMEM],
        out_shape=[jax.ShapeDtypeStruct(query.shape, BF16)] * 4 + [pltpu.VMEM((8, 128), F32)],
        scratch_shapes=[
            pltpu.VMEM((4, len(js), rows, HALVES * width), BF16),
            pltpu.SemaphoreType.DMA((4, len(js))),
            pltpu.VMEM((len(js), 2, HALVES, width // 128, rows, 128), F32),
        ],
        input_output_aliases={6 + len(got) + i: i for i in range(len(outs))},
        compiler_params=PARAMS,
        name="gate",
    )(me, query, grad, value, key, gain, *got, *outs)


def add_kernel(*refs):
    parts, (new_keep, new_send) = refs[:-2], refs[-2:]
    width = parts[0].shape[2]
    for h in range(len(parts) // 2):
        keep, got = parts[2 * h : 2 * h + 2]
        chans = slice(h * width, (h + 1) * width)
        for i in range(new_keep.shape[0]):
            new_keep[i, :, chans] = keep[2 * i] + got[2 * i].astype(F32)
            new_send[i, :, chans] = (keep[2 * i + 1] + got[2 * i + 1].astype(F32)).astype(BF16)


def turn_kernel(keep, got, out, nat):
    for g, lanes in enumerate(lane_groups(keep.shape[2])):
        total = keep[0, :, lanes] + got[0, :, lanes].astype(F32)
        out[lanes, :] = natural(nat.at[g], total).T


def trade(d, bit, send):
    return resident(lax.ppermute(send, "dp", [(i, i ^ bit) for i in range(d)]))


def add_grads(*parts):
    count, per, width = parts[0].shape
    shape = (count // 2, per, width * len(parts) // 2)
    return pl.pallas_call(
        add_kernel,
        in_specs=[VMEM] * len(parts),
        out_specs=[VMEM] * 2,
        out_shape=[pltpu.VMEM(shape, F32), pltpu.VMEM(shape, BF16)],
        compiler_params=PARAMS,
        name="add_grads",
    )(*parts)


def turn_grads(keep, got):
    _, per, chans = keep.shape
    return pl.pallas_call(
        turn_kernel,
        in_specs=[VMEM] * 2,
        out_specs=VMEM,
        out_shape=jax.ShapeDtypeStruct((chans, per), F32),
        scratch_shapes=[pltpu.VMEM((chans // 128, per, 128), F32)],
        compiler_params=PARAMS,
        name="turn_grads",
    )(keep, got)


def peers(n):
    return [0, 1, *range(2, n, 2), *range(3, n, 2)]


def back_peers(n):
    return [0, n - 2, 1, *range(2, n - 2, 2), n - 1, *range(3, n - 2, 2)]


def exchange(n, js, blocks):
    return [
        resident(lax.ppermute(block, "ctx", [(i, i ^ j) for i in range(n)])) if j else block
        for j, block in zip(js, blocks)
    ]


def after_kernel(*refs):
    pass


def after(arrived, blocks):
    count = len(arrived)
    return pl.pallas_call(
        after_kernel,
        in_specs=[VMEM] * (count + len(blocks)),
        out_specs=[VMEM] * len(blocks),
        out_shape=[pltpu.VMEM(b.shape, b.dtype) for b in blocks],
        input_output_aliases={count + i: i for i in range(len(blocks))},
        compiler_params=PARAMS,
        name="after",
    )(*arrived, *blocks)


def local(n, d, query_in, key_in, value_in, grad_out, filters, skip_gain):
    fwd, back = (resident(jnp.asarray(t)) for t in tables(filters.shape[1]))
    filters = resident(filters)
    gain = skip_gain[None, :]
    me = jnp.stack([lax.axis_index("ctx"), lax.axis_index("dp")]).astype(jnp.int32)

    arrays = [x[0] for x in (key_in, value_in, query_in, grad_out)]
    js = peers(n)
    cut = n // 2
    first = products(0, n, me, [in_hbm(x) for x in arrays], [])
    first = exchange(n, js, first)
    key, value, query, grad = arrays = [resident(x) for x in arrays]
    other = products(1, n, me, arrays, first[1:2])
    spec = filter_spectrum(0, filters, fwd, first[1:3])
    second = exchange(n, js[:cut], after([spec], other[:cut]))
    spec_other = filter_spectrum(1, filters, fwd, [spec])
    second += exchange(n, js[cut:], after([spec_other], other[cut:]))
    *mixed, keep, send = conv(n, d, 0, me, first, spec, fwd, back, [])
    traded = trade(d, 1, send)
    *mixed, keep_other, send = conv(n, d, 1, me, second, spec_other, fwd, back, mixed)

    bits = [1 << b for b in range(d.bit_length() - 1)]
    parts_ = keep, traded, keep_other, trade(d, 1, send)
    js = back_peers(n)
    mixed = exchange(n, js, mixed)
    for bit in bits[1:]:
        keep, send = add_grads(*parts_)
        parts_ = keep, trade(d, bit, send)

    outs = []
    early = n - 2
    for at in (slice(early), slice(early, n)):
        *outs, _ = gate(js[at], me, query, grad, value, key, gain, mixed[at], outs)
    grad_filter = turn_grads(*parts_)
    return *(x[None] for x in outs), grad_filter


def solution(mesh):
    rows = P("dp", "ctx", None)
    return jax.shard_map(
        functools.partial(local, mesh.shape["ctx"], mesh.shape["dp"]),
        mesh=mesh,
        in_specs=(rows, rows, rows, rows, P("ctx", None), P()),
        out_specs=(rows, rows, rows, rows, P("ctx", "dp")),
        check_vma=False,
    )
```

```python
import functools
import math

import jax
import jax.numpy as jnp
import ml_dtypes
import numpy as np
from jax import lax
from jax.experimental import pallas as pl
from jax.experimental.pallas import tpu as pltpu
from jax.sharding import PartitionSpec as P

F32 = jnp.float32
BF16 = jnp.bfloat16
CLASSES = 8
HALVES = 2
PARAMS = pltpu.CompilerParams(vmem_limit_bytes=16 * 1024 * 1024)
CONV_PARAMS = pltpu.CompilerParams(vmem_limit_bytes=34 * 1024 * 1024)
SMEM = pl.BlockSpec(memory_space=pltpu.SMEM)
VMEM = pl.BlockSpec(memory_space=pltpu.VMEM)
HBM = pl.BlockSpec(memory_space=pltpu.HBM)


def tables(length):
    m2 = length // CLASSES
    c = np.arange(CLASSES)[:, None, None]
    j = np.arange(m2)[None, :, None]
    m = np.arange(m2)[None, None, :]
    turn = ((CLASSES * m + c) * (2 * j + 1)) % (4 * length)
    angle = 2 * np.pi * turn / (4 * length)
    forward = np.concatenate([np.cos(angle), -np.sin(angle)], 1)
    back = np.swapaxes(forward, 1, 2) / length

    def parts(x):
        hi = x.astype(ml_dtypes.bfloat16)
        return hi, (x - hi.astype(np.float64)).astype(ml_dtypes.bfloat16)

    return np.concatenate(parts(forward), 2), back.astype(ml_dtypes.bfloat16)


def parts(x):
    hi = x.astype(BF16)
    return hi, (x - hi.astype(F32)).astype(BF16)


def dot(a, b):
    return jnp.dot(a, b, preferred_element_type=F32)


def dft(z, sign):
    n = len(z)
    if n == 1:
        return z
    even, odd = dft(z[0::2], sign), dft(z[1::2], sign)
    low, high = [], []
    for k in range(n // 2):
        (er, ei), (zr, zi) = even[k], odd[k]
        if k == 0:
            tr, ti = zr, zi
        elif 4 * k == n:
            tr, ti = (-zi, zr) if sign > 0 else (zi, -zr)
        else:
            c, s = math.cos(2 * math.pi * k / n), sign * math.sin(2 * math.pi * k / n)
            if 8 * k == n:
                tr, ti = (c * (zr - zi), c * (zi + zr)) if sign > 0 else (c * (zr + zi), c * (zi - zr))
            elif 8 * k == 3 * n:
                tr, ti = (c * (zr + zi), c * (zi - zr)) if sign > 0 else (c * (zr - zi), c * (zi + zr))
            else:
                tr, ti = c * zr - s * zi, c * zi + s * zr
        low.append((er + tr, ei + ti))
        high.append((er - tr, ei - ti))
    return low + high


def times(x, f, conj):
    (xr, xi), (fr, fi) = x, f
    if conj:
        return xr * fr + xi * fi, xi * fr - xr * fi
    return xr * fr - xi * fi, xr * fi + xi * fr


def resident(x):
    return pltpu.with_memory_space_constraint(x, pltpu.VMEM)


def in_hbm(x):
    return pltpu.with_memory_space_constraint(x, pltpu.HBM)


def peer_columns(me, j, width):
    return pl.ds(pl.multiple_of((me[0] ^ j) * width, 128), width)


def half_columns(me, j, half, width):
    return pl.ds(pl.multiple_of((HALVES * (me[0] ^ j) + half) * width, 128), width)


def first_kernel(n, me, key, value, query, grad, *refs):
    outs, (bufs, sems) = refs[:n], refs[n:]
    width = outs[0].shape[2]
    copies = []
    for i, j in enumerate(peers(n)):
        cols = half_columns(me, j, 0, width)
        copies.append(
            [
                pltpu.make_async_copy(src.at[:, cols], bufs.at[a, i], sems.at[a, i])
                for a, src in enumerate((key, value, query, grad))
            ]
        )
        for copy in copies[i]:
            copy.start()
    for i, out in enumerate(outs):
        for copy in copies[i]:
            copy.wait()
        for a in range(2):
            left, right = bufs[2 * a, i].astype(F32), bufs[2 * a + 1, i].astype(F32)
            out[a] = (left * right).astype(BF16)


def second_kernel(n, me, key, value, query, grad, *refs):
    outs = refs[-n:]
    width = outs[0].shape[2]
    for out, j in zip(outs, peers(n)):
        cols = half_columns(me, j, 1, width)
        for a, (left, right) in enumerate(((key, value), (query, grad))):
            out[a] = (left[:, cols].astype(F32) * right[:, cols].astype(F32)).astype(BF16)


def products(half, n, me, arrays, arrived):
    rows, total = arrays[0].shape
    width = total // n // HALVES
    scratch = [pltpu.VMEM((4, n, rows, width), BF16), pltpu.SemaphoreType.DMA((4, n))]
    return pl.pallas_call(
        functools.partial(second_kernel if half else first_kernel, n),
        in_specs=[SMEM] + [VMEM if half else HBM] * 4 + [VMEM] * len(arrived),
        out_specs=[VMEM] * n,
        out_shape=[pltpu.VMEM((2, rows, width), BF16)] * n,
        scratch_shapes=[] if half else scratch,
        compiler_params=PARAMS,
        name="products",
    )(me, *arrays, *arrived)


def lane_groups(width):
    return [slice(i, i + 128) for i in range(0, width, 128)]


def filter_kernel(half, filt, fwd, *refs):
    spec, x, u = refs[-3:]
    m2, width = x.shape[1] // CLASSES, u.shape[-1]
    groups = lane_groups(width)
    rows = m2 // CLASSES
    for g, lanes in enumerate(groups):
        x[g] = filt[half * width + lanes.start : half * width + lanes.stop, :].T
    for c in range(CLASSES):
        for g, lanes in enumerate(groups):
            hi, lo = parts(x[g, pl.ds(c, m2, stride=CLASSES), :])
            u[c, :, lanes] = dot(fwd[c], jnp.concatenate([hi, hi], 0)) + dot(fwd[c, :, :m2], lo)

    def step(i, carry):
        r = pl.multiple_of(i * rows, rows)
        re, im = pl.ds(r, rows), pl.ds(m2 + r, rows)
        for lanes in groups:
            z = dft([(u[c, re, lanes], u[c, im, lanes]) for c in range(CLASSES)], -1)
            for k in range(CLASSES):
                spec[k, re, lanes], spec[k, im, lanes] = z[k]
        return carry

    lax.fori_loop(0, CLASSES, step, 0)


def filter_spectrum(half, filters, fwd, arrived):
    chans, length = filters.shape
    width = chans // HALVES
    m2 = length // CLASSES
    return pl.pallas_call(
        functools.partial(filter_kernel, half),
        in_specs=[VMEM] * (2 + len(arrived)),
        out_specs=VMEM,
        out_shape=pltpu.VMEM((CLASSES, 2 * m2, width), F32),
        scratch_shapes=[
            pltpu.VMEM((width // 128, length, 128), F32),
            pltpu.VMEM((CLASSES, 2 * m2, width), F32),
        ],
        compiler_params=PARAMS,
        name="filter_spectrum",
    )(filters, fwd, *arrived)


def conv_kernel(n, d, half, me, *refs):
    got, (filt, fwd, back) = refs[:n], refs[n : n + 3]
    refs = refs[-(n + 2 + 6) :]
    out, (keep, send), (nat, x, u, y, turned, grad) = refs[:n], refs[n : n + 2], refs[n + 2 :]
    _, rows, width = got[0].shape
    m2 = x.shape[2]
    per = keep.shape[1] // CLASSES
    groups = lane_groups(width)
    step_rows = m2 // CLASSES
    part_rows = rows // CLASSES

    for a in range(2):
        for g, lanes in enumerate(groups):
            for i, j in enumerate(peers(n)):
                at = pl.multiple_of((me[0] ^ j) * rows, rows)
                nat[a, g, pl.ds(at, rows)] = got[i][a, :, lanes].astype(F32)
            for c in range(CLASSES):
                x[a, c, :, lanes] = nat[a, g, pl.ds(c, m2, stride=CLASSES), :].astype(BF16)
        for c in range(CLASSES):
            data = x[a, c]
            u[a, c] = dot(fwd[c], jnp.concatenate([data, data], 0))

    def middle(i, carry):
        r = pl.multiple_of(i * step_rows, step_rows)
        re, im = pl.ds(r, step_rows), pl.ds(m2 + r, step_rows)
        for lanes in groups:
            kv = dft([(u[0, c, re, lanes], u[0, c, im, lanes]) for c in range(CLASSES)], -1)
            wt = dft([(u[1, c, re, lanes], u[1, c, im, lanes]) for c in range(CLASSES)], -1)
            fs = [(filt[k, re, lanes], filt[k, im, lanes]) for k in range(CLASSES)]
            for o, (left, right, conj) in enumerate([(kv, fs, False), (wt, fs, True), (wt, kv, True)]):
                z = dft([times(s, t, conj) for s, t in zip(left, right)], 1)
                for c in range(CLASSES):
                    y[o, c, re, lanes] = z[c][0].astype(BF16)
                    y[o, c, im, lanes] = z[c][1].astype(BF16)
        return carry

    lax.fori_loop(0, CLASSES, middle, 0, unroll=4)

    for c in range(CLASSES):
        grad[c] = dot(back[c], y[2, c])
        for o in range(2):
            turned[o, c] = dot(back[c], y[o, c]).astype(BF16)
    for i, j in enumerate(back_peers(n)):
        at = pl.multiple_of((me[0] ^ j) * part_rows, part_rows)
        for o in range(2):
            for c in range(CLASSES):
                out[i][half, o, c * part_rows : (c + 1) * part_rows] = turned[o, c, pl.ds(at, part_rows)]
    for j in range(d):
        at = pl.multiple_of((me[1] ^ j) * per, per)
        for c in range(CLASSES):
            part = grad[c, pl.ds(at, per)]
            if j % 2:
                send[j // 2, c * per : (c + 1) * per] = part.astype(BF16)
            else:
                keep[j // 2, c * per : (c + 1) * per] = part


def conv(n, d, half, me, got, filt, fwd, back, before):
    _, rows, width = got[0].shape
    length = n * rows
    m2 = length // CLASSES
    out = pl.pallas_call(
        functools.partial(conv_kernel, n, d, half),
        in_specs=[SMEM] + [VMEM] * (n + 3 + len(before)),
        out_specs=[VMEM] * (n + 2),
        out_shape=[pltpu.VMEM((HALVES, 2, rows, width), BF16)] * n
        + [pltpu.VMEM((d // 2, length // d, width), dtype) for dtype in (F32, BF16)],
        scratch_shapes=[
            pltpu.VMEM((2, width // 128, length, 128), F32),
            pltpu.VMEM((2, CLASSES, m2, width), BF16),
            pltpu.VMEM((2, CLASSES, 2 * m2, width), F32),
            pltpu.VMEM((3, CLASSES, 2 * m2, width), BF16),
            pltpu.VMEM((2, CLASSES, m2, width), BF16),
            pltpu.VMEM((CLASSES, m2, width), F32),
        ],
        input_output_aliases={n + 4 + i: i for i in range(len(before))},
        compiler_params=CONV_PARAMS,
        name="conv",
    )(me, *got, filt, fwd, back, *before)
    return out


def natural(scratch, piece):
    rows = piece.shape[0] // CLASSES
    for c in range(CLASSES):
        scratch[pl.ds(c, rows, stride=CLASSES), :] = piece[c * rows : (c + 1) * rows]
    return scratch[...]


def gate_kernel(js, me, query, grad, value, key, gain, *refs):
    got, outs, token, (sent, sems, nat) = refs[: len(js)], refs[-8:-4], refs[-4], refs[-3:]
    token[...] = jnp.zeros_like(token)
    _, _, rows, width = got[0].shape
    copies = []
    for i, j in enumerate(js):
        block = peer_columns(me, j, HALVES * width)
        for half in range(HALVES):
            for g, lanes in enumerate(lane_groups(width)):
                at = half * width + lanes.start
                start = pl.multiple_of((me[0] ^ j) * HALVES * width + at, 128)
                cols = pl.ds(start, 128)
                to = slice(at, at + 128)
                scale = gain[:, cols]
                q, g_, v, k = (x[:, cols].astype(F32) for x in (query, grad, value, key))
                conv_out, corr_back = (
                    natural(nat.at[i, o, half, g], got[i][half, o, :, lanes].astype(F32)) for o in range(2)
                )
                mixing = conv_out + scale * (k * v).astype(BF16).astype(F32)
                sent[0, i, :, to] = (q * mixing).astype(BF16)
                sent[1, i, :, to] = (g_ * mixing).astype(BF16)
                total = corr_back + scale * (g_ * q).astype(BF16).astype(F32)
                sent[2, i, :, to] = (total * v).astype(BF16)
                sent[3, i, :, to] = (total * k).astype(BF16)
        for a in range(4):
            copy = pltpu.make_async_copy(sent.at[a, i], outs[a].at[:, block], sems.at[a, i])
            copy.start()
            copies.append(copy)
    for copy in copies:
        copy.wait()


def gate(js, me, query, grad, value, key, gain, got, outs):
    _, _, rows, width = got[0].shape
    return pl.pallas_call(
        functools.partial(gate_kernel, js),
        in_specs=[SMEM] + [VMEM] * (5 + len(got)) + [HBM] * len(outs),
        out_specs=[HBM] * 4 + [VMEM],
        out_shape=[jax.ShapeDtypeStruct(query.shape, BF16)] * 4 + [pltpu.VMEM((8, 128), F32)],
        scratch_shapes=[
            pltpu.VMEM((4, len(js), rows, HALVES * width), BF16),
            pltpu.SemaphoreType.DMA((4, len(js))),
            pltpu.VMEM((len(js), 2, HALVES, width // 128, rows, 128), F32),
        ],
        input_output_aliases={6 + len(got) + i: i for i in range(len(outs))},
        compiler_params=PARAMS,
        name="gate",
    )(me, query, grad, value, key, gain, *got, *outs)


def add_kernel(*refs):
    parts, (new_keep, new_send) = refs[:-2], refs[-2:]
    width = parts[0].shape[2]
    for h in range(len(parts) // 2):
        keep, got = parts[2 * h : 2 * h + 2]
        chans = slice(h * width, (h + 1) * width)
        for i in range(new_keep.shape[0]):
            new_keep[i, :, chans] = keep[2 * i] + got[2 * i].astype(F32)
            new_send[i, :, chans] = (keep[2 * i + 1] + got[2 * i + 1].astype(F32)).astype(BF16)


def turn_kernel(keep, got, out, nat):
    for g, lanes in enumerate(lane_groups(keep.shape[2])):
        total = keep[0, :, lanes] + got[0, :, lanes].astype(F32)
        out[lanes, :] = natural(nat.at[g], total).T


def trade(d, bit, send):
    return resident(lax.ppermute(send, "dp", [(i, i ^ bit) for i in range(d)]))


def add_grads(*parts):
    count, per, width = parts[0].shape
    shape = (count // 2, per, width * len(parts) // 2)
    return pl.pallas_call(
        add_kernel,
        in_specs=[VMEM] * len(parts),
        out_specs=[VMEM] * 2,
        out_shape=[pltpu.VMEM(shape, F32), pltpu.VMEM(shape, BF16)],
        compiler_params=PARAMS,
        name="add_grads",
    )(*parts)


def turn_grads(keep, got):
    _, per, chans = keep.shape
    return pl.pallas_call(
        turn_kernel,
        in_specs=[VMEM] * 2,
        out_specs=VMEM,
        out_shape=jax.ShapeDtypeStruct((chans, per), F32),
        scratch_shapes=[pltpu.VMEM((chans // 128, per, 128), F32)],
        compiler_params=PARAMS,
        name="turn_grads",
    )(keep, got)


def peers(n):
    return [0, 1, *range(2, n, 2), *range(3, n, 2)]


def back_peers(n):
    return [0, n - 2, 1, *range(2, n - 2, 2), *range(3, n, 2)]


def exchange(n, js, blocks):
    return [
        resident(lax.ppermute(block, "ctx", [(i, i ^ j) for i in range(n)])) if j else block
        for j, block in zip(js, blocks)
    ]


def after_kernel(*refs):
    pass


def after(arrived, blocks):
    count = len(arrived)
    return pl.pallas_call(
        after_kernel,
        in_specs=[VMEM] * (count + len(blocks)),
        out_specs=[VMEM] * len(blocks),
        out_shape=[pltpu.VMEM(b.shape, b.dtype) for b in blocks],
        input_output_aliases={count + i: i for i in range(len(blocks))},
        compiler_params=PARAMS,
        name="after",
    )(*arrived, *blocks)


def local(n, d, query_in, key_in, value_in, grad_out, filters, skip_gain):
    fwd, back = (resident(jnp.asarray(t)) for t in tables(filters.shape[1]))
    filters = resident(filters)
    gain = skip_gain[None, :]
    me = jnp.stack([lax.axis_index("ctx"), lax.axis_index("dp")]).astype(jnp.int32)

    arrays = [x[0] for x in (key_in, value_in, query_in, grad_out)]
    js = peers(n)
    cut = n // 2
    first = products(0, n, me, [in_hbm(x) for x in arrays], [])
    first = exchange(n, js, first)
    key, value, query, grad = arrays = [resident(x) for x in arrays]
    other = products(1, n, me, arrays, first[1:2])
    spec = filter_spectrum(0, filters, fwd, first[1:3])
    second = exchange(n, js[:cut], after([spec], other[:cut]))
    spec_other = filter_spectrum(1, filters, fwd, [spec])
    second += exchange(n, js[cut:], after([spec_other], other[cut:]))
    *mixed, keep, send = conv(n, d, 0, me, first, spec, fwd, back, [])
    traded = trade(d, 1, send)
    *mixed, keep_other, send = conv(n, d, 1, me, second, spec_other, fwd, back, mixed)

    bits = [1 << b for b in range(d.bit_length() - 1)]
    parts_ = keep, traded, keep_other, trade(d, 1, send)
    js = back_peers(n)
    mixed = exchange(n, js, mixed)
    for bit in bits[1:]:
        keep, send = add_grads(*parts_)
        parts_ = keep, trade(d, bit, send)

    outs = []
    early = n - 2
    for at in (slice(early), slice(early, n)):
        *outs, _ = gate(js[at], me, query, grad, value, key, gain, mixed[at], outs)
    grad_filter = turn_grads(*parts_)
    return *(x[None] for x in outs), grad_filter


def solution(mesh):
    rows = P("dp", "ctx", None)
    return jax.shard_map(
        functools.partial(local, mesh.shape["ctx"], mesh.shape["dp"]),
        mesh=mesh,
        in_specs=(rows, rows, rows, rows, P("ctx", None), P()),
        out_specs=(rows, rows, rows, rows, P("ctx", "dp")),
        check_vma=False,
    )
```
